32 devices in a mesh: dp: 2 (over x), ctx: 4 (over z), tp: 4 (over y, core).
Axes of the slice: x: 2, y: 2, z: 4, core: 2. Of those that a mesh axis runs over, the one named last changes fastest.
Arguments:
- tokens: bfloat16 [2, 2048, 2048], P('dp', ('ctx', 'tp')), may hold values from -6 to 6
- attn_gain: float32 [2048], replicated, may hold values from 0.25 to 1.75
- w_query: bfloat16 [2048, 2048], P(None, 'tp'), may hold values from -0.1875 to 0.1875
- w_key: bfloat16 [2048, 512], P(None, 'tp'), may hold values from -0.1875 to 0.1875
- w_value: bfloat16 [2048, 512], P(None, 'tp'), may hold values from -0.125 to 0.125
- w_out: bfloat16 [2048, 2048], P('tp'), may hold values from -0.75 to 0.75
- ffn_gain: float32 [2048], replicated, may hold values from 0.25 to 1.75
- w_gate: bfloat16 [2048, 8192], P(None, 'tp'), may hold values from -0.125 to 0.125
- w_up: bfloat16 [2048, 8192], P(None, 'tp'), may hold values from -0.125 to 0.125
- w_down: bfloat16 [8192, 2048], P('tp'), may hold values from -0.0625 to 0.0625
- out_cotangent: bfloat16 [2, 2048, 2048], P('dp', ('ctx', 'tp')), may hold values from -6 to 6
- doc_lengths: int32 [2, 8], P('dp'), may hold values from 1 to 1408, as said below
Outputs:
- layer_out: bfloat16 [2, 2048, 2048], P('dp', ('ctx', 'tp'))
- input_grad: float32 [2, 2048, 2048], P('dp', ('ctx', 'tp'))
- grad_attn_gain: float32 [2048], replicated
- grad_w_query: float32 [2048, 2048], P(('dp', 'ctx'), 'tp')
- grad_w_key: float32 [2048, 512], P(('dp', 'ctx'), 'tp')
- grad_w_value: float32 [2048, 512], P(('dp', 'ctx'), 'tp')
- grad_w_out: float32 [2048, 2048], P('tp', ('dp', 'ctx'))
- grad_ffn_gain: float32 [2048], replicated
- grad_w_gate: float32 [2048, 8192], P(('dp', 'ctx'), 'tp')
- grad_w_up: float32 [2048, 8192], P(('dp', 'ctx'), 'tp')
- grad_w_down: float32 [8192, 2048], P('tp', ('dp', 'ctx'))
The draws below stay inside these ranges and needn't reach their ends.
Inputs may be any that keep to these rules, and one draw needn't show every extreme that they name: `doc_lengths`: each row holds its 8 documents in this order from position 0, then padding. The first has exactly 1408 tokens, the others at least one; together they leave 1 to 255 padding positions.
All inputs are finite; a program needn't handle non-finite values.
Results may differ from the reference program's by a relative error of at most 0.024.
Values may be sent and summed in bfloat16 or wider, within the bound.
No kernel may reach another device: no remote copies, remote signals or barrier semaphores. Data moves between devices by JAX's collectives and lax.ppermute only.
A program may use at most 192 MiB of HBM per device.

```python
import math
import jax
import jax.numpy as jnp
import numpy as np
from jax import lax

D = 2048
HQ = 32
KV = 8
HD = 64
FF = 8192
NDOC = 8
CTX_TOK = 512
ROW_LEN = 2048
ROWS = 2
N_CTX = 4


def draw_doc_lengths(key, part):
    key = jax.random.fold_in(key, 7)
    row_total = CTX_TOK * N_CTX
    half_rows = CTX_TOK // 2
    longest = row_total // 2 + half_rows + CTX_TOK // 4
    pad_key, share_key = jax.random.split(key)
    padding = jax.random.randint(pad_key, (ROWS,), 1, half_rows, dtype=jnp.int32)
    spare = row_total - longest - padding
    weights = jax.random.randint(share_key, (ROWS, NDOC - 1), 1, 16, dtype=jnp.int32)
    shares = (spare - (NDOC - 1))[:, None] * weights // jnp.sum(weights, axis=1, keepdims=True)
    others = 1 + shares
    others = others.at[:, -1].add(spare - jnp.sum(others, axis=1))
    first_doc = jnp.full((ROWS, 1), longest, jnp.int32)
    return jnp.concatenate([first_doc, others], axis=1).astype(jnp.int32)


def block_levels(stream_key, shape, cuts, least, largest):
    def one(axis_at, shards_of):
        heights = jax.random.uniform(jax.random.fold_in(jax.random.fold_in(stream_key, 6), axis_at), (shards_of,), jnp.float32, least / len(cuts), largest / len(cuts))
        return jnp.repeat(jnp.exp(heights), shape[axis_at] // shards_of).reshape((-1,) + (1,) * (len(shape) - axis_at - 1))

    factor_of = one(*cuts[0])
    for cut in cuts[1:]:
        factor_of = factor_of * one(*cut)
    return factor_of


def noise(rng, shape, spread, reach, pieces=(), kind=jnp.bfloat16):
    values = spread * jax.random.normal(rng, shape, jnp.float32)
    if pieces:
        values = values * block_levels(rng, shape, pieces, -0.22, 0.18)
    return jnp.clip(values, -reach, reach).astype(kind)


def setup_inputs(seed: int = 0) -> dict:
    keys = jax.random.split(jax.random.key(seed), 13)
    tokens = noise(keys[0], (ROWS, ROW_LEN, D), 1.0, 6.0, ((0, 2), (1, 16)))
    attn_gain = jnp.clip(1.0 + 0.15 * jax.random.normal(keys[1], (D,), jnp.float32), 0.25, 1.75)
    w_query = noise(keys[2], (D, HQ * HD), (D // 2) ** -0.5, 0.1875, ((1, 4),))
    w_key = noise(keys[3], (D, KV * HD), (D // 2) ** -0.5, 0.1875, ((1, 4),))
    w_value = noise(keys[4], (D, KV * HD), D ** -0.5, 0.125, ((1, 4),))
    w_out = noise(keys[5], (HQ * HD, D), (HQ * HD // 32) ** -0.5, 0.75, ((0, 4),))
    ffn_gain = jnp.clip(1.0 + 0.15 * jax.random.normal(keys[6], (D,), jnp.float32), 0.25, 1.75)
    w_gate = noise(keys[7], (D, FF), D ** -0.5, 0.125, ((1, 4),))
    w_up = noise(keys[8], (D, FF), D ** -0.5, 0.125, ((1, 4),))
    w_down = noise(keys[9], (FF, D), FF ** -0.5, 0.0625, ((0, 4),))
    out_cotangent = noise(keys[10], (ROWS, ROW_LEN, D), 1.0, 6.0, ((0, 2), (1, 16)))
    doc_lengths = draw_doc_lengths(jax.random.fold_in(keys[12], 71), 0)
    return {"tokens": tokens, "attn_gain": attn_gain, "w_query": w_query, "w_key": w_key, "w_value": w_value, "w_out": w_out, "ffn_gain": ffn_gain, "w_gate": w_gate, "w_up": w_up, "w_down": w_down, "out_cotangent": out_cotangent, "doc_lengths": doc_lengths}


EPSILON = 1e-05
NEGATIVE = -1e+30
ROPE_THETA = 500000.0

@jax.custom_vjp
def low(v):
    return lax.optimization_barrier(v.astype(jnp.bfloat16)).astype(jnp.float32)

@jax.custom_vjp
def low_back(v):
    return v

def low_keep(v):
    return (low(v), None)

def low_pass(kept, grad):
    return (grad,)

def back_keep(v):
    return (v, None)

def back_low(kept, grad):
    return (low(grad),)
low.defvjp(low_keep, low_pass)
low_back.defvjp(back_keep, back_low)

def rope_table(head_size):
    base_freq = np.array([ROPE_THETA ** (-2.0 * index / head_size) for index in range(head_size // 2)])
    wavelength = 2.0 * math.pi / base_freq
    blend = (8192.0 / wavelength - 1.0) / 3.0
    middle = (1.0 - blend) * base_freq / 32.0 + blend * base_freq
    return np.where(wavelength > 8192.0, base_freq / 32.0, np.where(wavelength < 2048.0, base_freq, middle))

def stored_positions(first_row, row_count, ctx_rows, ctx_count):
    stored = first_row + jnp.arange(row_count, dtype=jnp.int32)
    owner = stored // ctx_rows
    within = stored % ctx_rows
    half_rows = ctx_rows // 2
    piece_num = jnp.where(within < half_rows, owner, 2 * ctx_count - 1 - owner)
    return (piece_num * half_rows + within % half_rows).astype(jnp.int32)

def doc_segments(positions, doc_row):
    ends = jnp.cumsum(doc_row).astype(jnp.int32)
    return lax.optimization_barrier(jnp.sum((positions[:, None] >= ends[None, :]).astype(jnp.int32), axis=1))

def rms_norm(values_in, gain_vec):
    return values_in * lax.rsqrt(lax.optimization_barrier(jnp.mean(values_in * values_in, axis=-1, keepdims=True)) + EPSILON) * gain_vec

def rotate(values_in, cosine, sine_part):
    halfway = values_in.shape[-1] // 2
    first_half = values_in[..., :halfway]
    second_half = values_in[..., halfway:]
    return jnp.concatenate([first_half * cosine - second_half * sine_part, second_half * cosine + first_half * sine_part], axis=-1)

def matmul(left, right):
    return jnp.dot(left, right, precision=lax.Precision.HIGHEST)

def reference(tokens, attn_gain, w_query, w_key, w_value, w_out, ffn_gain, w_gate, w_up, w_down, out_cotangent, doc_lengths):
    positions = stored_positions(0, ROW_LEN, CTX_TOK, N_CTX)
    segments = jnp.stack([doc_segments(positions, doc_lengths[row_num]) for row_num in range(ROWS)])
    is_valid = (segments < NDOC).astype(jnp.float32)
    inv_freq = jnp.asarray(rope_table(HD), jnp.float32)
    angles = positions.astype(jnp.float32)[:, None] * inv_freq[None, :]
    cosine = jnp.cos(angles)[:, None, :]
    sine_part = jnp.sin(angles)[:, None, :]
    block_rows = math.gcd(ROW_LEN, 128)
    blocks = ROW_LEN // block_rows
    per_group = HQ // KV
    score_scale = 1.0 / math.sqrt(HD)

    def forward_row(inputs, gain_one, query_w, key_w, value_w, out_w, gain_two, gate_w, up_w, down_w, seg_row, valid_row):
        normed = low(rms_norm(inputs, gain_one))
        queries = low_back(matmul(normed, query_w)).reshape(ROW_LEN, HQ, HD)
        keys_raw = low_back(matmul(normed, key_w)).reshape(ROW_LEN, KV, HD)
        values = low(low_back(matmul(normed, value_w))).reshape(ROW_LEN, KV, HD)
        rot_queries = low(rotate(queries, cosine, sine_part))
        rot_keys = low(rotate(keys_raw, cosine, sine_part))

        def attend_block(block_args):
            query_blk, query_pos, query_seg = block_args
            grouped = query_blk.reshape(block_rows, KV, per_group, HD)
            scores = jnp.einsum('bkgd,skd->kgbs', grouped, rot_keys, precision=lax.Precision.HIGHEST) * score_scale
            allowed = (query_seg[:, None] == seg_row[None, :]) & (positions[None, :] <= query_pos[:, None])
            scores = low_back(jnp.where(allowed[None, None], scores, NEGATIVE))
            probs = low(jax.nn.softmax(scores, axis=-1))
            attended = jnp.einsum('kgbs,skd->bkgd', probs, values, precision=lax.Precision.HIGHEST)
            return attended.reshape(block_rows, HQ * HD)
        attended = lax.map(jax.checkpoint(attend_block), (rot_queries.reshape(blocks, block_rows, HQ, HD), positions.reshape(blocks, block_rows), seg_row.reshape(blocks, block_rows)))
        attended = attended.reshape(ROW_LEN, HQ * HD)
        merged = low(low_back(attended * valid_row[:, None]))
        hidden_state = inputs + low_back(matmul(merged, out_w))
        normed_ffn = low(rms_norm(hidden_state, gain_two))
        gate = low_back(matmul(normed_ffn, gate_w))
        up_proj = low_back(matmul(normed_ffn, up_w))
        act = low(jax.nn.silu(gate) * up_proj)
        return hidden_state + low_back(matmul(act, down_w))

    def forward(inputs, gain_one, query_w, key_w, value_w, out_w, gain_two, gate_w, up_w, down_w):
        return jnp.stack([forward_row(inputs[row_num], gain_one, query_w, key_w, value_w, out_w, gain_two, gate_w, up_w, down_w, segments[row_num], is_valid[row_num]) for row_num in range(ROWS)])
    params = tuple((item.astype(jnp.float32) for item in (tokens, attn_gain, w_query, w_key, w_value, w_out, ffn_gain, w_gate, w_up, w_down)))
    result, pull = jax.vjp(forward, *params)
    grads = pull(out_cotangent.astype(jnp.float32))
    return (result.astype(jnp.bfloat16), grads[0], grads[1], grads[2], grads[3], grads[4], grads[5], grads[6], grads[7], grads[8], grads[9])
```

```python
import math

import jax
import jax.numpy as jnp
import numpy as np
from jax import lax
from jax.sharding import PartitionSpec as P

HD = 64


EPSILON = 1e-05
NEGATIVE = -1e30
START_MAX = -1e20
ROPE_THETA = 500000.0


def rope_table(head_size):
    base_freq = np.array(
        [ROPE_THETA ** (-2.0 * index / head_size) for index in range(head_size // 2)]
    )
    wavelength = 2.0 * math.pi / base_freq
    blend = (8192.0 / wavelength - 1.0) / 3.0
    middle = (1.0 - blend) * base_freq / 32.0 + blend * base_freq
    return np.where(
        wavelength > 8192.0, base_freq / 32.0, np.where(wavelength < 2048.0, base_freq, middle)
    )


def block_positions(owner, within, ctx_rows, ctx_count):
    half_rows = ctx_rows // 2
    piece_num = jnp.where(within < half_rows, owner, 2 * ctx_count - 1 - owner)
    return (piece_num * half_rows + within % half_rows).astype(jnp.int32)


def doc_segments(positions, doc_row):
    ends = jnp.cumsum(doc_row)
    return jnp.sum((positions[:, None] >= ends[None, :]).astype(jnp.int32), axis=1)


def rms_norm(values_in, gain_vec):
    return (
        values_in
        * lax.rsqrt(jnp.mean(values_in * values_in, axis=-1, keepdims=True) + EPSILON)
        * gain_vec
    )


def rotate(values_in, cosine, sine_part):
    halfway = values_in.shape[-1] // 2
    first_half = values_in[..., :halfway]
    second_half = values_in[..., halfway:]
    return jnp.concatenate(
        [
            first_half * cosine - second_half * sine_part,
            second_half * cosine + first_half * sine_part,
        ],
        axis=-1,
    )


def unrotate(values_in, cosine, sine_part):
    halfway = values_in.shape[-1] // 2
    first_half = values_in[..., :halfway]
    second_half = values_in[..., halfway:]
    return jnp.concatenate(
        [
            first_half * cosine + second_half * sine_part,
            second_half * cosine - first_half * sine_part,
        ],
        axis=-1,
    )


def contract_rows(left, right):
    return lax.dot_general(
        left, right, (((0,), (0,)), ((), ())), preferred_element_type=jnp.float32
    )


def contract_cols(left, right):
    return lax.dot_general(
        left, right, (((1,), (1,)), ((), ())), preferred_element_type=jnp.float32
    )


def matmul(left, right):
    return jnp.dot(left, right, preferred_element_type=jnp.float32)


def flip(values_in, axis, mask):
    count = lax.axis_size(axis)
    return lax.ppermute(values_in, axis, [(i, i ^ mask) for i in range(count)])


def tp_gather(shard):
    count = lax.axis_size("tp")
    parts = {0: shard}
    mask = 2
    while mask < count:
        parts.update({j ^ mask: flip(part, "tp", mask) for j, part in parts.items()})
        mask *= 2
    parts.update({j ^ 1: flip(part, "tp", 1) for j, part in parts.items()})
    return jnp.concatenate([parts[j] for j in range(count)], axis=0)


def tp_scatter(near, far):
    count = lax.axis_size("tp")
    rows = 2 * near.shape[0] // count
    blocks = {}
    for first, terms in ((count // 2, far), (0, near)):
        terms = terms.astype(jnp.bfloat16)
        for j in range(0, count // 2, 2):
            kept, sent = terms[j * rows : (j + 1) * rows], terms[(j + 1) * rows : (j + 2) * rows]
            blocks[first + j] = kept.astype(jnp.float32) + flip(sent, "tp", 1).astype(jnp.float32)
    mask = count // 2
    while mask > 1:
        for j in range(0, mask, 2):
            sent = flip(blocks[j + mask].astype(jnp.bfloat16), "tp", mask)
            blocks[j] = blocks[j] + sent.astype(jnp.float32)
        mask //= 2
    return blocks[0]


def line_scatter(terms, axis, dim):
    count = lax.axis_size(axis)
    rank = lax.axis_index(axis)
    size = terms.shape[dim] // count

    def chunk(index):
        index = jnp.clip(index, 0, count - 1)
        return lax.dynamic_slice_in_dim(terms, index * size, size, dim).astype(jnp.float32)

    up, down = None, None
    for step in range(1, count):
        up_term = chunk(count - step + rank)
        down_term = chunk(rank - count + step)
        if up is not None:
            up_term = up_term + up.astype(jnp.float32)
            down_term = down_term + down.astype(jnp.float32)
        up = lax.ppermute(
            up_term.astype(jnp.bfloat16), axis, [(i, i + 1) for i in range(step)]
        )
        down = lax.ppermute(
            down_term.astype(jnp.bfloat16),
            axis,
            [(count - 1 - i, count - 2 - i) for i in range(step)],
        )
    return chunk(rank) + up.astype(jnp.float32) + down.astype(jnp.float32)


def sum_everywhere(values_in):
    for axis in ("tp", "dp", "ctx"):
        mask = 1
        while mask < lax.axis_size(axis):
            values_in = values_in + flip(values_in, axis, mask)
            mask *= 2
    return values_in


def half_of(values_in, index):
    size = values_in.shape[1] // lax.axis_size("dp")
    return lax.dynamic_slice_in_dim(values_in, index * size, size, 1)


def wide_pair(shard, whole):
    me = lax.axis_index("dp")
    other = flip(half_of(shard, 1 - me), "dp", 1)
    return half_of(whole, me), tp_gather(other)


def weight_grad(narrow, wide, narrow_first):
    narrow_other = flip(narrow, "dp", 1)
    if narrow_first:
        terms = contract_rows(narrow, wide[0]) + contract_rows(narrow_other, wide[1])
        return line_scatter(terms.astype(jnp.bfloat16), "ctx", 1)
    terms = contract_rows(wide[0], narrow) + contract_rows(wide[1], narrow_other)
    return line_scatter(terms.astype(jnp.bfloat16), "ctx", 0)


def per_device(
    tokens,
    attn_gain,
    w_query,
    w_key,
    w_value,
    w_out,
    ffn_gain,
    w_gate,
    w_up,
    w_down,
    out_cotangent,
    doc_lengths,
):
    ctx_count = lax.axis_size("ctx")
    ctx_rank = lax.axis_index("ctx")
    tp_count = lax.axis_size("tp")
    tp_rows = tokens.shape[1]
    ctx_rows = tp_rows * tp_count
    near_rows = ctx_rows // 2
    kv_heads = w_key.shape[1] // HD
    q_heads = w_query.shape[1] // HD
    per_group = q_heads // kv_heads
    query_rows = per_group * ctx_rows
    score_scale = 1.0 / math.sqrt(HD)
    doc_row = doc_lengths[0]
    index = jnp.arange(ctx_rows, dtype=jnp.int32)
    within = (lax.axis_index("tp") ^ (index // tp_rows)) * tp_rows + index % tp_rows
    block_pos = [
        block_positions((ctx_rank + k) % ctx_count, within, ctx_rows, ctx_count)
        for k in range(ctx_count)
    ]
    block_seg = [doc_segments(pos, doc_row) for pos in block_pos]
    query_pos, query_seg = block_pos[0], block_seg[0]
    is_valid = (query_seg < doc_row.shape[0]).astype(jnp.float32)
    row_pos = jnp.tile(query_pos, per_group)
    row_seg = jnp.tile(query_seg, per_group)
    valid_rows = jnp.tile(is_valid, per_group)
    inv_freq = jnp.asarray(rope_table(HD), jnp.float32)
    angles = query_pos.astype(jnp.float32)[:, None] * inv_freq[None, :]
    cosine = jnp.cos(angles)[:, None, :]
    sine_part = jnp.sin(angles)[:, None, :]

    inputs = tokens[0].astype(jnp.float32)
    normed_local = rms_norm(inputs, attn_gain).astype(jnp.bfloat16)
    normed = tp_gather(normed_local)
    grad_fb_local = out_cotangent[0]
    grad_fb = tp_gather(grad_fb_local)
    grad_y = grad_fb_local.astype(jnp.float32)
    queries = matmul(normed, w_query).reshape(ctx_rows, q_heads, HD)
    keys_raw = matmul(normed, w_key).reshape(ctx_rows, kv_heads, HD)
    values = matmul(normed, w_value).astype(jnp.bfloat16)
    rot_queries = rotate(queries, cosine, sine_part).astype(jnp.bfloat16)
    rot_keys = (
        rotate(keys_raw, cosine, sine_part).astype(jnp.bfloat16).reshape(ctx_rows, kv_heads * HD)
    )
    query_mat = (
        rot_queries.reshape(ctx_rows, kv_heads, per_group, HD)
        .transpose(1, 2, 0, 3)
        .reshape(kv_heads, query_rows, HD)
    )
    packed = jnp.concatenate([rot_keys, values], axis=1)

    def shift(values_in, k):
        return lax.ppermute(
            values_in, "ctx", [((i + k) % ctx_count, i) for i in range(ctx_count)]
        )

    kv_blocks = [packed] + [shift(packed, k) for k in range(1, ctx_count)]
    kv_blocks = [blk.reshape(ctx_rows, 2, kv_heads, HD) for blk in kv_blocks]

    def scores_of(k):
        raw_scores = (
            jnp.einsum(
                "hrd,khd->hrk", query_mat, kv_blocks[k][:, 0], preferred_element_type=jnp.float32
            )
            * score_scale
        )
        allowed = (row_seg[:, None] == block_seg[k][None, :]) & (
            block_pos[k][None, :] <= row_pos[:, None]
        )
        return (jnp.where(allowed[None], raw_scores, NEGATIVE), allowed)

    row_max = jnp.full((kv_heads, query_rows), START_MAX, jnp.float32)
    row_sum = jnp.zeros((kv_heads, query_rows), jnp.float32)
    weighted = jnp.zeros((kv_heads, query_rows, HD), jnp.float32)
    for k in range(ctx_count):
        scores, allowed = scores_of(k)
        new_max = jnp.maximum(row_max, jnp.max(scores, axis=2))
        rescale = jnp.exp(row_max - new_max)
        expo = jnp.where(allowed[None], jnp.exp(scores - new_max[:, :, None]), 0.0)
        row_sum = row_sum * rescale + jnp.sum(expo, axis=2)
        weighted = weighted * rescale[:, :, None] + jnp.einsum(
            "hrk,khd->hrd",
            expo.astype(jnp.bfloat16),
            kv_blocks[k][:, 1],
            preferred_element_type=jnp.float32,
        )
        row_max = new_max
    attended = weighted / row_sum[:, :, None]
    log_total = row_max + jnp.log(row_sum)
    merged_heads = (attended * valid_rows[None, :, None]).astype(jnp.bfloat16)
    merged = (
        merged_heads.reshape(kv_heads, per_group, ctx_rows, HD)
        .transpose(2, 0, 1, 3)
        .reshape(ctx_rows, q_heads * HD)
    )
    hidden_state = inputs + tp_scatter(
        matmul(merged[:near_rows], w_out), matmul(merged[near_rows:], w_out)
    )
    normed_ffn_local = rms_norm(hidden_state, ffn_gain).astype(jnp.bfloat16)
    normed_ffn = tp_gather(normed_ffn_local)
    gate = matmul(normed_ffn, w_gate)
    up_proj = matmul(normed_ffn, w_up)
    act = (jax.nn.silu(gate) * up_proj).astype(jnp.bfloat16)
    wide_fb = wide_pair(grad_fb_local, grad_fb)
    grad_down = weight_grad(act, wide_fb, True)
    grad_act = contract_cols(grad_fb, w_down)
    sigma = jax.nn.sigmoid(gate)
    grad_gate = (grad_act * up_proj * sigma * (1.0 + gate * (1.0 - sigma))).astype(jnp.bfloat16)
    grad_up = (grad_act * gate * sigma).astype(jnp.bfloat16)
    wide_nffn = wide_pair(normed_ffn_local, normed_ffn)
    grad_gate_w = weight_grad(grad_gate, wide_nffn, False)
    grad_up_w = weight_grad(grad_up, wide_nffn, False)

    def nffn_terms(rows):
        return contract_cols(grad_gate[rows], w_gate) + contract_cols(grad_up[rows], w_up)

    near, far = slice(0, near_rows), slice(near_rows, ctx_rows)
    grad_nffn = tp_scatter(nffn_terms(near), nffn_terms(far))
    grad_state_norm, grad_ffn_gain = jax.vjp(rms_norm, hidden_state, ffn_gain)[1](grad_nffn)
    grad_state = grad_y + grad_state_norm
    grad_sb_local = grad_state.astype(jnp.bfloat16)
    grad_sb = tp_gather(grad_sb_local)
    grad_out_w = weight_grad(merged, wide_pair(grad_sb_local, grad_sb), True)
    layer_out = (
        hidden_state + tp_scatter(matmul(act[near], w_down), matmul(act[far], w_down))
    ).astype(jnp.bfloat16)
    grad_merged = contract_cols(grad_sb, w_out).astype(jnp.bfloat16)
    grad_att = grad_merged.reshape(ctx_rows, kv_heads, per_group, HD).transpose(1, 2, 0, 3).reshape(
        kv_heads, query_rows, HD
    ) * valid_rows[None, :, None].astype(jnp.bfloat16)
    delta = jnp.sum(grad_att.astype(jnp.float32) * attended, axis=2)

    grad_rows = jnp.zeros((kv_heads, query_rows, HD), jnp.float32)
    kv_grad = jnp.zeros((ctx_rows, 2, kv_heads, HD), jnp.float32)
    for k in reversed(range(ctx_count)):
        scores, allowed = scores_of(k)
        probs = jnp.where(allowed[None], jnp.exp(scores - log_total[:, :, None]), 0.0)
        grad_probs = jnp.einsum(
            "hrd,khd->hrk", grad_att, kv_blocks[k][:, 1], preferred_element_type=jnp.float32
        )
        grad_scores = (probs * (grad_probs - delta[:, :, None])).astype(jnp.bfloat16)
        grad_rows = (
            grad_rows
            + jnp.einsum(
                "hrk,khd->hrd",
                grad_scores,
                kv_blocks[k][:, 0],
                preferred_element_type=jnp.float32,
            )
            * score_scale
        )
        key_grad = (
            jnp.einsum("hrk,hrd->khd", grad_scores, query_mat, preferred_element_type=jnp.float32)
            * score_scale
        )
        value_grad = jnp.einsum(
            "hrk,hrd->khd", probs.astype(jnp.bfloat16), grad_att, preferred_element_type=jnp.float32
        )
        block_grad = jnp.stack([key_grad, value_grad], axis=1)
        if k:
            block_grad = lax.ppermute(
                block_grad.astype(jnp.bfloat16).reshape(ctx_rows, 2 * kv_heads * HD),
                "ctx",
                [(i, (i + k) % ctx_count) for i in range(ctx_count)],
            ).reshape(ctx_rows, 2, kv_heads, HD).astype(jnp.float32)
        kv_grad = kv_grad + block_grad
    grad_rk, grad_vals = kv_grad[:, 0], kv_grad[:, 1]
    grad_rq = (
        grad_rows.reshape(kv_heads, per_group, ctx_rows, HD)
        .transpose(2, 0, 1, 3)
        .reshape(ctx_rows, q_heads, HD)
    )
    grad_queries = (
        unrotate(grad_rq, cosine, sine_part).astype(jnp.bfloat16).reshape(ctx_rows, q_heads * HD)
    )
    grad_keys = (
        unrotate(grad_rk, cosine, sine_part).astype(jnp.bfloat16).reshape(ctx_rows, kv_heads * HD)
    )
    grad_vals_low = grad_vals.astype(jnp.bfloat16).reshape(ctx_rows, kv_heads * HD)
    grad_qkv = jnp.concatenate([grad_queries, grad_keys, grad_vals_low], axis=1)
    grad_qkv_w = weight_grad(grad_qkv, wide_pair(normed_local, normed), False)
    q_width, kv_width = q_heads * HD, kv_heads * HD

    def normed_terms(rows):
        return (
            contract_cols(grad_queries[rows], w_query)
            + contract_cols(grad_keys[rows], w_key)
            + contract_cols(grad_vals_low[rows], w_value)
        )

    grad_normed = tp_scatter(normed_terms(near), normed_terms(far))
    grad_input_norm, grad_attn_gain = jax.vjp(rms_norm, inputs, attn_gain)[1](grad_normed)
    input_grad = grad_state + grad_input_norm
    gains = sum_everywhere(jnp.stack([grad_attn_gain, grad_ffn_gain]))
    return (
        layer_out[None],
        input_grad[None],
        gains[0],
        grad_qkv_w[:, :q_width],
        grad_qkv_w[:, q_width : q_width + kv_width],
        grad_qkv_w[:, q_width + kv_width :],
        grad_out_w,
        gains[1],
        grad_gate_w,
        grad_up_w,
        grad_down,
    )


def solution(mesh):
    placed = (
        P("dp", ("ctx", "tp"), None),
        P(),
        P(None, "tp"),
        P(None, "tp"),
        P(None, "tp"),
        P("tp", None),
        P(),
        P(None, "tp"),
        P(None, "tp"),
        P("tp", None),
        P("dp", ("ctx", "tp"), None),
        P("dp", None),
    )
    return jax.shard_map(
        per_device,
        mesh=mesh,
        in_specs=placed,
        out_specs=(
            P("dp", ("ctx", "tp"), None),
            P("dp", ("ctx", "tp"), None),
            P(),
            P(("dp", "ctx"), "tp"),
            P(("dp", "ctx"), "tp"),
            P(("dp", "ctx"), "tp"),
            P("tp", ("dp", "ctx")),
            P(),
            P(("dp", "ctx"), "tp"),
            P(("dp", "ctx"), "tp"),
            P("tp", ("dp", "ctx")),
        ),
        check_vma=False,
    )
```

```python
import functools
import math

import jax
import jax.numpy as jnp
import numpy as np
from jax import lax
from jax.experimental import pallas as pl
from jax.experimental.pallas import tpu as pltpu
from jax.sharding import PartitionSpec as P

HD = 64
EPSILON = 1e-05
NEGATIVE = -1e30
ROPE_THETA = 500000.0


def rope_table(head_size):
    base_freq = np.array(
        [ROPE_THETA ** (-2.0 * index / head_size) for index in range(head_size // 2)]
    )
    wavelength = 2.0 * math.pi / base_freq
    blend = (8192.0 / wavelength - 1.0) / 3.0
    middle = (1.0 - blend) * base_freq / 32.0 + blend * base_freq
    return np.where(
        wavelength > 8192.0, base_freq / 32.0, np.where(wavelength < 2048.0, base_freq, middle)
    )


def rms_norm(values_in, gain_vec):
    return (
        values_in
        * lax.rsqrt(jnp.mean(values_in * values_in, axis=-1, keepdims=True) + EPSILON)
        * gain_vec
    )


F32, BF16 = jnp.float32, jnp.bfloat16
VMEM_BYTES = 62 * 1024 * 1024
NN = (((1,), (0,)), ((), ()))
NT = (((1,), (1,)), ((), ()))
TN = (((0,), (0,)), ((), ()))
VMEM = pl.BlockSpec(memory_space=pltpu.VMEM)
SMEM = pl.BlockSpec(memory_space=pltpu.SMEM)
ANYWHERE = pl.BlockSpec(memory_space=pl.ANY)


def dot(left, right, dims=NN):
    return lax.dot_general(left, right, dims, preferred_element_type=F32)


def part_specs(parts, rows, width, col):
    def spec(j):
        if j is None:
            return pl.BlockSpec((rows, width), lambda *at: (0, col(*at)))
        return pl.BlockSpec((rows, width), lambda *at: (at[-1][j], col(*at)))

    return [spec(part[1] if isinstance(part, tuple) else None) for part in parts]


def part_arrays(parts):
    return [part[0] if isinstance(part, tuple) else part for part in parts]


def rows_of(refs):
    return jnp.concatenate([ref[...] for ref in refs], axis=0)


class Chain:
    def __init__(self):
        self.held = []
        self.cost = 58 * 10**8

    def wait(self, *arrays):
        self.held = [*arrays, *self.held]

    def call(self, name, body, args, in_specs, out_specs, out_shape, flops, grid=(), scalars=0, scratch=()):
        held, count, outs = self.held, len(args), len(out_shape)

        def inner(*refs):
            rest = refs[count + len(held) :]
            body(*refs[:count], *rest[:outs], *rest[outs + 1 :])

        results = pl.pallas_call(
            inner,
            grid_spec=pltpu.PrefetchScalarGridSpec(
                num_scalar_prefetch=scalars,
                grid=grid,
                in_specs=list(in_specs) + [ANYWHERE] * len(held),
                out_specs=[*out_specs, ANYWHERE],
                scratch_shapes=list(scratch),
            ),
            out_shape=[*out_shape, jax.ShapeDtypeStruct((8, 128), F32)],
            compiler_params=pltpu.CompilerParams(
                vmem_limit_bytes=VMEM_BYTES, dimension_semantics=("arbitrary",) * len(grid)
            ),
            cost_estimate=pl.CostEstimate(
                flops=self.cost,
                bytes_accessed=1,
                transcendentals=0,
            ),
            name=name,
        )(*args, *held)
        self.held = [results[-1]]
        return results[:-1]


def fill_rows(parts, rows_ref):
    @pl.when(pl.program_id(0) == 0)
    def _():
        rows_ref[...] = rows_of(parts)


def ffn_front_body(count, *refs):
    gate_ref, up_ref, act_ref, slope_ref, silu_ref, rows_ref = refs[count:]
    fill_rows(refs[:count], rows_ref)
    rows = rows_ref[...]
    gate = dot(rows, gate_ref[...])
    up = dot(rows, up_ref[...])
    sigma = 1.0 / (1.0 + jnp.exp(-gate))
    silu = gate * sigma
    act_ref[...] = (silu * up).astype(BF16)
    slope_ref[...] = (up * sigma * (1.0 + gate * (1.0 - sigma))).astype(BF16)
    silu_ref[...] = silu.astype(BF16)


def whole(array):
    return pl.BlockSpec(array.shape, lambda *_: (0,) * array.ndim)


def ffn_front(chain, parts, w_gate, w_up, part=(0, 1), block=512):
    count, width = sum(p.shape[0] for p in parts), parts[0].shape[1]
    units = w_gate.shape[1] // part[1]
    block = min(block, units)
    first = part[0] * (units // block)
    weight = pl.BlockSpec((width, block), lambda j: (0, first + j))
    return chain.call(
        "ffn_front",
        functools.partial(ffn_front_body, len(parts)),
        (*parts, w_gate, w_up),
        [whole(p) for p in parts] + [weight, weight],
        [pl.BlockSpec((count, block), lambda j: (0, j))] * 3,
        [jax.ShapeDtypeStruct((count, units), BF16)] * 3,
        4 * count * width * units,
        grid=(units // block,),
        scratch=[pltpu.VMEM((count, width), BF16)],
    )


def ffn_back_body(count, perm_ref, *refs):
    down_ref, slope_ref, silu_ref, gate_ref, up_ref, rows_ref = refs[count:]
    fill_rows(refs[:count], rows_ref)
    grad_act = dot(rows_ref[...], down_ref[...], NT)
    gate_ref[...] = (grad_act * slope_ref[...].astype(F32)).astype(BF16)
    up_ref[...] = (grad_act * silu_ref[...].astype(F32)).astype(BF16)


def ffn_back(chain, perm, parts, w_down, slope, silu, block=512):
    count, units = slope.shape
    width = w_down.shape[1]
    block = min(block, units)
    tile = pl.BlockSpec((count, block), lambda j, _: (0, j))
    return chain.call(
        "ffn_back",
        functools.partial(ffn_back_body, len(parts)),
        (perm, *part_arrays(parts), w_down, slope, silu),
        part_specs(parts, count // len(parts), width, lambda *_: 0)
        + [pl.BlockSpec((block, width), lambda j, _: (j, 0)), tile, tile],
        [tile, tile],
        [jax.ShapeDtypeStruct((count, units), BF16)] * 2,
        2 * count * width * units,
        grid=(units // block,),
        scalars=1,
        scratch=[pltpu.VMEM((count, width), BF16)],
    )


def pull_body(count, dims, *refs):
    total = dot(refs[0][...], refs[count][...], dims)
    for i in range(1, count):
        total = total + dot(refs[i][...], refs[count + i][...], dims)
    outs = refs[2 * count :]
    rows = total.shape[0] // len(outs)
    for j, out in enumerate(outs):
        out[...] = total[j * rows : (j + 1) * rows].astype(BF16)


def pull(chain, grads, weights, blocks, dims=NT, block=1024):
    rows, at = grads[0].shape[0], 0 if dims == NT else 1
    width = weights[0].shape[at]
    depth = sum(w.shape[1 - at] for w in weights)
    return chain.call(
        "pull",
        functools.partial(pull_body, len(grads), dims),
        (*grads, *weights),
        [whole(g) for g in grads]
        + [
            pl.BlockSpec((block, w.shape[1]), lambda j: (j, 0))
            if dims == NT
            else pl.BlockSpec((w.shape[0], block), lambda j: (0, j))
            for w in weights
        ],
        [pl.BlockSpec((rows // blocks, block), lambda j: (0, j))] * blocks,
        [jax.ShapeDtypeStruct((rows // blocks, width), BF16)] * blocks,
        2 * rows * width * depth,
        grid=(width // block,),
    )


def push_body(blocks, perm_ref, rows_ref, weight_ref, out_ref):
    total = dot(rows_ref[...], weight_ref[...]).astype(BF16)
    rows = total.shape[0] // blocks
    for j in range(blocks):
        at = pl.ds(pl.multiple_of(perm_ref[j] * rows, rows), rows)
        out_ref[at] = total[j * rows : (j + 1) * rows]


def push(chain, perm, rows, weight, block=1024):
    count, depth = rows.shape
    width = weight.shape[1]
    return chain.call(
        "push",
        functools.partial(push_body, perm.shape[0]),
        (perm, rows, weight),
        [
            pl.BlockSpec((count, depth), lambda j, _: (0, 0)),
            pl.BlockSpec((depth, block), lambda j, _: (0, j)),
        ],
        [pl.BlockSpec((count, block), lambda j, _: (0, j))],
        [jax.ShapeDtypeStruct((count, width), BF16)],
        2 * count * depth * width,
        grid=(width // block,),
        scalars=1,
    )[0]


def terms_body(count, blocks, scalars, *refs):
    refs = refs[scalars:]
    wide, wide_pair = rows_of(refs[:count]), rows_of(refs[count : 2 * count])
    own, pair = refs[2 * count : 2 * count + 2]
    total = dot(wide, own[...], TN) + dot(wide_pair, pair[...], TN)
    if scalars == 3:
        refs[-1][...] = total.astype(BF16)
        return
    got, sent_ref, left_ref = refs[2 * count + 2 :]
    total = (total + got[...].astype(F32)).astype(BF16)

    @pl.when(pl.program_id(1) < blocks // 2)
    def _():
        sent_ref[...] = total

    @pl.when(pl.program_id(1) >= blocks // 2)
    def _():
        left_ref[...] = total


def weight_terms(chain, perm, wide, wide_pair, cols, cols_pair, narrow, narrow_pair, size, part, received=None, order=None):
    tokens, units = narrow.shape
    units //= part[1]
    blocks = cols.shape[0]
    block = units if units <= 2048 else math.gcd(2048, units)
    first = part[0] * (units // block)
    rows = tokens // len(wide)
    units_spec = pl.BlockSpec((tokens, block), lambda j, i, *_: (0, first + j))
    scalars = [cols, cols_pair, perm]
    in_specs = (
        part_specs(wide, rows, size, lambda j, i, *s: s[-3][i])
        + part_specs(wide_pair, rows, size, lambda j, i, *s: s[-2][i])
        + [units_spec, units_spec]
    )
    args = [*part_arrays(wide), *part_arrays(wide_pair), narrow, narrow_pair]
    if received is None:
        out_specs = [pl.BlockSpec((size, block), lambda j, i, *_: (i, j))]
        out = [jax.ShapeDtypeStruct((blocks * size, units), BF16)]
    else:
        half = blocks // 2
        scalars = [order] + scalars
        args.append(received)
        in_specs.append(pl.BlockSpec((size, block), lambda j, i, io, *_: (io[i], j)))
        out_specs = [
            pl.BlockSpec((size, block), lambda j, i, *_: (jnp.minimum(i, half - 1), j)),
            pl.BlockSpec((size, block), lambda j, i, *_: (jnp.maximum(i - half, 0), j)),
        ]
        out = [jax.ShapeDtypeStruct((half * size, units), BF16)] * 2
    return chain.call(
        "weight_terms",
        functools.partial(terms_body, len(wide), blocks, len(scalars)),
        (*scalars, *args),
        in_specs,
        out_specs,
        out,
        4 * tokens * units * blocks * size,
        grid=(units // block, blocks),
        scalars=len(scalars),
    )


def halve_body(mine, kept_send, got_send, kept, got, sent_ref, left_ref):
    sent_ref[...] = (kept_send[...].astype(F32) + got_send[...].astype(F32)).astype(BF16)
    left_ref[...] = (kept[...].astype(F32) + got[...].astype(F32)).astype(BF16)


def halve(chain, kept, received, mine, dim):
    steps = math.gcd(4, kept.shape[1 - dim] // 128)
    shape = list(kept.shape)
    shape[dim] //= 2
    block = list(shape)
    block[1 - dim] //= steps

    def spec(flip_half):
        def at(j, m):
            half = 1 - m[0] if flip_half else m[0]
            return (half, j) if dim == 0 else (j, half)

        return pl.BlockSpec(tuple(block), at)

    out_spec = pl.BlockSpec(tuple(block), lambda j, m: (0, j) if dim == 0 else (j, 0))
    out = jax.ShapeDtypeStruct(tuple(shape), BF16)
    return chain.call(
        "halve",
        halve_body,
        (mine, kept, received, kept, received),
        [spec(True), spec(True), spec(False), spec(False)],
        [out_spec, out_spec],
        [out, out],
        kept.size,
        grid=(steps,),
        scalars=1,
    )


def swap_halves(values_in):
    half = HD // 2
    width = values_in.shape[1]
    if width % 128:
        parts = []
        for at in range(0, width, HD):
            parts += [values_in[:, at + half : at + HD], values_in[:, at : at + half]]
        return jnp.concatenate(parts, axis=1)
    lane = lax.broadcasted_iota(jnp.int32, values_in.shape, 1)
    return jnp.where(
        lane % HD < half,
        pltpu.roll(values_in, width - half, 1),
        pltpu.roll(values_in, half, 1),
    )


def turn(values_in, cos_ref, sin_ref, sign):
    count = values_in.shape[1] // HD
    cos = jnp.concatenate([cos_ref[...]] * count, axis=1)
    sin = jnp.concatenate([sin_ref[...]] * count, axis=1)
    return values_in * cos + sign * (swap_halves(values_in) * sin)


def project_body(count, *refs):
    q_ref, k_ref, v_ref, cos_ref, sin_ref, kv_ref, query_ref = refs[count:]
    rows = rows_of(refs[:count])
    width = k_ref.shape[1]
    kv_ref[:, :width] = turn(dot(rows, k_ref[...]), cos_ref, sin_ref, 1.0).astype(BF16)
    kv_ref[:, width:] = dot(rows, v_ref[...]).astype(BF16)
    queries = turn(dot(rows, q_ref[...]), cos_ref, sin_ref, 1.0).astype(BF16)
    query_ref[...] = (queries.astype(F32) * (1.0 / math.sqrt(HD))).astype(BF16)


def project(chain, parts, w_query, w_key, w_value, cos, sin):
    count = sum(p.shape[0] for p in parts)
    kv = jax.ShapeDtypeStruct((count, 2 * w_key.shape[1]), BF16)
    query = jax.ShapeDtypeStruct((count, w_query.shape[1]), BF16)
    return chain.call(
        "project",
        functools.partial(project_body, len(parts)),
        (*parts, w_query, w_key, w_value, cos, sin),
        [VMEM] * (len(parts) + 5),
        [VMEM] * 2,
        [kv, query],
        2 * count * parts[0].shape[1] * (query.shape[1] + kv.shape[1]),
    )


def half_piece(places_ref, half, halves):
    top = places_ref[2] // halves
    return jnp.where(top == half, places_ref[0], 2 * places_ref[1] - 1 - places_ref[0])


def doc_start(places_ref, docs, position):
    end = 0
    start = position * 0
    for i in range(docs):
        end = end + places_ref[4 + i]
        start = jnp.where(position >= end, end, start)
    return start, position < end


def positions_of(places_ref, piece, halves, rows, shape, dim):
    row = lax.broadcasted_iota(jnp.int32, shape, dim)
    inner = lax.rem(places_ref[2], halves) * places_ref[3]
    return piece * rows + (row ^ inner)


def tiles_of(places_ref, docs, halves, rows, kv_ref, tile_refs):
    tiles = [(kv_ref, h * rows, half_piece(places_ref, h, halves)) for h in range(2)]
    for ref in tile_refs:
        for row in range(0, ref.shape[0], rows):
            tiles.append((ref, row, places_ref[4 + docs + len(tiles) - 2]))
    return tiles


def tile_count(tiles, rows):
    return sum(t.shape[0] for t in tiles) // rows + 2


def half_of(places_ref, docs, halves, half, rows):
    piece = half_piece(places_ref, half, halves)
    position = positions_of(places_ref, piece, halves, rows, (rows, 1), 0)
    start, valid = doc_start(places_ref, docs, position)
    return piece, position, start, valid, doc_start(places_ref, docs, piece * rows)[0]


def attend_body(docs, halves, count, places_ref, q_ref, kv_ref, *refs):
    tile_refs, (merged_ref, total_ref, scores_ref) = refs[:count], refs[count:]
    tokens, q_width = q_ref.shape
    rows = tokens // 2
    kv_heads = kv_ref.shape[1] // 2 // HD
    group = q_width // HD // kv_heads
    tiles = tiles_of(places_ref, docs, halves, rows, kv_ref, tile_refs)
    for half in range(2):
        at = pl.ds(half * rows, rows)
        q_piece, q_pos, q_start, valid, first = half_of(places_ref, docs, halves, half, rows)
        for g in range(kv_heads):
            stacked = jnp.concatenate(
                [q_ref[at, (g * group + i) * HD : (g * group + i + 1) * HD] for i in range(group)],
                axis=0,
            )
            peak_ref = scores_ref.at[len(tiles)]
            peak_ref[...] = jnp.full(peak_ref.shape, NEGATIVE, F32)
            for t, (ref, row, piece) in enumerate(tiles):

                @pl.when((piece <= q_piece) & ((piece + 1) * rows > first))
                def _(t=t, ref=ref, row=row, piece=piece):
                    keys = ref[row : row + rows, g * HD : (g + 1) * HD]
                    k_pos = positions_of(places_ref, piece, halves, rows, (1, rows), 1)
                    allowed = (k_pos <= q_pos) & (k_pos >= q_start)
                    scores = dot(stacked, keys, NT).reshape(group, rows, rows)
                    scores = jnp.where(allowed[None], scores, NEGATIVE).reshape(group * rows, rows)
                    scores_ref[t] = scores
                    peak_ref[...] = jnp.maximum(peak_ref[...], scores)

            peak = jnp.max(peak_ref[...], axis=1, keepdims=True)
            sums_ref = scores_ref.at[len(tiles), :, : 2 * HD]
            sums_ref[...] = jnp.zeros(sums_ref.shape, F32)
            for t, (ref, row, piece) in enumerate(tiles):

                @pl.when((piece <= q_piece) & ((piece + 1) * rows > first))
                def _(t=t, ref=ref, row=row):
                    values = ref[row : row + rows, (kv_heads + g) * HD : (kv_heads + g + 1) * HD]
                    values = jnp.concatenate([values, jnp.ones_like(values)], axis=1)
                    expo = jnp.exp(scores_ref[t] - peak).astype(BF16)
                    sums_ref[...] += dot(expo, values)

            sums = sums_ref[...]
            total = sums[:, HD : HD + 1]
            out = sums[:, :HD] / total
            log_total = peak + jnp.log(total)
            for i in range(group):
                head = g * group + i
                part = slice(i * rows, (i + 1) * rows)
                merged_ref[at, head * HD : (head + 1) * HD] = jnp.where(valid, out[part], 0.0).astype(BF16)
                total_ref[at, head : head + 1] = log_total[part]


def attend(chain, places, docs, halves, query, kv, tiles):
    tokens, width = query.shape
    rows = tokens // 2
    heads, kv_heads = width // HD, kv.shape[1] // 2 // HD
    return chain.call(
        "attend",
        functools.partial(attend_body, docs, halves, len(tiles)),
        (places, query, kv, *tiles),
        [SMEM] + [VMEM] * (2 + len(tiles)),
        [VMEM] * 2,
        [jax.ShapeDtypeStruct((tokens, width), BF16), jax.ShapeDtypeStruct((tokens, heads), F32)],
        8 * tokens * rows * tile_count(tiles, rows) * width,
        scratch=[pltpu.VMEM((1 + tile_count(tiles, rows), heads // kv_heads * rows, rows), F32)],
    )


def attend_back_body(docs, halves, count, parts, *refs):
    places_ref, q_ref, merged_ref, total_ref, cos_ref, sin_ref, w_ref = refs[:7]
    kv_ref, tile_refs = refs[7 + parts], refs[8 + parts : 8 + parts + count]
    grad_q_ref, grad_own_ref, *grad_tile_refs = refs[8 + parts + count : 10 + parts + 2 * count]
    grad_ref, q_sum_ref, kv_sum_ref = refs[10 + parts + 2 * count :]
    tokens, q_width = q_ref.shape
    rows = tokens // 2
    kv_heads = kv_ref.shape[1] // 2 // HD
    group = q_width // HD // kv_heads
    grad_ref[...] = dot(rows_of(refs[7 : 7 + parts]), w_ref[...], NT).astype(BF16)
    q_sum_ref[...] = jnp.zeros(q_sum_ref.shape, F32)
    kv_sum_ref[...] = jnp.zeros(kv_sum_ref.shape, F32)
    tiles = tiles_of(places_ref, docs, halves, rows, kv_ref, tile_refs)
    for half in range(2):
        at = pl.ds(half * rows, rows)
        q_piece, q_pos, q_start, valid, first = half_of(places_ref, docs, halves, half, rows)
        for g in range(kv_heads):
            heads = [slice((g * group + i) * HD, (g * group + i + 1) * HD) for i in range(group)]
            queries = jnp.concatenate([q_ref[at, h] for h in heads], axis=0)
            grads = jnp.concatenate(
                [jnp.where(valid, grad_ref[at, h].astype(F32), 0.0).astype(BF16) for h in heads], axis=0
            )
            outs = jnp.concatenate([merged_ref[at, h] for h in heads], axis=0)
            delta = jnp.sum(grads.astype(F32) * outs.astype(F32), axis=1, keepdims=True)
            totals = jnp.concatenate(
                [total_ref[at, g * group + i : g * group + i + 1] for i in range(group)], axis=0
            )
            for t, (ref, row, piece) in enumerate(tiles):

                @pl.when((piece <= q_piece) & ((piece + 1) * rows > first))
                def _(t=t, ref=ref, row=row, piece=piece):
                    keys = ref[row : row + rows, g * HD : (g + 1) * HD]
                    values = ref[row : row + rows, (kv_heads + g) * HD : (kv_heads + g + 1) * HD]
                    k_pos = positions_of(places_ref, piece, halves, rows, (1, rows), 1)
                    allowed = (k_pos <= q_pos) & (k_pos >= q_start)
                    scores = dot(queries, keys, NT) - totals
                    probs = jnp.exp(
                        jnp.where(allowed[None], scores.reshape(group, rows, rows), NEGATIVE)
                    ).reshape(group * rows, rows)
                    grad_probs = dot(grads, values, NT)
                    grad_scores = (probs * (grad_probs - delta)).astype(BF16)
                    q_sum_ref[half, g] += dot(grad_scores, keys)
                    kv_sum_ref[t, 0, g] += dot(grad_scores, queries, TN)
                    kv_sum_ref[t, 1, g] += dot(probs.astype(BF16), grads, TN)

            for i, head in enumerate(heads):
                part = q_sum_ref[half, g, i * rows : (i + 1) * rows] * (1.0 / math.sqrt(HD))
                part = part * cos_ref[at] - swap_halves(part) * sin_ref[at]
                grad_q_ref[at, head] = part.astype(BF16)
    targets = [
        (out, row) for out in (grad_own_ref, *grad_tile_refs) for row in range(0, out.shape[0], rows)
    ]
    for t, (out_ref, row) in enumerate(targets):
        for part in range(2):
            for g in range(kv_heads):
                cols = slice((part * kv_heads + g) * HD, (part * kv_heads + g + 1) * HD)
                out_ref[row : row + rows, cols] = kv_sum_ref[t, part, g].astype(out_ref.dtype)


def attend_back(chain, places, docs, halves, query, merged, totals, cos, sin, w_out, grads, kv, tiles):
    tokens, width = query.shape
    rows = tokens // 2
    kv_heads = kv.shape[1] // 2 // HD
    group = width // HD // kv_heads
    return chain.call(
        "attend_back",
        functools.partial(attend_back_body, docs, halves, len(tiles), len(grads)),
        (places, query, merged, totals, cos, sin, w_out, *grads, kv, *tiles),
        [SMEM] + [VMEM] * (7 + len(grads) + len(tiles)),
        [VMEM] * (2 + len(tiles)),
        [jax.ShapeDtypeStruct((tokens, width), BF16), jax.ShapeDtypeStruct(kv.shape, F32)]
        + [jax.ShapeDtypeStruct(t.shape, BF16) for t in tiles],
        16 * tokens * rows * tile_count(tiles, rows) * width,
        scratch=[
            pltpu.VMEM((tokens, width), BF16),
            pltpu.VMEM((2, kv_heads, group * rows, HD), F32),
            pltpu.VMEM((tile_count(tiles, rows), 2, kv_heads, rows, HD), F32),
        ],
    )


def finish_body(starts_ref, cos_ref, sin_ref, query_ref, own_ref, *refs):
    parts, (all_ref, key_ref, value_ref, total_ref) = refs[:-4], refs[-4:]
    total_ref[...] = own_ref[...]
    rows = own_ref.shape[0] // 2
    tiles = [(part, row) for part in parts for row in range(0, part.shape[0], rows)]
    for t, (part, row) in enumerate(tiles):
        at = pl.ds(pl.multiple_of(starts_ref[t] * rows, rows), rows)
        total_ref[at] += part[row : row + rows].astype(F32)
    width = key_ref.shape[1]
    keys = turn(total_ref[:, :width], cos_ref, sin_ref, -1.0).astype(BF16)
    values = total_ref[:, width:].astype(BF16)
    key_ref[...] = keys
    value_ref[...] = values
    wide = query_ref.shape[1]
    all_ref[:, :wide] = query_ref[...]
    all_ref[:, wide : wide + width] = keys
    all_ref[:, wide + width :] = values


def finish(chain, starts, cos, sin, grad_query, own, parts):
    tokens, width = own.shape
    wide = grad_query.shape[1] + width
    one = jax.ShapeDtypeStruct((tokens, width // 2), BF16)
    return chain.call(
        "finish",
        finish_body,
        (starts, cos, sin, grad_query, own, *parts),
        [SMEM] + [VMEM] * (4 + len(parts)),
        [VMEM] * 3,
        [jax.ShapeDtypeStruct((tokens, wide), BF16), one, one],
        20 * tokens * width,
        scratch=[pltpu.VMEM((tokens, width), F32)],
    )


def flip(values_in, axis, mask):
    count = lax.axis_size(axis)
    return lax.ppermute(values_in, axis, [(i, i ^ mask) for i in range(count)])


def after(values_in, *others):
    if not others:
        return values_in
    return lax.optimization_barrier((values_in, *others))[0]


def tp_gather(shard, *hold):
    count = lax.axis_size("tp")
    parts = {0: shard}
    mask = 2
    while mask < count:
        parts.update({j ^ mask: flip(part, "tp", mask) for j, part in parts.items()})
        mask *= 2
    across = {j ^ 1: flip(after(part, *hold) if hold and j else part, "tp", 1) for j, part in parts.items()}
    parts.update(across)
    return [parts[j] for j in range(count)]


def tp_gather_all(shard):
    whole_rows = lax.all_gather(shard, "tp", axis=0, tiled=True)
    return [(whole_rows, j) for j in range(lax.axis_size("tp"))]


def tp_scatter(terms, hold=lambda: ()):
    count = len(terms)
    blocks, received = {}, {j: flip(terms[j + 1], "tp", 1) for j in reversed(range(0, count, 2))}
    held = hold()
    for j, part in received.items():
        blocks[j] = terms[j].astype(F32) + after(part, *held).astype(F32)
    mask = count // 2
    while mask > 2:
        for j in range(0, mask, 2):
            blocks[j] = blocks[j] + flip(blocks[j + mask].astype(BF16), "tp", mask).astype(F32)
        mask //= 2
    sent = blocks[2].astype(BF16)
    return sent, lambda *held: blocks[0] + after(flip(sent, "tp", 2), *held).astype(F32)


def sum_over(values_in, axis):
    mask = 1
    while mask < lax.axis_size(axis):
        values_in = values_in + flip(values_in, axis, mask)
        mask *= 2
    return values_in


def tile_plan(count):
    ends = 2 * count + 3
    needed = []
    for c in range(count):
        pieces = set()
        for held in (c, 2 * count - 1 - c):
            first = ends // 2 if 2 * held >= ends else 0
            pieces |= set(range(first, held + 1))
        needed.append(pieces - {c, 2 * count - 1 - c})
    plan = []
    for k in range(1, count):
        chosen = {}
        for c in range(count):
            source = (c + k) % count
            pieces = sorted(needed[c] & {source, 2 * count - 1 - source})
            if pieces:
                chosen[source] = (c, pieces)
        if chosen:
            plan.append(([(s, c) for s, (c, _) in chosen.items()], {s: p for s, (_, p) in chosen.items()}))
    return plan


def other_columns(values_in, pick_odd, size):
    blocks = values_in.shape[1] // size
    even, odd = (
        jnp.concatenate([values_in[:, b * size : (b + 1) * size] for b in range(at, blocks, 2)], axis=1)
        for at in (0, 1)
    )
    return jnp.where(pick_odd, odd, even)


def per_device(
    tokens,
    attn_gain,
    w_query,
    w_key,
    w_value,
    w_out,
    ffn_gain,
    w_gate,
    w_up,
    w_down,
    out_cotangent,
    doc_lengths,
):
    ctx_count, ctx_rank = lax.axis_size("ctx"), lax.axis_index("ctx")
    dp_count, dp_rank = lax.axis_size("dp"), lax.axis_index("dp")
    tp_count, tp_rank = lax.axis_size("tp"), lax.axis_index("tp")
    tp_rows, width = tokens.shape[1:]
    ctx_rows = tp_rows * tp_count
    near_rows = ctx_rows // 2
    halves = tp_count // 2
    docs = doc_lengths.shape[1]
    size = width // (dp_count * ctx_count)
    chain = Chain()

    plan = tile_plan(ctx_count)
    nowhere = 2 * ctx_count
    widths = [max(len(p) for p in pieces.values()) for _, pieces in plan]
    got = np.full((ctx_count, sum(widths)), nowhere, np.int32)
    gave = np.zeros((ctx_count, sum(widths)), np.int32)
    for t, (moves, pieces) in enumerate(plan):
        first = sum(widths[:t])
        for source, target in moves:
            listed = pieces[source]
            got[target, first : first + len(listed)] = listed
            high = int(listed[0] != source)
            gave[source, first : first + widths[t]] = [high, 1 - high][: widths[t]]
    top = tp_rank // halves
    starts = jnp.asarray(gave)[ctx_rank] ^ top
    here = jnp.stack([ctx_rank, jnp.int32(ctx_count), tp_rank, jnp.int32(tp_rows)])
    places = jnp.concatenate([here, doc_lengths[0], jnp.asarray(got)[ctx_rank]]).astype(jnp.int32)

    within = jnp.arange(ctx_rows, dtype=jnp.int32) ^ (tp_rank * tp_rows)
    piece = jnp.where(within < near_rows, ctx_rank, 2 * ctx_count - 1 - ctx_rank)
    position = (piece * near_rows + within % near_rows).astype(F32)
    inv_freq = jnp.asarray(rope_table(HD), F32)
    angles = position[:, None] * inv_freq[None, :]
    cosine, sine = jnp.cos(angles), jnp.sin(angles)
    cos = jnp.concatenate([cosine, cosine], axis=1)
    sin = jnp.concatenate([-sine, sine], axis=1)

    perm = jnp.arange(tp_count, dtype=jnp.int32) ^ tp_rank
    mine = ctx_rank % 2
    pairs = ctx_count // 2
    steps = jnp.arange(pairs, dtype=jnp.int32)

    def cols_of(dp_index):
        return (dp_index * ctx_count + 2 * steps + mine).astype(jnp.int32)

    def packed_cols_of(dp_index):
        return (dp_index * pairs + steps).astype(jnp.int32)

    bit = ctx_rank // pairs % 2
    order = ((1 - bit) * (pairs // 2) + steps) % pairs

    class WeightGrad:
        def __init__(self, wide, wide_pair, packed, narrow, narrow_pair, part=(0, 1)):
            def terms(dp_index, *received):
                cols = cols_of(dp_index)
                cols_pair = packed_cols_of(dp_index) if packed else cols
                if received:
                    cols, cols_pair = cols[order], cols_pair[order]
                return weight_terms(
                    chain, perm, wide, wide_pair, cols, cols_pair, narrow, narrow_pair, size, part, *received
                )

            self.terms = terms

        def send(self):
            self.sent = self.terms(1 - dp_rank)[0]
            self.received = flip(self.sent, "dp", 1)
            return self

        def keep(self):
            sent, self.kept = self.terms(dp_rank, self.received, order)
            self.received = flip(sent, "ctx", pairs)
            mask = pairs // 2
            while mask > 1:
                half = jnp.reshape(ctx_rank // mask % 2, (1,))
                sent, self.kept = halve(chain, self.kept, self.received, half, 0)
                self.received = flip(sent, "ctx", mask)
                mask //= 2

        def total(self, *others):
            return after(self.kept, *others).astype(F32) + self.received.astype(F32)

    inputs = tokens[0].astype(F32)
    normed_local = rms_norm(inputs, attn_gain).astype(BF16)
    normed = tp_gather(normed_local, cos, sin, places)
    grad_fb_local = out_cotangent[0]
    fb_shard = flip(grad_fb_local, "ctx", 1)
    normed_shard = flip(other_columns(normed_local, mine == 0, size), "ctx", 1)
    chain.wait(fb_shard)
    kv, query = project(chain, normed, w_query, w_key, w_value, cos, sin)
    low_half = lax.dynamic_slice_in_dim(kv, top * near_rows, near_rows, 0)
    high_half = lax.dynamic_slice_in_dim(kv, (1 - top) * near_rows, near_rows, 0)
    tiles = []
    for t, (moves, _) in enumerate(plan):
        low_first = jnp.asarray(gave)[ctx_rank, sum(widths[:t])] == 0
        held = [jnp.where(low_first, low_half, high_half), jnp.where(low_first, high_half, low_half)]
        held = jnp.concatenate(held[: widths[t]], axis=0)
        tiles.append(lax.ppermute(held, "ctx", moves))
    grad_fb = tp_gather_all(after(grad_fb_local, kv))
    grad_fb_pair = tp_gather_all(after(fb_shard, kv))
    normed_pair = tp_gather_all(after(normed_shard, kv))
    chain.wait(normed_shard)
    merged, totals = attend(chain, places, docs, halves, query, kv, tiles)
    out_terms = pull(chain, [merged], [w_out], tp_count, NN)
    _, attention = tp_scatter(out_terms)
    merged_pair = flip(merged, "ctx", 1)
    hidden_state = inputs + attention()

    normed_ffn_local = rms_norm(hidden_state, ffn_gain).astype(BF16)
    normed_ffn = tp_gather(normed_ffn_local)
    act, slope, silu = ffn_front(chain, normed_ffn, w_gate, w_up)
    ffn_shard = flip(after(normed_ffn_local, normed_ffn[1]), "ctx", 1)
    normed_ffn_pair = tp_gather(ffn_shard, act)
    chain.wait(merged_pair)
    act_pair, slope_pair, silu_pair = ffn_front(chain, normed_ffn_pair, w_gate, w_up)

    down_w = WeightGrad(grad_fb, grad_fb_pair, False, act, act_pair).send()
    grad_gate, grad_up = ffn_back(chain, perm, grad_fb, w_down, slope, silu)
    nffn_terms = pull(chain, [grad_gate, grad_up], [w_gate, w_up], tp_count)
    nffn_sent, nffn_sum = tp_scatter(nffn_terms)
    grad_gate_pair, grad_up_pair = ffn_back(chain, perm, grad_fb_pair, w_down, slope_pair, silu_pair)
    chain.wait(nffn_sent)
    gate_w = WeightGrad(normed_ffn, normed_ffn_pair, False, grad_gate, grad_gate_pair).send()
    up_w = WeightGrad(normed_ffn, normed_ffn_pair, False, grad_up, grad_up_pair)
    down_w.keep()
    grad_nffn = nffn_sum()
    grad_state_norm, grad_ffn_gain = jax.vjp(rms_norm, hidden_state, ffn_gain)[1](grad_nffn)
    grad_state = grad_fb_local.astype(F32) + grad_state_norm
    grad_sb_local = grad_state.astype(BF16)
    grad_sb = tp_gather(grad_sb_local)
    chain.wait(grad_sb_local)
    up_w.send()
    layer_terms = push(chain, perm, act, w_down)
    layer_sum = lax.psum_scatter(layer_terms, "tp", scatter_dimension=0, tiled=True)
    layer_out = (hidden_state + layer_sum.astype(F32)).astype(BF16)

    grad_query, own, *sent = attend_back(
        chain, places, docs, halves, query, merged, totals, cos, sin, w_out, grad_sb, kv, tiles
    )
    returned = [
        lax.ppermute(part, "ctx", [(target, source) for source, target in moves])
        for part, (moves, _) in zip(sent, plan)
    ]
    chain.wait(down_w.received)
    gate_w.keep()
    grad_sb_shard = flip(other_columns(after(grad_sb_local, *chain.held), mine == 0, size), "ctx", 1)
    grad_qkv, grad_key, grad_value = finish(chain, starts, cos, sin, grad_query, own, returned)
    grad_qkv_pair = flip(grad_qkv, "ctx", 1)
    grad_sb_pair = tp_gather(grad_sb_shard)
    back_terms = pull(chain, [grad_query, grad_key, grad_value], [w_query, w_key, w_value], tp_count)
    out_w = WeightGrad(grad_sb, grad_sb_pair, True, merged, merged_pair).send()
    normed_sent, normed_sum = tp_scatter(back_terms)
    up_w.keep()
    qkv_w = WeightGrad(normed, normed_pair, True, grad_qkv, grad_qkv_pair).send()
    out_w.keep()
    qkv_w.keep()
    zero = jnp.minimum(jnp.abs(qkv_w.kept[0, 0].astype(F32)), 0.0)
    grad_normed = normed_sum() + zero
    grad_input_norm, grad_attn_gain = jax.vjp(rms_norm, inputs, attn_gain)[1](grad_normed)
    input_grad = grad_state + grad_input_norm
    gains = jnp.stack([grad_attn_gain, grad_ffn_gain])
    for axis in ("tp", "dp", "ctx"):
        gains = sum_over(gains, axis)
    q_width, kv_width = w_query.shape[1], w_key.shape[1]
    out_total = out_w.total(zero).T
    qkv_total = qkv_w.total(zero)
    return (
        layer_out[None],
        input_grad[None],
        gains[0],
        qkv_total[:, :q_width],
        qkv_total[:, q_width : q_width + kv_width],
        qkv_total[:, q_width + kv_width :],
        out_total,
        gains[1],
        gate_w.total(zero),
        up_w.total(zero),
        down_w.total(zero).T,
    )


def solution(mesh):
    placed = (
        P("dp", ("ctx", "tp"), None),
        P(),
        P(None, "tp"),
        P(None, "tp"),
        P(None, "tp"),
        P("tp", None),
        P(),
        P(None, "tp"),
        P(None, "tp"),
        P("tp", None),
        P("dp", ("ctx", "tp"), None),
        P("dp", None),
    )
    return jax.shard_map(
        per_device,
        mesh=mesh,
        in_specs=placed,
        out_specs=(
            P("dp", ("ctx", "tp"), None),
            P("dp", ("ctx", "tp"), None),
            P(),
            P(("dp", "ctx"), "tp"),
            P(("dp", "ctx"), "tp"),
            P(("dp", "ctx"), "tp"),
            P("tp", ("dp", "ctx")),
            P(),
            P(("dp", "ctx"), "tp"),
            P(("dp", "ctx"), "tp"),
            P("tp", ("dp", "ctx")),
        ),
        check_vma=False,
    )
```

```python
import functools
import math

import jax
import jax.numpy as jnp
import numpy as np
from jax import lax
from jax.experimental import pallas as pl
from jax.experimental.pallas import tpu as pltpu
from jax.sharding import PartitionSpec as P

HD = 64
EPSILON = 1e-05
NEGATIVE = -1e30
ROPE_THETA = 500000.0


def rope_table(head_size):
    base_freq = np.array(
        [ROPE_THETA ** (-2.0 * index / head_size) for index in range(head_size // 2)]
    )
    wavelength = 2.0 * math.pi / base_freq
    blend = (8192.0 / wavelength - 1.0) / 3.0
    middle = (1.0 - blend) * base_freq / 32.0 + blend * base_freq
    return np.where(
        wavelength > 8192.0, base_freq / 32.0, np.where(wavelength < 2048.0, base_freq, middle)
    )


def rms_norm(values_in, gain_vec):
    return (
        values_in
        * lax.rsqrt(jnp.mean(values_in * values_in, axis=-1, keepdims=True) + EPSILON)
        * gain_vec
    )


F32, BF16 = jnp.float32, jnp.bfloat16
VMEM_BYTES = 62 * 1024 * 1024
NN = (((1,), (0,)), ((), ()))
NT = (((1,), (1,)), ((), ()))
TN = (((0,), (0,)), ((), ()))
VMEM = pl.BlockSpec(memory_space=pltpu.VMEM)
SMEM = pl.BlockSpec(memory_space=pltpu.SMEM)
ANYWHERE = pl.BlockSpec(memory_space=pl.ANY)


def dot(left, right, dims=NN):
    return lax.dot_general(left, right, dims, preferred_element_type=F32)


def part_specs(parts, rows, width, col):
    def spec(part):
        if not isinstance(part, tuple):
            return pl.BlockSpec((rows, width), lambda *at: (0, col(*at)))
        j, first = part[1:]
        return pl.BlockSpec(
            (rows, width), lambda *at: (0 if j is None else at[-1][j], first // width + col(*at))
        )

    return [spec(part) for part in parts]


def part_arrays(parts):
    return [part[0] if isinstance(part, tuple) else part for part in parts]


def rows_of(refs):
    return jnp.concatenate([ref[...] for ref in refs], axis=0)


class Chain:
    def __init__(self):
        self.held = []
        self.cost = 58 * 10**8

    def wait(self, *arrays):
        self.held = [*arrays, *self.held]

    def call(
        self, name, body, args, in_specs, out_specs, out_shape, flops, grid=(), scalars=0, scratch=(), zero=False
    ):
        held, count, outs = self.held, len(args), len(out_shape)
        marks, mark_specs = [jax.ShapeDtypeStruct((8, 128), F32)], [ANYWHERE]
        if zero:
            marks.append(jax.ShapeDtypeStruct((1, 1), F32))
            mark_specs.append(SMEM)

        def inner(*refs):
            rest = refs[count + len(held) :]
            given = refs[:scalars] + refs[scalars + len(held) : count + len(held)]
            body(*given, *rest[:outs], *rest[outs + len(marks) :])
            if zero:
                rest[outs + 1][0, 0] = 0.0

        results = pl.pallas_call(
            inner,
            grid_spec=pltpu.PrefetchScalarGridSpec(
                num_scalar_prefetch=scalars,
                grid=grid,
                in_specs=[ANYWHERE] * len(held) + list(in_specs),
                out_specs=[*out_specs, *mark_specs],
                scratch_shapes=list(scratch),
            ),
            out_shape=[*out_shape, *marks],
            compiler_params=pltpu.CompilerParams(
                vmem_limit_bytes=VMEM_BYTES, dimension_semantics=("arbitrary",) * len(grid)
            ),
            cost_estimate=pl.CostEstimate(flops=self.cost, bytes_accessed=1, transcendentals=0),
            name=name,
        )(*args[:scalars], *held, *args[scalars:])
        self.held = [results[outs]]
        if zero:
            self.zero = results[outs + 1][0, 0]
        return results[:outs]


def fill_rows(parts, rows_ref):
    @pl.when(pl.program_id(0) == 0)
    def _():
        rows_ref[...] = rows_of(parts)


def ffn_front_body(count, *refs):
    gate_ref, up_ref, act_ref, slope_ref, silu_ref, rows_ref = refs[count:]
    fill_rows(refs[:count], rows_ref)
    rows = rows_ref[...]
    gate = dot(rows, gate_ref[...])
    up = dot(rows, up_ref[...])
    sigma = 1.0 / (1.0 + jnp.exp(-gate))
    silu = gate * sigma
    act_ref[...] = (silu * up).astype(BF16)
    slope_ref[...] = (up * sigma * (1.0 + gate * (1.0 - sigma))).astype(BF16)
    silu_ref[...] = silu.astype(BF16)


def whole(array):
    return pl.BlockSpec(array.shape, lambda *_: (0,) * array.ndim)


def ffn_front(chain, parts, w_gate, w_up, part=(0, 1), block=512):
    count, width = sum(p.shape[0] for p in parts), parts[0].shape[1]
    units = w_gate.shape[1] // part[1]
    block = min(block, units)
    first = part[0] * (units // block)
    weight = pl.BlockSpec((width, block), lambda j: (0, first + j))
    return chain.call(
        "ffn_front",
        functools.partial(ffn_front_body, len(parts)),
        (*parts, w_gate, w_up),
        [whole(p) for p in parts] + [weight, weight],
        [pl.BlockSpec((count, block), lambda j: (0, j))] * 3,
        [jax.ShapeDtypeStruct((count, units), BF16)] * 3,
        4 * count * width * units,
        grid=(units // block,),
        scratch=[pltpu.VMEM((count, width), BF16)],
        zero=True,
    )


def ffn_back_body(count, perm_ref, *refs):
    down_ref, slope_ref, silu_ref, gate_ref, up_ref, rows_ref = refs[count:]
    fill_rows(refs[:count], rows_ref)
    grad_act = dot(rows_ref[...], down_ref[...], NT)
    gate_ref[...] = (grad_act * slope_ref[...].astype(F32)).astype(BF16)
    up_ref[...] = (grad_act * silu_ref[...].astype(F32)).astype(BF16)


def ffn_back(chain, perm, parts, w_down, slope, silu, block=512):
    count, units = slope.shape
    width = w_down.shape[1]
    block = min(block, units)
    tile = pl.BlockSpec((count, block), lambda j, _: (0, j))
    return chain.call(
        "ffn_back",
        functools.partial(ffn_back_body, len(parts)),
        (perm, *part_arrays(parts), w_down, slope, silu),
        part_specs(parts, count // len(parts), width, lambda *_: 0)
        + [pl.BlockSpec((block, width), lambda j, _: (j, 0)), tile, tile],
        [tile, tile],
        [jax.ShapeDtypeStruct((count, units), BF16)] * 2,
        2 * count * width * units,
        grid=(units // block,),
        scalars=1,
        scratch=[pltpu.VMEM((count, width), BF16)],
    )


def pull_body(count, dims, *refs):
    total = dot(refs[0][...], refs[count][...], dims)
    for i in range(1, count):
        total = total + dot(refs[i][...], refs[count + i][...], dims)
    outs = refs[2 * count :]
    rows = total.shape[0] // len(outs)
    for j, out in enumerate(outs):
        out[...] = total[j * rows : (j + 1) * rows].astype(BF16)


def pull(chain, grads, weights, blocks, dims=NT, block=1024):
    rows, at = grads[0].shape[0], 0 if dims == NT else 1
    width = weights[0].shape[at]
    depth = sum(w.shape[1 - at] for w in weights)
    return chain.call(
        "pull",
        functools.partial(pull_body, len(grads), dims),
        (*grads, *weights),
        [whole(g) for g in grads]
        + [
            pl.BlockSpec((block, w.shape[1]), lambda j: (j, 0))
            if dims == NT
            else pl.BlockSpec((w.shape[0], block), lambda j: (0, j))
            for w in weights
        ],
        [pl.BlockSpec((rows // blocks, block), lambda j: (0, j))] * blocks,
        [jax.ShapeDtypeStruct((rows // blocks, width), BF16)] * blocks,
        2 * rows * width * depth,
        grid=(width // block,),
        zero=True,
    )


def push_body(blocks, perm_ref, rows_ref, weight_ref, out_ref):
    total = dot(rows_ref[...], weight_ref[...]).astype(BF16)
    rows = total.shape[0] // blocks
    for j in range(blocks):
        at = pl.ds(pl.multiple_of(perm_ref[j] * rows, rows), rows)
        out_ref[at] = total[j * rows : (j + 1) * rows]


def push(chain, perm, rows, weight, block=1024):
    count, depth = rows.shape
    width = weight.shape[1]
    return chain.call(
        "push",
        functools.partial(push_body, perm.shape[0]),
        (perm, rows, weight),
        [
            pl.BlockSpec((count, depth), lambda j, _: (0, 0)),
            pl.BlockSpec((depth, block), lambda j, _: (0, j)),
        ],
        [pl.BlockSpec((count, block), lambda j, _: (0, j))],
        [jax.ShapeDtypeStruct((count, width), BF16)],
        2 * count * depth * width,
        grid=(width // block,),
        scalars=1,
    )[0]


def terms_body(count, blocks, scalars, *refs):
    refs = refs[scalars:]
    wide, wide_pair = rows_of(refs[:count]), rows_of(refs[count : 2 * count])
    own, pair = refs[2 * count : 2 * count + 2]
    total = dot(wide, own[...], TN) + dot(wide_pair, pair[...], TN)
    if scalars == 3:
        refs[-1][...] = total.astype(BF16)
        return
    got, sent_ref, left_ref = refs[2 * count + 2 :]
    total = (total + got[...].astype(F32)).astype(BF16)

    @pl.when(pl.program_id(1) < blocks // 2)
    def _():
        sent_ref[...] = total

    @pl.when(pl.program_id(1) >= blocks // 2)
    def _():
        left_ref[...] = total


def weight_terms(chain, perm, wide, wide_pair, cols, cols_pair, narrow, narrow_pair, size, part, received=None, order=None, zero=False):
    tokens, units = narrow.shape
    units //= part[1]
    blocks = cols.shape[0]
    block = units if units <= 2048 else math.gcd(2048, units)
    first = part[0] * (units // block)
    rows = tokens // len(wide)
    units_spec = pl.BlockSpec((tokens, block), lambda j, i, *_: (0, first + j))
    scalars = [cols, cols_pair, perm]
    in_specs = (
        part_specs(wide, rows, size, lambda j, i, *s: s[-3][i])
        + part_specs(wide_pair, rows, size, lambda j, i, *s: s[-2][i])
        + [units_spec, units_spec]
    )
    args = [*part_arrays(wide), *part_arrays(wide_pair), narrow, narrow_pair]
    if received is None:
        out_specs = [pl.BlockSpec((size, block), lambda j, i, *_: (i, j))]
        out = [jax.ShapeDtypeStruct((blocks * size, units), BF16)]
    else:
        half = blocks // 2
        scalars = [order] + scalars
        args.append(received)
        in_specs.append(pl.BlockSpec((size, block), lambda j, i, io, *_: (io[i], j)))
        out_specs = [
            pl.BlockSpec((size, block), lambda j, i, *_: (jnp.minimum(i, half - 1), j)),
            pl.BlockSpec((size, block), lambda j, i, *_: (jnp.maximum(i - half, 0), j)),
        ]
        out = [jax.ShapeDtypeStruct((half * size, units), BF16)] * 2
    return chain.call(
        "weight_terms",
        functools.partial(terms_body, len(wide), blocks, len(scalars)),
        (*scalars, *args),
        in_specs,
        out_specs,
        out,
        4 * tokens * units * blocks * size,
        grid=(units // block, blocks),
        scalars=len(scalars),
        zero=zero or received is not None,
    )


def own_terms_body(count, blocks, scalars, *refs):
    refs = refs[scalars:]
    total = dot(rows_of(refs[:count]), refs[count][...], TN)
    if scalars == 2:
        refs[-1][...] = total.astype(BF16)
        return
    got, sent_ref, left_ref = refs[count + 1 :]
    total = (total + got[...].astype(F32)).astype(BF16)

    @pl.when(pl.program_id(0) < blocks // 2)
    def _():
        sent_ref[...] = total

    @pl.when(pl.program_id(0) >= blocks // 2)
    def _():
        left_ref[...] = total


def own_terms(chain, perm, wide, cols, narrow, size, received=None, order=None):
    tokens, units = narrow.shape
    blocks = cols.shape[0]
    rows = tokens // len(wide)
    half = blocks // 2
    scalars = [cols, perm]
    args = [*part_arrays(wide), narrow]
    in_specs = part_specs(wide, rows, size, lambda i, *s: s[-2][i]) + [whole(narrow)]
    if received is None:
        out_specs = [pl.BlockSpec((size, units), lambda i, *_: (i, 0))]
        out = [jax.ShapeDtypeStruct((blocks * size, units), BF16)]
    else:
        scalars = [order] + scalars
        args.append(received)
        in_specs.append(pl.BlockSpec((size, units), lambda i, io, *_: (io[i], 0)))
        out_specs = [
            pl.BlockSpec((size, units), lambda i, *_: (jnp.minimum(i, half - 1), 0)),
            pl.BlockSpec((size, units), lambda i, *_: (jnp.maximum(i - half, 0), 0)),
        ]
        out = [jax.ShapeDtypeStruct((half * size, units), BF16)] * 2
    return chain.call(
        "own_terms",
        functools.partial(own_terms_body, len(wide), blocks, len(scalars)),
        (*scalars, *args),
        in_specs,
        out_specs,
        out,
        2 * tokens * units * blocks * size,
        grid=(blocks,),
        scalars=len(scalars),
        zero=True,
    )


def halve_body(mine, kept_send, got_send, kept, got, sent_ref, left_ref):
    sent_ref[...] = (kept_send[...].astype(F32) + got_send[...].astype(F32)).astype(BF16)
    left_ref[...] = (kept[...].astype(F32) + got[...].astype(F32)).astype(BF16)


def halve(chain, kept, received, mine, dim):
    steps = math.gcd(4, kept.shape[1 - dim] // 128)
    shape = list(kept.shape)
    shape[dim] //= 2
    block = list(shape)
    block[1 - dim] //= steps

    def spec(flip_half):
        def at(j, m):
            half = 1 - m[0] if flip_half else m[0]
            return (half, j) if dim == 0 else (j, half)

        return pl.BlockSpec(tuple(block), at)

    out_spec = pl.BlockSpec(tuple(block), lambda j, m: (0, j) if dim == 0 else (j, 0))
    out = jax.ShapeDtypeStruct(tuple(shape), BF16)
    return chain.call(
        "halve",
        halve_body,
        (mine, kept, received, kept, received),
        [spec(True), spec(True), spec(False), spec(False)],
        [out_spec, out_spec],
        [out, out],
        kept.size,
        grid=(steps,),
        scalars=1,
        zero=True,
    )


def swap_halves(values_in):
    half = HD // 2
    width = values_in.shape[1]
    if width % 128:
        parts = []
        for at in range(0, width, HD):
            parts += [values_in[:, at + half : at + HD], values_in[:, at : at + half]]
        return jnp.concatenate(parts, axis=1)
    lane = lax.broadcasted_iota(jnp.int32, values_in.shape, 1)
    return jnp.where(
        lane % HD < half,
        pltpu.roll(values_in, width - half, 1),
        pltpu.roll(values_in, half, 1),
    )


def turn(values_in, cos_ref, sin_ref, sign):
    count = values_in.shape[1] // HD
    cos = jnp.concatenate([cos_ref[...]] * count, axis=1)
    sin = jnp.concatenate([sin_ref[...]] * count, axis=1)
    return values_in * cos + sign * (swap_halves(values_in) * sin)


def project_body(count, *refs):
    q_ref, k_ref, v_ref, cos_ref, sin_ref, kv_ref, query_ref = refs[count:]
    rows = rows_of(refs[:count])
    width = k_ref.shape[1]
    kv_ref[:, :width] = turn(dot(rows, k_ref[...]), cos_ref, sin_ref, 1.0).astype(BF16)
    kv_ref[:, width:] = dot(rows, v_ref[...]).astype(BF16)
    queries = turn(dot(rows, q_ref[...]), cos_ref, sin_ref, 1.0).astype(BF16)
    query_ref[...] = (queries.astype(F32) * (1.0 / math.sqrt(HD))).astype(BF16)


def project(chain, parts, w_query, w_key, w_value, cos, sin):
    count = sum(p.shape[0] for p in parts)
    kv = jax.ShapeDtypeStruct((count, 2 * w_key.shape[1]), BF16)
    query = jax.ShapeDtypeStruct((count, w_query.shape[1]), BF16)
    return chain.call(
        "project",
        functools.partial(project_body, len(parts)),
        (*parts, w_query, w_key, w_value, cos, sin),
        [VMEM] * (len(parts) + 5),
        [VMEM] * 2,
        [kv, query],
        2 * count * parts[0].shape[1] * (query.shape[1] + kv.shape[1]),
    )


def half_piece(places_ref, half, halves):
    top = places_ref[2] // halves
    return jnp.where(top == half, places_ref[0], 2 * places_ref[1] - 1 - places_ref[0])


def doc_start(places_ref, docs, position):
    end = 0
    start = position * 0
    for i in range(docs):
        end = end + places_ref[4 + i]
        start = jnp.where(position >= end, end, start)
    return start, position < end


def positions_of(places_ref, piece, halves, rows, shape, dim):
    row = lax.broadcasted_iota(jnp.int32, shape, dim)
    inner = lax.rem(places_ref[2], halves) * places_ref[3]
    return piece * rows + (row ^ inner)


def tile_count(tiles, rows):
    return sum(t.shape[0] for t in tiles) // rows + 2


def half_of(places_ref, docs, halves, half, rows, group):
    piece = half_piece(places_ref, half, halves)
    position = positions_of(places_ref, piece, halves, rows, (1, rows), 1)
    start, valid = doc_start(places_ref, docs, position)
    first = doc_start(places_ref, docs, piece * rows)[0]
    position, start, valid = (
        jnp.concatenate([v] * group, axis=1) for v in (position, start, valid.astype(jnp.int32))
    )
    return piece, position, start, valid, first


def tile_piece(places_ref, docs, halves, t):
    given = places_ref[4 + docs + jnp.maximum(t - 2, 0)]
    own = jnp.where(t == 0, half_piece(places_ref, 0, halves), half_piece(places_ref, 1, halves))
    return jnp.where(t < 2, own, given)


def split_tiles(kv_refs, rows, keys_ref, values_ref, ones):
    kv_heads = keys_ref.shape[0]
    t = 0
    for ref in kv_refs:
        for row in range(0, ref.shape[0], rows):
            for g in range(kv_heads):
                keys_ref[g, t] = ref[row : row + rows, g * HD : (g + 1) * HD]
                values = ref[row : row + rows, (kv_heads + g) * HD : (kv_heads + g + 1) * HD]
                if ones:
                    values = jnp.concatenate([values, jnp.ones_like(values)], axis=1)
                values_ref[g, t] = values
            t += 1


def split_heads(ref, rows, group, out_ref, change=lambda v, half: v):
    kv_heads = out_ref.shape[0] // 2
    for half in range(2):
        for g in range(kv_heads):
            for i in range(group):
                head = (g * group + i) * HD
                values = ref[half * rows : (half + 1) * rows, head : head + HD]
                out_ref[half * kv_heads + g, i * rows : (i + 1) * rows] = change(values, half)


def attend_body(docs, halves, count, places_ref, q_ref, kv_ref, *refs):
    tile_refs, (merged_ref, total_ref) = refs[:count], refs[count : count + 2]
    keys_ref, values_ref, stack_ref, scores_ref, peak_ref, sums_ref, out_ref = refs[count + 2 :]
    rows = q_ref.shape[0] // 2
    kv_heads, tiles = keys_ref.shape[:2]
    group = q_ref.shape[1] // HD // kv_heads
    split_tiles([kv_ref, *tile_refs], rows, keys_ref, values_ref, True)
    split_heads(q_ref, rows, group, stack_ref)

    def one(hg, carry):
        half, g = hg // kv_heads, hg % kv_heads
        q_piece, q_pos, q_start, valid, first = half_of(places_ref, docs, halves, half, rows, group)
        peak_ref[...] = jnp.full(peak_ref.shape, NEGATIVE, F32)
        sums_ref[...] = jnp.zeros(sums_ref.shape, F32)

        def score(t, carry):
            piece = tile_piece(places_ref, docs, halves, t)

            @pl.when((piece <= q_piece) & ((piece + 1) * rows > first))
            def _():
                k_pos = positions_of(places_ref, piece, halves, rows, (rows, 1), 0)
                scores = dot(keys_ref[g, t], stack_ref[hg], NT)
                scores = jnp.where((k_pos <= q_pos) & (k_pos >= q_start), scores, NEGATIVE)
                scores_ref[t] = scores
                top = jnp.max(scores.reshape(rows // 8, 8, group * rows), axis=0)
                peak_ref[...] = jnp.maximum(peak_ref[...], top)

            return carry

        lax.fori_loop(0, tiles, score, 0)
        peak = jnp.max(peak_ref[...], axis=0, keepdims=True)

        def weigh(t, carry):
            piece = tile_piece(places_ref, docs, halves, t)

            @pl.when((piece <= q_piece) & ((piece + 1) * rows > first))
            def _():
                expo = jnp.exp(scores_ref[t] - peak).astype(BF16)
                sums_ref[...] += dot(values_ref[g, t], expo, TN)

            return carry

        lax.fori_loop(0, tiles, weigh, 0)
        total = sums_ref[HD : HD + 1]
        out_ref[hg] = jnp.where(valid > 0, sums_ref[...] / total, 0.0).T.astype(BF16)
        total_ref[hg] = peak + jnp.log(total)
        return carry

    lax.fori_loop(0, 2 * kv_heads, one, 0)
    for half in range(2):
        for g in range(kv_heads):
            for i in range(group):
                head = (g * group + i) * HD
                merged_ref[half * rows : (half + 1) * rows, head : head + HD] = out_ref[
                    half * kv_heads + g, i * rows : (i + 1) * rows, :HD
                ]


def attend(chain, places, docs, halves, query, kv, tiles):
    tokens, width = query.shape
    rows = tokens // 2
    heads, kv_heads = width // HD, kv.shape[1] // 2 // HD
    span = heads // kv_heads * rows
    tile_num = tile_count(tiles, rows)
    return chain.call(
        "attend",
        functools.partial(attend_body, docs, halves, len(tiles)),
        (places, query, kv, *tiles),
        [SMEM] + [VMEM] * (2 + len(tiles)),
        [VMEM] * 2,
        [
            jax.ShapeDtypeStruct((tokens, width), BF16),
            jax.ShapeDtypeStruct((2 * kv_heads, 1, span), F32),
        ],
        8 * tokens * rows * tile_num * width,
        scratch=[
            pltpu.VMEM((kv_heads, tile_num, rows, HD), BF16),
            pltpu.VMEM((kv_heads, tile_num, rows, 2 * HD), BF16),
            pltpu.VMEM((2 * kv_heads, span, HD), BF16),
            pltpu.VMEM((tile_num, rows, span), F32),
            pltpu.VMEM((8, span), F32),
            pltpu.VMEM((2 * HD, span), F32),
            pltpu.VMEM((2 * kv_heads, span, 2 * HD), BF16),
        ],
    )


def attend_back_body(docs, halves, count, parts, *refs):
    places_ref, q_ref, merged_ref, total_ref, cos_ref, sin_ref, w_ref = refs[:7]
    kv_ref, tile_refs = refs[7 + parts], refs[8 + parts : 8 + parts + count]
    grad_q_ref, grad_own_ref, *grad_tile_refs = refs[8 + parts + count : 10 + parts + 2 * count]
    grad_ref, keys_ref, values_ref, stack_ref, grads_ref, outs_ref, q_sum_ref, kv_sum_ref = refs[
        10 + parts + 2 * count :
    ]
    rows = q_ref.shape[0] // 2
    kv_heads, tiles = keys_ref.shape[:2]
    group = q_ref.shape[1] // HD // kv_heads
    grad_ref[...] = dot(rows_of(refs[7 : 7 + parts]), w_ref[...], NT).astype(BF16)
    split_tiles([kv_ref, *tile_refs], rows, keys_ref, values_ref, False)
    split_heads(q_ref, rows, group, stack_ref)
    split_heads(merged_ref, rows, group, outs_ref)
    shown = []
    for half in range(2):
        piece = half_piece(places_ref, half, halves)
        position = positions_of(places_ref, piece, halves, rows, (rows, 1), 0)
        shown.append(doc_start(places_ref, docs, position)[1])

    def masked(values, half):
        return jnp.where(shown[half], values.astype(F32), 0.0).astype(BF16)

    split_heads(grad_ref, rows, group, grads_ref, masked)
    kv_sum_ref[...] = jnp.zeros(kv_sum_ref.shape, F32)
    q_sum_ref[...] = jnp.zeros(q_sum_ref.shape, F32)

    def one(hg, carry):
        half, g = hg // kv_heads, hg % kv_heads
        q_piece, q_pos, q_start, _, first = half_of(places_ref, docs, halves, half, rows, group)
        product = grads_ref[hg].astype(F32) * outs_ref[hg].astype(F32)
        high = product.astype(BF16)
        low = (product - high.astype(F32)).astype(BF16)
        ones = jnp.ones((8, HD), BF16)
        delta = (dot(ones, high, NT) + dot(ones, low, NT))[:1]
        totals = total_ref[hg]

        def back(t, carry):
            piece = tile_piece(places_ref, docs, halves, t)

            @pl.when((piece <= q_piece) & ((piece + 1) * rows > first))
            def _():
                k_pos = positions_of(places_ref, piece, halves, rows, (rows, 1), 0)
                keys, queries, grads = keys_ref[g, t], stack_ref[hg], grads_ref[hg]
                scores = dot(keys, queries, NT) - totals
                scores = jnp.where((k_pos <= q_pos) & (k_pos >= q_start), scores, NEGATIVE)
                probs = jnp.exp(scores)
                grad_probs = dot(values_ref[g, t], grads, NT)
                grad_scores = (probs * (grad_probs - delta)).astype(BF16)
                q_sum_ref[hg, :HD] += dot(keys, grad_scores, TN)
                kv_sum_ref[t, 0, g] += dot(grad_scores, queries)
                kv_sum_ref[t, 1, g] += dot(probs.astype(BF16), grads)

            return carry

        lax.fori_loop(0, tiles, back, 0)
        return carry

    lax.fori_loop(0, 2 * kv_heads, one, 0)
    for half in range(2):
        at = pl.ds(half * rows, rows)
        for g in range(kv_heads):
            q_sum = q_sum_ref[half * kv_heads + g].T
            for i in range(group):
                head = (g * group + i) * HD
                part = q_sum[i * rows : (i + 1) * rows, :HD] * (1.0 / math.sqrt(HD))
                part = part * cos_ref[at] - swap_halves(part) * sin_ref[at]
                grad_q_ref[at, head : head + HD] = part.astype(BF16)
    targets = [
        (out, row) for out in (grad_own_ref, *grad_tile_refs) for row in range(0, out.shape[0], rows)
    ]
    for t, (out_ref, row) in enumerate(targets):
        for part in range(2):
            for g in range(kv_heads):
                cols = slice((part * kv_heads + g) * HD, (part * kv_heads + g + 1) * HD)
                out_ref[row : row + rows, cols] = kv_sum_ref[t, part, g].astype(out_ref.dtype)


def attend_back(chain, places, docs, halves, query, merged, totals, cos, sin, w_out, grads, kv, tiles):
    tokens, width = query.shape
    rows = tokens // 2
    kv_heads = kv.shape[1] // 2 // HD
    span = width // HD // kv_heads * rows
    tile_num = tile_count(tiles, rows)
    stack = pltpu.VMEM((2 * kv_heads, span, HD), BF16)
    return chain.call(
        "attend_back",
        functools.partial(attend_back_body, docs, halves, len(tiles), len(grads)),
        (places, query, merged, totals, cos, sin, w_out, *grads, kv, *tiles),
        [SMEM] + [VMEM] * (7 + len(grads) + len(tiles)),
        [VMEM] * (2 + len(tiles)),
        [jax.ShapeDtypeStruct((tokens, width), BF16), jax.ShapeDtypeStruct(kv.shape, F32)]
        + [jax.ShapeDtypeStruct(t.shape, BF16) for t in tiles],
        16 * tokens * rows * tile_num * width,
        scratch=[
            pltpu.VMEM((tokens, width), BF16),
            pltpu.VMEM((kv_heads, tile_num, rows, HD), BF16),
            pltpu.VMEM((kv_heads, tile_num, rows, HD), BF16),
            stack,
            stack,
            stack,
            pltpu.VMEM((2 * kv_heads, 2 * HD, span), F32),
            pltpu.VMEM((tile_num, 2, kv_heads, rows, HD), F32),
        ],
    )


def finish_body(starts_ref, cos_ref, sin_ref, query_ref, own_ref, *refs):
    parts, (all_ref, key_ref, value_ref, total_ref) = refs[:-4], refs[-4:]
    total_ref[...] = own_ref[...]
    rows = own_ref.shape[0] // 2
    tiles = [(part, row) for part in parts for row in range(0, part.shape[0], rows)]
    for t, (part, row) in enumerate(tiles):
        at = pl.ds(pl.multiple_of(starts_ref[t] * rows, rows), rows)
        total_ref[at] += part[row : row + rows].astype(F32)
    width = key_ref.shape[1]
    keys = turn(total_ref[:, :width], cos_ref, sin_ref, -1.0).astype(BF16)
    values = total_ref[:, width:].astype(BF16)
    key_ref[...] = keys
    value_ref[...] = values
    wide = query_ref.shape[1]
    all_ref[:, :wide] = query_ref[...]
    all_ref[:, wide : wide + width] = keys
    all_ref[:, wide + width :] = values


def finish(chain, starts, cos, sin, grad_query, own, parts):
    tokens, width = own.shape
    wide = grad_query.shape[1] + width
    one = jax.ShapeDtypeStruct((tokens, width // 2), BF16)
    return chain.call(
        "finish",
        finish_body,
        (starts, cos, sin, grad_query, own, *parts),
        [SMEM] + [VMEM] * (4 + len(parts)),
        [VMEM] * 3,
        [jax.ShapeDtypeStruct((tokens, wide), BF16), one, one],
        20 * tokens * width,
        scratch=[pltpu.VMEM((tokens, width), F32)],
    )


def flip(values_in, axis, mask):
    count = lax.axis_size(axis)
    return lax.ppermute(values_in, axis, [(i, i ^ mask) for i in range(count)])


def later(values_in, zero):
    return (values_in.astype(F32) + zero).astype(BF16)


def tp_gather(shard, zero=None):
    count = lax.axis_size("tp")
    parts = {0: shard}
    mask = 2
    while mask < count:
        parts.update({j ^ mask: flip(part, "tp", mask) for j, part in parts.items()})
        mask *= 2
    for j, part in list(parts.items()):
        parts[j ^ 1] = flip(later(part, zero) if j and zero is not None else part, "tp", 1)
    return [parts[j] for j in range(count)]


def tp_scatter(terms):
    count = len(terms)
    received = {j: flip(terms[j + 1], "tp", 1) for j in reversed(range(0, count, 2))}
    blocks = {j: terms[j].astype(F32) + part.astype(F32) for j, part in received.items()}
    mask = count // 2
    while mask > 2:
        for j in range(0, mask, 2):
            blocks[j] = blocks[j] + flip(blocks[j + mask].astype(BF16), "tp", mask).astype(F32)
        mask //= 2
    sent = blocks[2].astype(BF16)
    return sent, lambda: blocks[0] + flip(sent, "tp", 2).astype(F32)


def sum_over(values_in, axis):
    mask = 1
    while mask < lax.axis_size(axis):
        values_in = values_in + flip(values_in, axis, mask)
        mask *= 2
    return values_in


def tile_plan(count):
    ends = 2 * count + 3
    needed = []
    for c in range(count):
        pieces = set()
        for held in (c, 2 * count - 1 - c):
            first = ends // 2 if 2 * held >= ends else 0
            pieces |= set(range(first, held + 1))
        needed.append(pieces - {c, 2 * count - 1 - c})
    plan = []
    for k in range(1, count):
        chosen = {}
        for c in range(count):
            source = (c + k) % count
            pieces = sorted(needed[c] & {source, 2 * count - 1 - source})
            if pieces:
                chosen[source] = (c, pieces)
        if chosen:
            plan.append(([(s, c) for s, (c, _) in chosen.items()], {s: p for s, (_, p) in chosen.items()}))
    return plan


def other_columns(values_in, pick_odd, size):
    blocks = values_in.shape[1] // size
    even, odd = (
        jnp.concatenate([values_in[:, b * size : (b + 1) * size] for b in range(at, blocks, 2)], axis=1)
        for at in (0, 1)
    )
    return jnp.where(pick_odd, odd, even)


def per_device(
    tokens,
    attn_gain,
    w_query,
    w_key,
    w_value,
    w_out,
    ffn_gain,
    w_gate,
    w_up,
    w_down,
    out_cotangent,
    doc_lengths,
):
    ctx_count, ctx_rank = lax.axis_size("ctx"), lax.axis_index("ctx")
    dp_count, dp_rank = lax.axis_size("dp"), lax.axis_index("dp")
    tp_count, tp_rank = lax.axis_size("tp"), lax.axis_index("tp")
    tp_rows, width = tokens.shape[1:]
    ctx_rows = tp_rows * tp_count
    near_rows = ctx_rows // 2
    halves = tp_count // 2
    docs = doc_lengths.shape[1]
    size = width // (dp_count * ctx_count)
    chain = Chain()

    plan = tile_plan(ctx_count)
    nowhere = 2 * ctx_count
    widths = [max(len(p) for p in pieces.values()) for _, pieces in plan]
    got = np.full((ctx_count, sum(widths)), nowhere, np.int32)
    gave = np.zeros((ctx_count, sum(widths)), np.int32)
    for t, (moves, pieces) in enumerate(plan):
        first = sum(widths[:t])
        for source, target in moves:
            listed = pieces[source]
            got[target, first : first + len(listed)] = listed
            high = int(listed[0] != source)
            gave[source, first : first + widths[t]] = [high, 1 - high][: widths[t]]
    top = tp_rank // halves
    starts = jnp.asarray(gave)[ctx_rank] ^ top
    here = jnp.stack([ctx_rank, jnp.int32(ctx_count), tp_rank, jnp.int32(tp_rows)])
    places = jnp.concatenate([here, doc_lengths[0], jnp.asarray(got)[ctx_rank]]).astype(jnp.int32)

    within = jnp.arange(ctx_rows, dtype=jnp.int32) ^ (tp_rank * tp_rows)
    piece = jnp.where(within < near_rows, ctx_rank, 2 * ctx_count - 1 - ctx_rank)
    position = (piece * near_rows + within % near_rows).astype(F32)
    inv_freq = jnp.asarray(rope_table(HD), F32)
    angles = position[:, None] * inv_freq[None, :]
    cosine, sine = jnp.cos(angles), jnp.sin(angles)
    cos = jnp.concatenate([cosine, cosine], axis=1)
    sin = jnp.concatenate([-sine, sine], axis=1)

    perm = jnp.arange(tp_count, dtype=jnp.int32) ^ tp_rank
    mine = ctx_rank % 2
    pairs = ctx_count // 2
    steps = jnp.arange(pairs, dtype=jnp.int32)

    def cols_of(dp_index):
        return (dp_index * ctx_count + 2 * steps + mine).astype(jnp.int32)

    def packed_cols_of(dp_index):
        return (dp_index * pairs + steps).astype(jnp.int32)

    bit = ctx_rank // pairs % 2
    order = ((1 - bit) * (pairs // 2) + steps) % pairs

    class WeightGrad:
        def __init__(self, wide, wide_pair, packed, narrow, narrow_pair, part=(0, 1)):
            def terms(dp_index, *received, zero=False):
                cols = cols_of(dp_index)
                cols_pair = packed_cols_of(dp_index) if packed else cols
                if received:
                    cols, cols_pair = cols[order], cols_pair[order]
                return weight_terms(
                    chain, perm, wide, wide_pair, cols, cols_pair, narrow, narrow_pair, size, part, *received, zero=zero
                )

            self.terms = terms

        def send(self, zero=False):
            self.sent = self.terms(1 - dp_rank, zero=zero)[0]
            self.received = flip(self.sent, "dp", 1)
            return self

        def keep(self):
            chain.wait(self.received)
            sent, self.kept = self.terms(dp_rank, self.received, order)
            self.received = flip(sent, "ctx", pairs)
            self.spread(pairs // 2)

        def spread(self, mask):
            while mask > 1:
                half = jnp.reshape(ctx_rank // mask % 2, (1,))
                sent, self.kept = halve(chain, self.kept, self.received, half, 0)
                self.received = flip(sent, "ctx", mask)
                mask //= 2

        def total(self, zero):
            return (self.kept.astype(F32) + zero) + self.received.astype(F32)

    class OutGrad(WeightGrad):
        def __init__(self, wide, narrow):
            self.wide, self.narrow = wide, narrow

        def pair(self):
            both = jnp.concatenate([steps, steps + pairs])
            cols = (2 * both + 1 - mine).astype(jnp.int32)
            self.received = flip(own_terms(chain, perm, self.wide, cols, self.narrow, size)[0], "ctx", 1)

        def send(self):
            half = ((1 - dp_rank) * pairs + steps).astype(jnp.int32)
            order = jnp.concatenate([half, (dp_rank * pairs + steps).astype(jnp.int32)])
            chain.wait(self.received)
            sent, self.kept = own_terms(
                chain, perm, self.wide, 2 * order + mine, self.narrow, size, self.received, order
            )
            self.received = flip(sent, "dp", 1)

        def keep(self):
            chain.wait(self.received)
            self.spread(pairs)

    inputs = tokens[0].astype(F32)
    normed_local = rms_norm(inputs, attn_gain).astype(BF16)
    normed = tp_gather(normed_local)
    grad_fb_local = out_cotangent[0]
    from_pair = flip(
        jnp.concatenate([grad_fb_local, other_columns(normed_local, mine == 0, size)], axis=1), "ctx", 1
    )
    gathered = lax.all_gather(
        jnp.concatenate([grad_fb_local, from_pair], axis=1), "tp", axis=0, tiled=True
    )
    grad_fb, grad_fb_pair, normed_pair = (
        [(gathered, j, first) for j in range(tp_count)] for first in (0, width, 2 * width)
    )
    kv, query = project(chain, normed, w_query, w_key, w_value, cos, sin)
    low_half = lax.dynamic_slice_in_dim(kv, top * near_rows, near_rows, 0)
    high_half = lax.dynamic_slice_in_dim(kv, (1 - top) * near_rows, near_rows, 0)
    tiles = []
    for t, (moves, _) in enumerate(plan):
        low_first = jnp.asarray(gave)[ctx_rank, sum(widths[:t])] == 0
        held = [jnp.where(low_first, low_half, high_half), jnp.where(low_first, high_half, low_half)]
        held = jnp.concatenate(held[: widths[t]], axis=0)
        tiles.append(lax.ppermute(held, "ctx", moves))
    chain.wait(*tiles)
    merged, totals = attend(chain, places, docs, halves, query, kv, tiles)
    out_terms = pull(chain, [merged], [w_out], tp_count, NN)
    hidden_state = inputs + tp_scatter(out_terms)[1]()

    normed_ffn_local = rms_norm(hidden_state, ffn_gain).astype(BF16)
    normed_ffn = tp_gather(normed_ffn_local)
    act, slope, silu = ffn_front(chain, normed_ffn, w_gate, w_up)
    normed_ffn_pair = tp_gather(flip(normed_ffn_local, "ctx", 1), chain.zero)
    act_pair, slope_pair, silu_pair = ffn_front(chain, normed_ffn_pair, w_gate, w_up)

    down_w = WeightGrad(grad_fb, grad_fb_pair, False, act, act_pair).send()
    grad_gate, grad_up = ffn_back(chain, perm, grad_fb, w_down, slope, silu)
    nffn_terms = pull(chain, [grad_gate, grad_up], [w_gate, w_up], tp_count)
    nffn_sent, nffn_sum = tp_scatter(nffn_terms)
    grad_gate_pair, grad_up_pair = ffn_back(chain, perm, grad_fb_pair, w_down, slope_pair, silu_pair)
    chain.wait(nffn_sent)
    gate_w = WeightGrad(normed_ffn, normed_ffn_pair, False, grad_gate, grad_gate_pair).send()
    up_w = WeightGrad(normed_ffn, normed_ffn_pair, False, grad_up, grad_up_pair)
    down_w.keep()
    grad_nffn = nffn_sum() + chain.zero
    grad_state_norm, grad_ffn_gain = jax.vjp(rms_norm, hidden_state, ffn_gain)[1](grad_nffn)
    grad_state = grad_fb_local.astype(F32) + grad_state_norm
    grad_sb_local = grad_state.astype(BF16)
    grad_sb = tp_gather(grad_sb_local)
    chain.wait(grad_sb_local)
    up_w.send()

    grad_query, own, *sent = attend_back(
        chain, places, docs, halves, query, merged, totals, cos, sin, w_out, grad_sb, kv, tiles
    )
    returned = [
        lax.ppermute(part, "ctx", [(target, source) for source, target in moves])
        for part, (moves, _) in zip(sent, plan)
    ]
    chain.wait(down_w.received)
    gate_w.keep()
    chain.wait(*returned)
    grad_qkv, grad_key, grad_value = finish(chain, starts, cos, sin, grad_query, own, returned)
    grad_qkv_pair = flip(grad_qkv, "ctx", 1)
    up_w.keep()
    out_w = OutGrad(grad_sb, merged)
    out_w.pair()
    back_terms = pull(chain, [grad_query, grad_key, grad_value], [w_query, w_key, w_value], tp_count)
    layer_terms = push(chain, perm, act, w_down)
    layer_sum = lax.psum_scatter(layer_terms, "tp", scatter_dimension=0, tiled=True)
    layer_out = (hidden_state + layer_sum.astype(F32)).astype(BF16)
    normed_sent, normed_sum = tp_scatter(back_terms)
    chain.wait(grad_qkv_pair)
    qkv_w = WeightGrad(normed, normed_pair, True, grad_qkv, grad_qkv_pair).send(True)
    grad_normed = normed_sum() + chain.zero
    grad_input_norm, grad_attn_gain = jax.vjp(rms_norm, inputs, attn_gain)[1](grad_normed)
    input_grad = grad_state + grad_input_norm
    sent_zero = chain.zero
    chain.wait(gate_w.received)
    qkv_w.keep()
    out_w.send()
    out_zero = chain.zero
    chain.wait(up_w.received)
    out_w.keep()
    zero = chain.zero
    gains = sum_over(jnp.stack([grad_attn_gain, grad_ffn_gain]) + out_zero, "tp")
    gains = sum_over(sum_over(gains + zero, "dp"), "ctx")
    q_width, kv_width = w_query.shape[1], w_key.shape[1]
    out_total = out_w.total(zero).T
    qkv_total = qkv_w.total(zero)
    return (
        layer_out[None],
        input_grad[None],
        gains[0],
        qkv_total[:, :q_width],
        qkv_total[:, q_width : q_width + kv_width],
        qkv_total[:, q_width + kv_width :],
        out_total,
        gains[1],
        gate_w.total(out_zero),
        up_w.total(zero),
        down_w.total(sent_zero).T,
    )


def solution(mesh):
    placed = (
        P("dp", ("ctx", "tp"), None),
        P(),
        P(None, "tp"),
        P(None, "tp"),
        P(None, "tp"),
        P("tp", None),
        P(),
        P(None, "tp"),
        P(None, "tp"),
        P("tp", None),
        P("dp", ("ctx", "tp"), None),
        P("dp", None),
    )
    return jax.shard_map(
        per_device,
        mesh=mesh,
        in_specs=placed,
        out_specs=(
            P("dp", ("ctx", "tp"), None),
            P("dp", ("ctx", "tp"), None),
            P(),
            P(("dp", "ctx"), "tp"),
            P(("dp", "ctx"), "tp"),
            P(("dp", "ctx"), "tp"),
            P("tp", ("dp", "ctx")),
            P(),
            P(("dp", "ctx"), "tp"),
            P(("dp", "ctx"), "tp"),
            P("tp", ("dp", "ctx")),
        ),
        check_vma=False,
    )
```

```python
import functools
import math

import jax
import jax.numpy as jnp
import numpy as np
from jax import lax
from jax.experimental import pallas as pl
from jax.experimental.pallas import tpu as pltpu
from jax.sharding import PartitionSpec as P

HD = 64
EPSILON = 1e-05
NEGATIVE = -1e30
ROPE_THETA = 500000.0


def rope_table(head_size):
    base_freq = np.array(
        [ROPE_THETA ** (-2.0 * index / head_size) for index in range(head_size // 2)]
    )
    wavelength = 2.0 * math.pi / base_freq
    blend = (8192.0 / wavelength - 1.0) / 3.0
    middle = (1.0 - blend) * base_freq / 32.0 + blend * base_freq
    return np.where(
        wavelength > 8192.0, base_freq / 32.0, np.where(wavelength < 2048.0, base_freq, middle)
    )


def rms_norm(values_in, gain_vec):
    return (
        values_in
        * lax.rsqrt(jnp.mean(values_in * values_in, axis=-1, keepdims=True) + EPSILON)
        * gain_vec
    )


F32, BF16 = jnp.float32, jnp.bfloat16
VMEM_BYTES = 62 * 1024 * 1024
NN = (((1,), (0,)), ((), ()))
NT = (((1,), (1,)), ((), ()))
TN = (((0,), (0,)), ((), ()))
VMEM = pl.BlockSpec(memory_space=pltpu.VMEM)
SMEM = pl.BlockSpec(memory_space=pltpu.SMEM)
ANYWHERE = pl.BlockSpec(memory_space=pl.ANY)


def dot(left, right, dims=NN):
    return lax.dot_general(left, right, dims, preferred_element_type=F32)


def part_specs(parts, rows, width, col):
    def spec(part):
        if not isinstance(part, tuple):
            return pl.BlockSpec((rows, width), lambda *at: (0, col(*at)))
        j, first = part[1:]
        return pl.BlockSpec(
            (rows, width), lambda *at: (0 if j is None else at[-1][j], first // width + col(*at))
        )

    return [spec(part) for part in parts]


def part_arrays(parts):
    return [part[0] if isinstance(part, tuple) else part for part in parts]


def rows_of(refs):
    return jnp.concatenate([ref[...] for ref in refs], axis=0)


class Chain:
    def __init__(self):
        self.held = []
        self.cost = 58 * 10**8
        self.room = VMEM_BYTES // 2

    def wait(self, *arrays):
        self.held = [*arrays, *self.held]

    def call(
        self, name, body, args, in_specs, out_specs, out_shape, flops, grid=(), scalars=0, scratch=(), zero=False
    ):
        held, count, outs = self.held, len(args), len(out_shape)
        marks, mark_specs = [jax.ShapeDtypeStruct((8, 128), F32)], [ANYWHERE]
        if zero:
            marks.append(jax.ShapeDtypeStruct((1, 1), F32))
            mark_specs.append(SMEM)

        def inner(*refs):
            rest = refs[count + len(held) :]
            given = refs[:scalars] + refs[scalars + len(held) : count + len(held)]
            body(*given, *rest[:outs], *rest[outs + len(marks) :])
            if zero:
                rest[outs + 1][0, 0] = 0.0

        results = pl.pallas_call(
            inner,
            grid_spec=pltpu.PrefetchScalarGridSpec(
                num_scalar_prefetch=scalars,
                grid=grid,
                in_specs=[ANYWHERE] * len(held) + list(in_specs),
                out_specs=[*out_specs, *mark_specs],
                scratch_shapes=list(scratch),
            ),
            out_shape=[*out_shape, *marks],
            compiler_params=pltpu.CompilerParams(
                vmem_limit_bytes=self.room, dimension_semantics=("arbitrary",) * len(grid)
            ),
            cost_estimate=pl.CostEstimate(flops=self.cost, bytes_accessed=1, transcendentals=0),
            name=name,
        )(*args[:scalars], *held, *args[scalars:])
        self.held = [results[outs]]
        if zero:
            self.zero = results[outs + 1][0, 0]
        return results[:outs]


def fill_rows(parts, rows_ref):
    @pl.when(pl.program_id(0) == 0)
    def _():
        rows_ref[...] = rows_of(parts)


def ffn_front_body(count, *refs):
    gate_ref, up_ref, act_ref, slope_ref, silu_ref, rows_ref = refs[count:]
    fill_rows(refs[:count], rows_ref)
    rows = rows_ref[...]
    gate = dot(rows, gate_ref[...])
    up = dot(rows, up_ref[...])
    sigma = 1.0 / (1.0 + jnp.exp(-gate))
    silu = gate * sigma
    act_ref[...] = (silu * up).astype(BF16)
    slope_ref[...] = (up * sigma * (1.0 + gate * (1.0 - sigma))).astype(BF16)
    silu_ref[...] = silu.astype(BF16)


def whole(array):
    return pl.BlockSpec(array.shape, lambda *_: (0,) * array.ndim)


def ffn_front(chain, parts, w_gate, w_up, part=(0, 1), block=512):
    count, width = sum(p.shape[0] for p in parts), parts[0].shape[1]
    units = w_gate.shape[1] // part[1]
    block = min(block, units)
    first = part[0] * (units // block)
    weight = pl.BlockSpec((width, block), lambda j: (0, first + j))
    return chain.call(
        "ffn_front",
        functools.partial(ffn_front_body, len(parts)),
        (*parts, w_gate, w_up),
        [whole(p) for p in parts] + [weight, weight],
        [pl.BlockSpec((count, block), lambda j: (0, j))] * 3,
        [jax.ShapeDtypeStruct((count, units), BF16)] * 3,
        4 * count * width * units,
        grid=(units // block,),
        scratch=[pltpu.VMEM((count, width), BF16)],
        zero=True,
    )


def ffn_back_body(count, perm_ref, *refs):
    down_ref, slope_ref, silu_ref, gate_ref, up_ref, rows_ref = refs[count:]
    fill_rows(refs[:count], rows_ref)
    grad_act = dot(rows_ref[...], down_ref[...], NT)
    gate_ref[...] = (grad_act * slope_ref[...].astype(F32)).astype(BF16)
    up_ref[...] = (grad_act * silu_ref[...].astype(F32)).astype(BF16)


def ffn_back(chain, perm, parts, w_down, slope, silu, block=512):
    count, units = slope.shape
    width = w_down.shape[1]
    block = min(block, units)
    tile = pl.BlockSpec((count, block), lambda j, _: (0, j))
    return chain.call(
        "ffn_back",
        functools.partial(ffn_back_body, len(parts)),
        (perm, *part_arrays(parts), w_down, slope, silu),
        part_specs(parts, count // len(parts), width, lambda *_: 0)
        + [pl.BlockSpec((block, width), lambda j, _: (j, 0)), tile, tile],
        [tile, tile],
        [jax.ShapeDtypeStruct((count, units), BF16)] * 2,
        2 * count * width * units,
        grid=(units // block,),
        scalars=1,
        scratch=[pltpu.VMEM((count, width), BF16)],
    )


def pull_body(count, dims, *refs):
    total = dot(refs[0][...], refs[count][...], dims)
    for i in range(1, count):
        total = total + dot(refs[i][...], refs[count + i][...], dims)
    outs = refs[2 * count :]
    rows = total.shape[0] // len(outs)
    for j, out in enumerate(outs):
        out[...] = total[j * rows : (j + 1) * rows].astype(BF16)


def pull(chain, grads, weights, blocks, dims=NT, block=1024):
    rows, at = grads[0].shape[0], 0 if dims == NT else 1
    width = weights[0].shape[at]
    depth = sum(w.shape[1 - at] for w in weights)
    return chain.call(
        "pull",
        functools.partial(pull_body, len(grads), dims),
        (*grads, *weights),
        [whole(g) for g in grads]
        + [
            pl.BlockSpec((block, w.shape[1]), lambda j: (j, 0))
            if dims == NT
            else pl.BlockSpec((w.shape[0], block), lambda j: (0, j))
            for w in weights
        ],
        [pl.BlockSpec((rows // blocks, block), lambda j: (0, j))] * blocks,
        [jax.ShapeDtypeStruct((rows // blocks, width), BF16)] * blocks,
        2 * rows * width * depth,
        grid=(width // block,),
        zero=True,
    )


def push_body(blocks, perm_ref, rows_ref, weight_ref, out_ref):
    total = dot(rows_ref[...], weight_ref[...]).astype(BF16)
    rows = total.shape[0] // blocks
    for j in range(blocks):
        at = pl.ds(pl.multiple_of(perm_ref[j] * rows, rows), rows)
        out_ref[at] = total[j * rows : (j + 1) * rows]


def push(chain, perm, rows, weight, block=1024):
    count, depth = rows.shape
    width = weight.shape[1]
    return chain.call(
        "push",
        functools.partial(push_body, perm.shape[0]),
        (perm, rows, weight),
        [
            pl.BlockSpec((count, depth), lambda j, _: (0, 0)),
            pl.BlockSpec((depth, block), lambda j, _: (0, j)),
        ],
        [pl.BlockSpec((count, block), lambda j, _: (0, j))],
        [jax.ShapeDtypeStruct((count, width), BF16)],
        2 * count * depth * width,
        grid=(width // block,),
        scalars=1,
    )[0]


def terms_body(count, blocks, scalars, *refs):
    refs = refs[scalars:]
    wide, wide_pair = rows_of(refs[:count]), rows_of(refs[count : 2 * count])
    own, pair = refs[2 * count : 2 * count + 2]
    total = dot(wide, own[...], TN) + dot(wide_pair, pair[...], TN)
    if scalars == 3:
        refs[-1][...] = total.astype(BF16)
        return
    got, sent_ref, left_ref = refs[2 * count + 2 :]
    total = (total + got[...].astype(F32)).astype(BF16)

    @pl.when(pl.program_id(1) < blocks // 2)
    def _():
        sent_ref[...] = total

    @pl.when(pl.program_id(1) >= blocks // 2)
    def _():
        left_ref[...] = total


def weight_terms(chain, perm, wide, wide_pair, cols, cols_pair, narrow, narrow_pair, size, part, received=None, order=None, zero=False):
    tokens, units = narrow.shape
    units //= part[1]
    blocks = cols.shape[0]
    block = units if units <= 2048 else math.gcd(2048, units)
    first = part[0] * (units // block)
    rows = tokens // len(wide)
    units_spec = pl.BlockSpec((tokens, block), lambda j, i, *_: (0, first + j))
    scalars = [cols, cols_pair, perm]
    in_specs = (
        part_specs(wide, rows, size, lambda j, i, *s: s[-3][i])
        + part_specs(wide_pair, rows, size, lambda j, i, *s: s[-2][i])
        + [units_spec, units_spec]
    )
    args = [*part_arrays(wide), *part_arrays(wide_pair), narrow, narrow_pair]
    if received is None:
        out_specs = [pl.BlockSpec((size, block), lambda j, i, *_: (i, j))]
        out = [jax.ShapeDtypeStruct((blocks * size, units), BF16)]
    else:
        half = blocks // 2
        scalars = [order] + scalars
        args.append(received)
        in_specs.append(pl.BlockSpec((size, block), lambda j, i, io, *_: (io[i], j)))
        out_specs = [
            pl.BlockSpec((size, block), lambda j, i, *_: (jnp.minimum(i, half - 1), j)),
            pl.BlockSpec((size, block), lambda j, i, *_: (jnp.maximum(i - half, 0), j)),
        ]
        out = [jax.ShapeDtypeStruct((half * size, units), BF16)] * 2
    return chain.call(
        "weight_terms",
        functools.partial(terms_body, len(wide), blocks, len(scalars)),
        (*scalars, *args),
        in_specs,
        out_specs,
        out,
        4 * tokens * units * blocks * size,
        grid=(units // block, blocks),
        scalars=len(scalars),
        zero=zero or received is not None,
    )


def own_terms_body(count, blocks, scalars, *refs):
    refs = refs[scalars:]
    total = dot(rows_of(refs[:count]), refs[count][...], TN)
    if scalars == 2:
        refs[-1][...] = total.astype(BF16)
        return
    got, sent_ref, left_ref = refs[count + 1 :]
    total = (total + got[...].astype(F32)).astype(BF16)

    @pl.when(pl.program_id(0) < blocks // 2)
    def _():
        sent_ref[...] = total

    @pl.when(pl.program_id(0) >= blocks // 2)
    def _():
        left_ref[...] = total


def own_terms(chain, perm, wide, cols, narrow, size, received=None, order=None):
    tokens, units = narrow.shape
    blocks = cols.shape[0]
    rows = tokens // len(wide)
    half = blocks // 2
    scalars = [cols, perm]
    args = [*part_arrays(wide), narrow]
    in_specs = part_specs(wide, rows, size, lambda i, *s: s[-2][i]) + [whole(narrow)]
    if received is None:
        out_specs = [pl.BlockSpec((size, units), lambda i, *_: (i, 0))]
        out = [jax.ShapeDtypeStruct((blocks * size, units), BF16)]
    else:
        scalars = [order] + scalars
        args.append(received)
        in_specs.append(pl.BlockSpec((size, units), lambda i, io, *_: (io[i], 0)))
        out_specs = [
            pl.BlockSpec((size, units), lambda i, *_: (jnp.minimum(i, half - 1), 0)),
            pl.BlockSpec((size, units), lambda i, *_: (jnp.maximum(i - half, 0), 0)),
        ]
        out = [jax.ShapeDtypeStruct((half * size, units), BF16)] * 2
    return chain.call(
        "own_terms",
        functools.partial(own_terms_body, len(wide), blocks, len(scalars)),
        (*scalars, *args),
        in_specs,
        out_specs,
        out,
        2 * tokens * units * blocks * size,
        grid=(blocks,),
        scalars=len(scalars),
        zero=True,
    )


def halve_body(mine, kept_send, got_send, kept, got, sent_ref, left_ref):
    sent_ref[...] = (kept_send[...].astype(F32) + got_send[...].astype(F32)).astype(BF16)
    left_ref[...] = (kept[...].astype(F32) + got[...].astype(F32)).astype(BF16)


def halve(chain, kept, received, mine, dim):
    steps = math.gcd(4, kept.shape[1 - dim] // 128)
    shape = list(kept.shape)
    shape[dim] //= 2
    block = list(shape)
    block[1 - dim] //= steps

    def spec(flip_half):
        def at(j, m):
            half = 1 - m[0] if flip_half else m[0]
            return (half, j) if dim == 0 else (j, half)

        return pl.BlockSpec(tuple(block), at)

    out_spec = pl.BlockSpec(tuple(block), lambda j, m: (0, j) if dim == 0 else (j, 0))
    out = jax.ShapeDtypeStruct(tuple(shape), BF16)
    return chain.call(
        "halve",
        halve_body,
        (mine, kept, received, kept, received),
        [spec(True), spec(True), spec(False), spec(False)],
        [out_spec, out_spec],
        [out, out],
        kept.size,
        grid=(steps,),
        scalars=1,
        zero=True,
    )


def swap_halves(values_in):
    half = HD // 2
    width = values_in.shape[1]
    if width % 128:
        parts = []
        for at in range(0, width, HD):
            parts += [values_in[:, at + half : at + HD], values_in[:, at : at + half]]
        return jnp.concatenate(parts, axis=1)
    lane = lax.broadcasted_iota(jnp.int32, values_in.shape, 1)
    return jnp.where(
        lane % HD < half,
        pltpu.roll(values_in, width - half, 1),
        pltpu.roll(values_in, half, 1),
    )


def turn(values_in, cos_ref, sin_ref, sign):
    count = values_in.shape[1] // HD
    cos = jnp.concatenate([cos_ref[...]] * count, axis=1)
    sin = jnp.concatenate([sin_ref[...]] * count, axis=1)
    return values_in * cos + sign * (swap_halves(values_in) * sin)


def project_body(count, *refs):
    q_ref, k_ref, v_ref, cos_ref, sin_ref, kv_ref, query_ref = refs[count:]
    rows = rows_of(refs[:count])
    width = k_ref.shape[1]
    kv_ref[:, :width] = turn(dot(rows, k_ref[...]), cos_ref, sin_ref, 1.0).astype(BF16)
    kv_ref[:, width:] = dot(rows, v_ref[...]).astype(BF16)
    queries = turn(dot(rows, q_ref[...]), cos_ref, sin_ref, 1.0).astype(BF16)
    query_ref[...] = (queries.astype(F32) * (1.0 / math.sqrt(HD))).astype(BF16)


def project(chain, parts, w_query, w_key, w_value, cos, sin):
    count = sum(p.shape[0] for p in parts)
    kv = jax.ShapeDtypeStruct((count, 2 * w_key.shape[1]), BF16)
    query = jax.ShapeDtypeStruct((count, w_query.shape[1]), BF16)
    return chain.call(
        "project",
        functools.partial(project_body, len(parts)),
        (*parts, w_query, w_key, w_value, cos, sin),
        [VMEM] * (len(parts) + 5),
        [VMEM] * 2,
        [kv, query],
        2 * count * parts[0].shape[1] * (query.shape[1] + kv.shape[1]),
    )


def half_piece(places_ref, half, halves):
    top = places_ref[2] // halves
    return jnp.where(top == half, places_ref[0], 2 * places_ref[1] - 1 - places_ref[0])


def doc_start(places_ref, docs, position):
    end = 0
    start = position * 0
    for i in range(docs):
        end = end + places_ref[4 + i]
        start = jnp.where(position >= end, end, start)
    return start, position < end


def positions_of(places_ref, piece, halves, rows, shape, dim):
    row = lax.broadcasted_iota(jnp.int32, shape, dim)
    inner = lax.rem(places_ref[2], halves) * places_ref[3]
    return piece * rows + (row ^ inner)


def tile_count(tiles, rows):
    return sum(t.shape[0] for t in tiles) // rows + 2


def half_of(places_ref, docs, halves, half, rows, group):
    piece = half_piece(places_ref, half, halves)
    position = positions_of(places_ref, piece, halves, rows, (1, rows), 1)
    start, valid = doc_start(places_ref, docs, position)
    first = doc_start(places_ref, docs, piece * rows)[0]
    position, start, valid = (
        jnp.concatenate([v] * group, axis=1) for v in (position, start, valid.astype(jnp.int32))
    )
    return piece, position, start, valid, first


def tile_piece(places_ref, docs, halves, t):
    given = places_ref[4 + docs + jnp.maximum(t - 2, 0)]
    own = jnp.where(t == 0, half_piece(places_ref, 0, halves), half_piece(places_ref, 1, halves))
    return jnp.where(t < 2, own, given)


def split_tiles(kv_refs, rows, keys_ref, values_ref, ones):
    kv_heads = keys_ref.shape[0]
    t = 0
    for ref in kv_refs:
        for row in range(0, ref.shape[0], rows):
            for g in range(kv_heads):
                keys_ref[g, t] = ref[row : row + rows, g * HD : (g + 1) * HD]
                values = ref[row : row + rows, (kv_heads + g) * HD : (kv_heads + g + 1) * HD]
                if ones:
                    values = jnp.concatenate([values, jnp.ones_like(values)], axis=1)
                values_ref[g, t] = values
            t += 1


def split_heads(ref, rows, group, out_ref, change=lambda v, half: v):
    kv_heads = out_ref.shape[0] // 2
    for half in range(2):
        for g in range(kv_heads):
            for i in range(group):
                head = (g * group + i) * HD
                values = ref[half * rows : (half + 1) * rows, head : head + HD]
                out_ref[half * kv_heads + g, i * rows : (i + 1) * rows] = change(values, half)


def attend_body(docs, halves, count, places_ref, q_ref, kv_ref, *refs):
    tile_refs, (merged_ref, total_ref) = refs[:count], refs[count : count + 2]
    keys_ref, values_ref, stack_ref, scores_ref, peak_ref, sums_ref, out_ref = refs[count + 2 :]
    rows = q_ref.shape[0] // 2
    kv_heads, tiles = keys_ref.shape[:2]
    group = q_ref.shape[1] // HD // kv_heads
    split_tiles([kv_ref, *tile_refs], rows, keys_ref, values_ref, True)
    split_heads(q_ref, rows, group, stack_ref)

    def one(hg, carry):
        half, g = hg // kv_heads, hg % kv_heads
        q_piece, q_pos, q_start, valid, first = half_of(places_ref, docs, halves, half, rows, group)
        peak_ref[...] = jnp.full(peak_ref.shape, NEGATIVE, F32)
        sums_ref[...] = jnp.zeros(sums_ref.shape, F32)

        def score(t, carry):
            piece = tile_piece(places_ref, docs, halves, t)

            @pl.when((piece <= q_piece) & ((piece + 1) * rows > first))
            def _():
                k_pos = positions_of(places_ref, piece, halves, rows, (rows, 1), 0)
                scores = dot(keys_ref[g, t], stack_ref[hg], NT)
                scores = jnp.where((k_pos <= q_pos) & (k_pos >= q_start), scores, NEGATIVE)
                scores_ref[t] = scores
                top = jnp.max(scores.reshape(rows // 8, 8, group * rows), axis=0)
                peak_ref[...] = jnp.maximum(peak_ref[...], top)

            return carry

        lax.fori_loop(0, tiles, score, 0)
        peak = jnp.max(peak_ref[...], axis=0, keepdims=True)

        def weigh(t, carry):
            piece = tile_piece(places_ref, docs, halves, t)

            @pl.when((piece <= q_piece) & ((piece + 1) * rows > first))
            def _():
                expo = jnp.exp(scores_ref[t] - peak).astype(BF16)
                sums_ref[...] += dot(values_ref[g, t], expo, TN)

            return carry

        lax.fori_loop(0, tiles, weigh, 0)
        total = sums_ref[HD : HD + 1]
        out_ref[hg] = jnp.where(valid > 0, sums_ref[...] / total, 0.0).T.astype(BF16)
        total_ref[hg] = peak + jnp.log(total)
        return carry

    lax.fori_loop(0, 2 * kv_heads, one, 0)
    for half in range(2):
        for g in range(kv_heads):
            for i in range(group):
                head = (g * group + i) * HD
                merged_ref[half * rows : (half + 1) * rows, head : head + HD] = out_ref[
                    half * kv_heads + g, i * rows : (i + 1) * rows, :HD
                ]


def attend(chain, places, docs, halves, query, kv, tiles):
    tokens, width = query.shape
    rows = tokens // 2
    heads, kv_heads = width // HD, kv.shape[1] // 2 // HD
    span = heads // kv_heads * rows
    tile_num = tile_count(tiles, rows)
    return chain.call(
        "attend",
        functools.partial(attend_body, docs, halves, len(tiles)),
        (places, query, kv, *tiles),
        [SMEM] + [VMEM] * (2 + len(tiles)),
        [VMEM] * 2,
        [
            jax.ShapeDtypeStruct((tokens, width), BF16),
            jax.ShapeDtypeStruct((2 * kv_heads, 1, span), F32),
        ],
        8 * tokens * rows * tile_num * width,
        scratch=[
            pltpu.VMEM((kv_heads, tile_num, rows, HD), BF16),
            pltpu.VMEM((kv_heads, tile_num, rows, 2 * HD), BF16),
            pltpu.VMEM((2 * kv_heads, span, HD), BF16),
            pltpu.VMEM((tile_num, rows, span), F32),
            pltpu.VMEM((8, span), F32),
            pltpu.VMEM((2 * HD, span), F32),
            pltpu.VMEM((2 * kv_heads, span, 2 * HD), BF16),
        ],
    )


def attend_back_body(docs, halves, count, parts, *refs):
    places_ref, q_ref, merged_ref, total_ref, cos_ref, sin_ref, w_ref = refs[:7]
    kv_ref, tile_refs = refs[7 + parts], refs[8 + parts : 8 + parts + count]
    grad_q_ref, grad_own_ref, *grad_tile_refs = refs[8 + parts + count : 10 + parts + 2 * count]
    grad_ref, keys_ref, values_ref, stack_ref, grads_ref, outs_ref, q_sum_ref, kv_sum_ref = refs[
        10 + parts + 2 * count :
    ]
    rows = q_ref.shape[0] // 2
    kv_heads, tiles = keys_ref.shape[:2]
    group = q_ref.shape[1] // HD // kv_heads
    grad_ref[...] = dot(rows_of(refs[7 : 7 + parts]), w_ref[...], NT).astype(BF16)
    split_tiles([kv_ref, *tile_refs], rows, keys_ref, values_ref, False)
    split_heads(q_ref, rows, group, stack_ref)
    split_heads(merged_ref, rows, group, outs_ref)
    shown = []
    for half in range(2):
        piece = half_piece(places_ref, half, halves)
        position = positions_of(places_ref, piece, halves, rows, (rows, 1), 0)
        shown.append(doc_start(places_ref, docs, position)[1])

    def masked(values, half):
        return jnp.where(shown[half], values.astype(F32), 0.0).astype(BF16)

    split_heads(grad_ref, rows, group, grads_ref, masked)
    kv_sum_ref[...] = jnp.zeros(kv_sum_ref.shape, F32)
    q_sum_ref[...] = jnp.zeros(q_sum_ref.shape, F32)

    def one(hg, carry):
        half, g = hg // kv_heads, hg % kv_heads
        q_piece, q_pos, q_start, _, first = half_of(places_ref, docs, halves, half, rows, group)
        product = grads_ref[hg].astype(F32) * outs_ref[hg].astype(F32)
        high = product.astype(BF16)
        low = (product - high.astype(F32)).astype(BF16)
        ones = jnp.ones((8, HD), BF16)
        delta = (dot(ones, high, NT) + dot(ones, low, NT))[:1]
        totals = total_ref[hg]

        def back(t, carry):
            piece = tile_piece(places_ref, docs, halves, t)

            @pl.when((piece <= q_piece) & ((piece + 1) * rows > first))
            def _():
                k_pos = positions_of(places_ref, piece, halves, rows, (rows, 1), 0)
                keys, queries, grads = keys_ref[g, t], stack_ref[hg], grads_ref[hg]
                scores = dot(keys, queries, NT) - totals
                scores = jnp.where((k_pos <= q_pos) & (k_pos >= q_start), scores, NEGATIVE)
                probs = jnp.exp(scores)
                grad_probs = dot(values_ref[g, t], grads, NT)
                grad_scores = (probs * (grad_probs - delta)).astype(BF16)
                q_sum_ref[hg, :HD] += dot(keys, grad_scores, TN)
                kv_sum_ref[t, 0, g] += dot(grad_scores, queries)
                kv_sum_ref[t, 1, g] += dot(probs.astype(BF16), grads)

            return carry

        lax.fori_loop(0, tiles, back, 0)
        return carry

    lax.fori_loop(0, 2 * kv_heads, one, 0)
    for half in range(2):
        at = pl.ds(half * rows, rows)
        for g in range(kv_heads):
            q_sum = q_sum_ref[half * kv_heads + g].T
            for i in range(group):
                head = (g * group + i) * HD
                part = q_sum[i * rows : (i + 1) * rows, :HD] * (1.0 / math.sqrt(HD))
                part = part * cos_ref[at] - swap_halves(part) * sin_ref[at]
                grad_q_ref[at, head : head + HD] = part.astype(BF16)
    targets = [
        (out, row) for out in (grad_own_ref, *grad_tile_refs) for row in range(0, out.shape[0], rows)
    ]
    for t, (out_ref, row) in enumerate(targets):
        for part in range(2):
            for g in range(kv_heads):
                cols = slice((part * kv_heads + g) * HD, (part * kv_heads + g + 1) * HD)
                out_ref[row : row + rows, cols] = kv_sum_ref[t, part, g].astype(out_ref.dtype)


def attend_back(chain, places, docs, halves, query, merged, totals, cos, sin, w_out, grads, kv, tiles):
    tokens, width = query.shape
    rows = tokens // 2
    kv_heads = kv.shape[1] // 2 // HD
    span = width // HD // kv_heads * rows
    tile_num = tile_count(tiles, rows)
    stack = pltpu.VMEM((2 * kv_heads, span, HD), BF16)
    return chain.call(
        "attend_back",
        functools.partial(attend_back_body, docs, halves, len(tiles), len(grads)),
        (places, query, merged, totals, cos, sin, w_out, *grads, kv, *tiles),
        [SMEM] + [VMEM] * (7 + len(grads) + len(tiles)),
        [VMEM] * (2 + len(tiles)),
        [jax.ShapeDtypeStruct((tokens, width), BF16), jax.ShapeDtypeStruct(kv.shape, F32)]
        + [jax.ShapeDtypeStruct(t.shape, BF16) for t in tiles],
        16 * tokens * rows * tile_num * width,
        scratch=[
            pltpu.VMEM((tokens, width), BF16),
            pltpu.VMEM((kv_heads, tile_num, rows, HD), BF16),
            pltpu.VMEM((kv_heads, tile_num, rows, HD), BF16),
            stack,
            stack,
            stack,
            pltpu.VMEM((2 * kv_heads, 2 * HD, span), F32),
            pltpu.VMEM((tile_num, 2, kv_heads, rows, HD), F32),
        ],
    )


def finish_body(starts_ref, cos_ref, sin_ref, query_ref, own_ref, *refs):
    parts, (all_ref, key_ref, value_ref, total_ref) = refs[:-4], refs[-4:]
    total_ref[...] = own_ref[...]
    rows = own_ref.shape[0] // 2
    tiles = [(part, row) for part in parts for row in range(0, part.shape[0], rows)]
    for t, (part, row) in enumerate(tiles):
        at = pl.ds(pl.multiple_of(starts_ref[t] * rows, rows), rows)
        total_ref[at] += part[row : row + rows].astype(F32)
    width = key_ref.shape[1]
    keys = turn(total_ref[:, :width], cos_ref, sin_ref, -1.0).astype(BF16)
    values = total_ref[:, width:].astype(BF16)
    key_ref[...] = keys
    value_ref[...] = values
    wide = query_ref.shape[1]
    all_ref[:, :wide] = query_ref[...]
    all_ref[:, wide : wide + width] = keys
    all_ref[:, wide + width :] = values


def finish(chain, starts, cos, sin, grad_query, own, parts):
    tokens, width = own.shape
    wide = grad_query.shape[1] + width
    one = jax.ShapeDtypeStruct((tokens, width // 2), BF16)
    return chain.call(
        "finish",
        finish_body,
        (starts, cos, sin, grad_query, own, *parts),
        [SMEM] + [VMEM] * (4 + len(parts)),
        [VMEM] * 3,
        [jax.ShapeDtypeStruct((tokens, wide), BF16), one, one],
        20 * tokens * width,
        scratch=[pltpu.VMEM((tokens, width), F32)],
    )


def flip(values_in, axis, mask):
    count = lax.axis_size(axis)
    return lax.ppermute(values_in, axis, [(i, i ^ mask) for i in range(count)])


def later(values_in, zero):
    return (values_in.astype(F32) + zero).astype(BF16)


def tp_gather(shard, zero=None):
    count = lax.axis_size("tp")
    parts = {0: shard}
    mask = 2
    while mask < count:
        parts.update({j ^ mask: flip(part, "tp", mask) for j, part in parts.items()})
        mask *= 2
    for j, part in list(parts.items()):
        parts[j ^ 1] = flip(later(part, zero) if j and zero is not None else part, "tp", 1)
    return [parts[j] for j in range(count)]


def tp_scatter(terms):
    count = len(terms)
    received = {j: flip(terms[j + 1], "tp", 1) for j in reversed(range(0, count, 2))}
    blocks = {j: terms[j].astype(F32) + part.astype(F32) for j, part in received.items()}
    mask = count // 2
    while mask > 2:
        for j in range(0, mask, 2):
            blocks[j] = blocks[j] + flip(blocks[j + mask].astype(BF16), "tp", mask).astype(F32)
        mask //= 2
    sent = blocks[2].astype(BF16)
    return sent, lambda: blocks[0] + flip(sent, "tp", 2).astype(F32)


def sum_over(values_in, axis):
    mask = 1
    while mask < lax.axis_size(axis):
        values_in = values_in + flip(values_in, axis, mask)
        mask *= 2
    return values_in


def tile_plan(count):
    ends = 2 * count + 3
    needed = []
    for c in range(count):
        pieces = set()
        for held in (c, 2 * count - 1 - c):
            first = ends // 2 if 2 * held >= ends else 0
            pieces |= set(range(first, held + 1))
        needed.append(pieces - {c, 2 * count - 1 - c})
    plan = []
    for k in range(1, count):
        chosen = {}
        for c in range(count):
            source = (c + k) % count
            pieces = sorted(needed[c] & {source, 2 * count - 1 - source})
            if pieces:
                chosen[source] = (c, pieces)
        if chosen:
            plan.append(([(s, c) for s, (c, _) in chosen.items()], {s: p for s, (_, p) in chosen.items()}))
    return plan


def other_columns(values_in, pick_odd, size):
    blocks = values_in.shape[1] // size
    even, odd = (
        jnp.concatenate([values_in[:, b * size : (b + 1) * size] for b in range(at, blocks, 2)], axis=1)
        for at in (0, 1)
    )
    return jnp.where(pick_odd, odd, even)


def per_device(
    tokens,
    attn_gain,
    w_query,
    w_key,
    w_value,
    w_out,
    ffn_gain,
    w_gate,
    w_up,
    w_down,
    out_cotangent,
    doc_lengths,
):
    ctx_count, ctx_rank = lax.axis_size("ctx"), lax.axis_index("ctx")
    dp_count, dp_rank = lax.axis_size("dp"), lax.axis_index("dp")
    tp_count, tp_rank = lax.axis_size("tp"), lax.axis_index("tp")
    tp_rows, width = tokens.shape[1:]
    ctx_rows = tp_rows * tp_count
    near_rows = ctx_rows // 2
    halves = tp_count // 2
    docs = doc_lengths.shape[1]
    size = width // (dp_count * ctx_count)
    chain = Chain()

    plan = tile_plan(ctx_count)
    nowhere = 2 * ctx_count
    widths = [max(len(p) for p in pieces.values()) for _, pieces in plan]
    got = np.full((ctx_count, sum(widths)), nowhere, np.int32)
    gave = np.zeros((ctx_count, sum(widths)), np.int32)
    for t, (moves, pieces) in enumerate(plan):
        first = sum(widths[:t])
        for source, target in moves:
            listed = pieces[source]
            got[target, first : first + len(listed)] = listed
            high = int(listed[0] != source)
            gave[source, first : first + widths[t]] = [high, 1 - high][: widths[t]]
    top = tp_rank // halves
    starts = jnp.asarray(gave)[ctx_rank] ^ top
    here = jnp.stack([ctx_rank, jnp.int32(ctx_count), tp_rank, jnp.int32(tp_rows)])
    places = jnp.concatenate([here, doc_lengths[0], jnp.asarray(got)[ctx_rank]]).astype(jnp.int32)

    within = jnp.arange(ctx_rows, dtype=jnp.int32) ^ (tp_rank * tp_rows)
    piece = jnp.where(within < near_rows, ctx_rank, 2 * ctx_count - 1 - ctx_rank)
    position = (piece * near_rows + within % near_rows).astype(F32)
    inv_freq = jnp.asarray(rope_table(HD), F32)
    angles = position[:, None] * inv_freq[None, :]
    cosine, sine = jnp.cos(angles), jnp.sin(angles)
    cos = jnp.concatenate([cosine, cosine], axis=1)
    sin = jnp.concatenate([-sine, sine], axis=1)

    perm = jnp.arange(tp_count, dtype=jnp.int32) ^ tp_rank
    mine = ctx_rank % 2
    pairs = ctx_count // 2
    steps = jnp.arange(pairs, dtype=jnp.int32)

    def cols_of(dp_index):
        return (dp_index * ctx_count + 2 * steps + mine).astype(jnp.int32)

    def packed_cols_of(dp_index):
        return (dp_index * pairs + steps).astype(jnp.int32)

    bit = ctx_rank // pairs % 2
    order = ((1 - bit) * (pairs // 2) + steps) % pairs

    class WeightGrad:
        def __init__(self, wide, wide_pair, packed, narrow, narrow_pair, part=(0, 1)):
            def terms(dp_index, *received, zero=False):
                cols = cols_of(dp_index)
                cols_pair = packed_cols_of(dp_index) if packed else cols
                if received:
                    cols, cols_pair = cols[order], cols_pair[order]
                return weight_terms(
                    chain, perm, wide, wide_pair, cols, cols_pair, narrow, narrow_pair, size, part, *received, zero=zero
                )

            self.terms = terms

        def send(self, zero=False):
            self.sent = self.terms(1 - dp_rank, zero=zero)[0]
            self.received = flip(self.sent, "dp", 1)
            return self

        def keep(self):
            chain.wait(self.received)
            sent, self.kept = self.terms(dp_rank, self.received, order)
            self.received = flip(sent, "ctx", pairs)
            self.spread(pairs // 2)

        def spread(self, mask):
            while mask > 1:
                half = jnp.reshape(ctx_rank // mask % 2, (1,))
                sent, self.kept = halve(chain, self.kept, self.received, half, 0)
                self.received = flip(sent, "ctx", mask)
                mask //= 2

        def total(self, zero):
            return (self.kept.astype(F32) + zero) + self.received.astype(F32)

    class OutGrad(WeightGrad):
        def __init__(self, wide, narrow):
            self.wide, self.narrow = wide, narrow

        def pair(self):
            both = jnp.concatenate([steps, steps + pairs])
            cols = (2 * both + 1 - mine).astype(jnp.int32)
            self.received = flip(own_terms(chain, perm, self.wide, cols, self.narrow, size)[0], "ctx", 1)

        def send(self):
            half = ((1 - dp_rank) * pairs + steps).astype(jnp.int32)
            order = jnp.concatenate([half, (dp_rank * pairs + steps).astype(jnp.int32)])
            chain.wait(self.received)
            sent, self.kept = own_terms(
                chain, perm, self.wide, 2 * order + mine, self.narrow, size, self.received, order
            )
            self.received = flip(sent, "dp", 1)

        def keep(self):
            chain.wait(self.received)
            self.spread(pairs)

    inputs = tokens[0].astype(F32)
    normed_local = rms_norm(inputs, attn_gain).astype(BF16)
    normed = tp_gather(normed_local)
    grad_fb_local = out_cotangent[0]
    from_pair = flip(
        jnp.concatenate([grad_fb_local, other_columns(normed_local, mine == 0, size)], axis=1), "ctx", 1
    )
    gathered = lax.all_gather(
        jnp.concatenate([grad_fb_local, from_pair], axis=1), "tp", axis=0, tiled=True
    )
    grad_fb, grad_fb_pair, normed_pair = (
        [(gathered, j, first) for j in range(tp_count)] for first in (0, width, 2 * width)
    )
    kv, query = project(chain, normed, w_query, w_key, w_value, cos, sin)
    low_half = lax.dynamic_slice_in_dim(kv, top * near_rows, near_rows, 0)
    high_half = lax.dynamic_slice_in_dim(kv, (1 - top) * near_rows, near_rows, 0)
    tiles = []
    for t, (moves, _) in enumerate(plan):
        low_first = jnp.asarray(gave)[ctx_rank, sum(widths[:t])] == 0
        held = [jnp.where(low_first, low_half, high_half), jnp.where(low_first, high_half, low_half)]
        held = jnp.concatenate(held[: widths[t]], axis=0)
        tiles.append(lax.ppermute(held, "ctx", moves))
    chain.wait(*tiles)
    merged, totals = attend(chain, places, docs, halves, query, kv, tiles)
    out_terms = pull(chain, [merged], [w_out], tp_count, NN)
    hidden_state = inputs + tp_scatter(out_terms)[1]()

    normed_ffn_local = rms_norm(hidden_state, ffn_gain).astype(BF16)
    normed_ffn = tp_gather(normed_ffn_local)
    chain.room = 52 * 1024 * 1024
    act, slope, silu = ffn_front(chain, normed_ffn, w_gate, w_up)
    normed_ffn_pair = tp_gather(flip(normed_ffn_local, "ctx", 1), chain.zero)
    act_pair, slope_pair, silu_pair = ffn_front(chain, normed_ffn_pair, w_gate, w_up)

    down_w = WeightGrad(grad_fb, grad_fb_pair, False, act, act_pair).send()
    grad_gate, grad_up = ffn_back(chain, perm, grad_fb, w_down, slope, silu)
    nffn_terms = pull(chain, [grad_gate, grad_up], [w_gate, w_up], tp_count)
    nffn_sent, nffn_sum = tp_scatter(nffn_terms)
    grad_gate_pair, grad_up_pair = ffn_back(chain, perm, grad_fb_pair, w_down, slope_pair, silu_pair)
    chain.wait(nffn_sent)
    gate_w = WeightGrad(normed_ffn, normed_ffn_pair, False, grad_gate, grad_gate_pair).send()
    up_w = WeightGrad(normed_ffn, normed_ffn_pair, False, grad_up, grad_up_pair)
    down_w.keep()
    grad_nffn = nffn_sum() + chain.zero
    grad_state_norm, grad_ffn_gain = jax.vjp(rms_norm, hidden_state, ffn_gain)[1](grad_nffn)
    grad_state = grad_fb_local.astype(F32) + grad_state_norm
    grad_sb_local = grad_state.astype(BF16)
    grad_sb = tp_gather(grad_sb_local)
    chain.wait(grad_sb_local)
    up_w.send()

    grad_query, own, *sent = attend_back(
        chain, places, docs, halves, query, merged, totals, cos, sin, w_out, grad_sb, kv, tiles
    )
    chain.room = VMEM_BYTES * 3 // 4
    returned = [
        lax.ppermute(part, "ctx", [(target, source) for source, target in moves])
        for part, (moves, _) in zip(sent, plan)
    ]
    chain.wait(down_w.received)
    gate_w.keep()
    chain.wait(*returned)
    grad_qkv, grad_key, grad_value = finish(chain, starts, cos, sin, grad_query, own, returned)
    grad_qkv_pair = flip(grad_qkv, "ctx", 1)
    up_w.keep()
    out_w = OutGrad(grad_sb, merged)
    out_w.pair()
    back_terms = pull(chain, [grad_query, grad_key, grad_value], [w_query, w_key, w_value], tp_count)
    layer_terms = push(chain, perm, act, w_down)
    layer_sum = lax.psum_scatter(layer_terms, "tp", scatter_dimension=0, tiled=True)
    layer_out = (hidden_state + layer_sum.astype(F32)).astype(BF16)
    normed_sent, normed_sum = tp_scatter(back_terms)
    chain.wait(grad_qkv_pair)
    qkv_w = WeightGrad(normed, normed_pair, True, grad_qkv, grad_qkv_pair).send(True)
    grad_normed = normed_sum() + chain.zero
    grad_input_norm, grad_attn_gain = jax.vjp(rms_norm, inputs, attn_gain)[1](grad_normed)
    input_grad = grad_state + grad_input_norm
    sent_zero = chain.zero
    chain.wait(gate_w.received)
    qkv_w.keep()
    out_w.send()
    out_zero = chain.zero
    chain.wait(up_w.received)
    out_w.keep()
    zero = chain.zero
    gains = sum_over(jnp.stack([grad_attn_gain, grad_ffn_gain]) + out_zero, "tp")
    gains = sum_over(sum_over(gains + zero, "dp"), "ctx")
    q_width, kv_width = w_query.shape[1], w_key.shape[1]
    out_total = out_w.total(zero).T
    qkv_total = qkv_w.total(zero)
    return (
        layer_out[None],
        input_grad[None],
        gains[0],
        qkv_total[:, :q_width],
        qkv_total[:, q_width : q_width + kv_width],
        qkv_total[:, q_width + kv_width :],
        out_total,
        gains[1],
        gate_w.total(out_zero),
        up_w.total(zero),
        down_w.total(sent_zero).T,
    )


def solution(mesh):
    placed = (
        P("dp", ("ctx", "tp"), None),
        P(),
        P(None, "tp"),
        P(None, "tp"),
        P(None, "tp"),
        P("tp", None),
        P(),
        P(None, "tp"),
        P(None, "tp"),
        P("tp", None),
        P("dp", ("ctx", "tp"), None),
        P("dp", None),
    )
    return jax.shard_map(
        per_device,
        mesh=mesh,
        in_specs=placed,
        out_specs=(
            P("dp", ("ctx", "tp"), None),
            P("dp", ("ctx", "tp"), None),
            P(),
            P(("dp", "ctx"), "tp"),
            P(("dp", "ctx"), "tp"),
            P(("dp", "ctx"), "tp"),
            P("tp", ("dp", "ctx")),
            P(),
            P(("dp", "ctx"), "tp"),
            P(("dp", "ctx"), "tp"),
            P("tp", ("dp", "ctx")),
        ),
        check_vma=False,
    )
```

```python
import functools
import math

import jax
import jax.numpy as jnp
import numpy as np
from jax import lax
from jax.experimental import pallas as pl
from jax.experimental.pallas import tpu as pltpu
from jax.sharding import PartitionSpec as P

HD = 64
EPSILON = 1e-05
NEGATIVE = -1e30
ROPE_THETA = 500000.0


def rope_table(head_size):
    base_freq = np.array(
        [ROPE_THETA ** (-2.0 * index / head_size) for index in range(head_size // 2)]
    )
    wavelength = 2.0 * math.pi / base_freq
    blend = (8192.0 / wavelength - 1.0) / 3.0
    middle = (1.0 - blend) * base_freq / 32.0 + blend * base_freq
    return np.where(
        wavelength > 8192.0, base_freq / 32.0, np.where(wavelength < 2048.0, base_freq, middle)
    )


def rms_norm(values_in, gain_vec):
    return (
        values_in
        * lax.rsqrt(jnp.mean(values_in * values_in, axis=-1, keepdims=True) + EPSILON)
        * gain_vec
    )


F32, BF16 = jnp.float32, jnp.bfloat16
VMEM_BYTES = 62 * 1024 * 1024
NN = (((1,), (0,)), ((), ()))
NT = (((1,), (1,)), ((), ()))
TN = (((0,), (0,)), ((), ()))
VMEM = pl.BlockSpec(memory_space=pltpu.VMEM)
SMEM = pl.BlockSpec(memory_space=pltpu.SMEM)
ANYWHERE = pl.BlockSpec(memory_space=pl.ANY)


def dot(left, right, dims=NN):
    return lax.dot_general(left, right, dims, preferred_element_type=F32)


def part_specs(parts, rows, width, col):
    def spec(part):
        if not isinstance(part, tuple):
            return pl.BlockSpec((rows, width), lambda *at: (0, col(*at)))
        j, first = part[1:]
        return pl.BlockSpec(
            (rows, width), lambda *at: (0 if j is None else at[-1][j], first // width + col(*at))
        )

    return [spec(part) for part in parts]


def part_arrays(parts):
    return [part[0] if isinstance(part, tuple) else part for part in parts]


def rows_of(refs):
    return jnp.concatenate([ref[...] for ref in refs], axis=0)


class Chain:
    def __init__(self):
        self.held = []
        self.cost = 69 * 10**8
        self.room = VMEM_BYTES // 2

    def wait(self, *arrays):
        self.held = [*arrays, *self.held]

    def call(
        self, name, body, args, in_specs, out_specs, out_shape, flops, grid=(), scalars=0, scratch=(), zero=False
    ):
        held, count, outs = self.held, len(args), len(out_shape)
        marks, mark_specs = [jax.ShapeDtypeStruct((8, 128), F32)], [ANYWHERE]
        if zero:
            marks.append(jax.ShapeDtypeStruct((1, 1), F32))
            mark_specs.append(SMEM)

        def inner(*refs):
            rest = refs[count + len(held) :]
            given = refs[:scalars] + refs[scalars + len(held) : count + len(held)]
            body(*given, *rest[:outs], *rest[outs + len(marks) :])
            if zero:
                rest[outs + 1][0, 0] = 0.0

        results = pl.pallas_call(
            inner,
            grid_spec=pltpu.PrefetchScalarGridSpec(
                num_scalar_prefetch=scalars,
                grid=grid,
                in_specs=[ANYWHERE] * len(held) + list(in_specs),
                out_specs=[*out_specs, *mark_specs],
                scratch_shapes=list(scratch),
            ),
            out_shape=[*out_shape, *marks],
            compiler_params=pltpu.CompilerParams(
                vmem_limit_bytes=self.room, dimension_semantics=("arbitrary",) * len(grid)
            ),
            cost_estimate=pl.CostEstimate(flops=self.cost, bytes_accessed=1, transcendentals=0),
            name=name,
        )(*args[:scalars], *held, *args[scalars:])
        self.held = [results[outs]]
        if zero:
            self.zero = results[outs + 1][0, 0]
        return results[:outs]


def fill_rows(parts, rows_ref):
    @pl.when(pl.program_id(0) == 0)
    def _():
        rows_ref[...] = rows_of(parts)


def ffn_front_body(count, *refs):
    gate_ref, up_ref, act_ref, slope_ref, silu_ref, rows_ref = refs[count:]
    fill_rows(refs[:count], rows_ref)
    rows = rows_ref[...]
    gate = dot(rows, gate_ref[...])
    up = dot(rows, up_ref[...])
    sigma = 1.0 / (1.0 + jnp.exp(-gate))
    silu = gate * sigma
    act_ref[...] = (silu * up).astype(BF16)
    slope_ref[...] = (up * sigma * (1.0 + gate * (1.0 - sigma))).astype(BF16)
    silu_ref[...] = silu.astype(BF16)


def whole(array):
    return pl.BlockSpec(array.shape, lambda *_: (0,) * array.ndim)


def ffn_front(chain, parts, w_gate, w_up, part=(0, 1), block=512):
    count, width = sum(p.shape[0] for p in parts), parts[0].shape[1]
    units = w_gate.shape[1] // part[1]
    block = min(block, units)
    first = part[0] * (units // block)
    weight = pl.BlockSpec((width, block), lambda j: (0, first + j))
    return chain.call(
        "ffn_front",
        functools.partial(ffn_front_body, len(parts)),
        (*parts, w_gate, w_up),
        [whole(p) for p in parts] + [weight, weight],
        [pl.BlockSpec((count, block), lambda j: (0, j))] * 3,
        [jax.ShapeDtypeStruct((count, units), BF16)] * 3,
        4 * count * width * units,
        grid=(units // block,),
        scratch=[pltpu.VMEM((count, width), BF16)],
        zero=True,
    )


def ffn_back_body(count, perm_ref, *refs):
    down_ref, slope_ref, silu_ref, gate_ref, up_ref, rows_ref = refs[count:]
    fill_rows(refs[:count], rows_ref)
    grad_act = dot(rows_ref[...], down_ref[...], NT)
    gate_ref[...] = (grad_act * slope_ref[...].astype(F32)).astype(BF16)
    up_ref[...] = (grad_act * silu_ref[...].astype(F32)).astype(BF16)


def ffn_back(chain, perm, parts, w_down, slope, silu, block=512):
    count, units = slope.shape
    width = w_down.shape[1]
    block = min(block, units)
    tile = pl.BlockSpec((count, block), lambda j, _: (0, j))
    return chain.call(
        "ffn_back",
        functools.partial(ffn_back_body, len(parts)),
        (perm, *part_arrays(parts), w_down, slope, silu),
        part_specs(parts, count // len(parts), width, lambda *_: 0)
        + [pl.BlockSpec((block, width), lambda j, _: (j, 0)), tile, tile],
        [tile, tile],
        [jax.ShapeDtypeStruct((count, units), BF16)] * 2,
        2 * count * width * units,
        grid=(units // block,),
        scalars=1,
        scratch=[pltpu.VMEM((count, width), BF16)],
    )


def pull_body(count, dims, *refs):
    total = dot(refs[0][...], refs[count][...], dims)
    for i in range(1, count):
        total = total + dot(refs[i][...], refs[count + i][...], dims)
    outs = refs[2 * count :]
    rows = total.shape[0] // len(outs)
    for j, out in enumerate(outs):
        out[...] = total[j * rows : (j + 1) * rows].astype(BF16)


def pull(chain, grads, weights, blocks, dims=NT, block=1024):
    rows, at = grads[0].shape[0], 0 if dims == NT else 1
    width = weights[0].shape[at]
    depth = sum(w.shape[1 - at] for w in weights)
    return chain.call(
        "pull",
        functools.partial(pull_body, len(grads), dims),
        (*grads, *weights),
        [whole(g) for g in grads]
        + [
            pl.BlockSpec((block, w.shape[1]), lambda j: (j, 0))
            if dims == NT
            else pl.BlockSpec((w.shape[0], block), lambda j: (0, j))
            for w in weights
        ],
        [pl.BlockSpec((rows // blocks, block), lambda j: (0, j))] * blocks,
        [jax.ShapeDtypeStruct((rows // blocks, width), BF16)] * blocks,
        2 * rows * width * depth,
        grid=(width // block,),
        zero=True,
    )


def push_body(blocks, perm_ref, rows_ref, weight_ref, out_ref):
    total = dot(rows_ref[...], weight_ref[...]).astype(BF16)
    rows = total.shape[0] // blocks
    for j in range(blocks):
        at = pl.ds(pl.multiple_of(perm_ref[j] * rows, rows), rows)
        out_ref[at] = total[j * rows : (j + 1) * rows]


def push(chain, perm, rows, weight, block=1024):
    count, depth = rows.shape
    width = weight.shape[1]
    return chain.call(
        "push",
        functools.partial(push_body, perm.shape[0]),
        (perm, rows, weight),
        [
            pl.BlockSpec((count, depth), lambda j, _: (0, 0)),
            pl.BlockSpec((depth, block), lambda j, _: (0, j)),
        ],
        [pl.BlockSpec((count, block), lambda j, _: (0, j))],
        [jax.ShapeDtypeStruct((count, width), BF16)],
        2 * count * depth * width,
        grid=(width // block,),
        scalars=1,
    )[0]


def terms_body(count, blocks, scalars, *refs):
    refs = refs[scalars:]
    wide, wide_pair = rows_of(refs[:count]), rows_of(refs[count : 2 * count])
    own, pair = refs[2 * count : 2 * count + 2]
    total = dot(wide, own[...], TN) + dot(wide_pair, pair[...], TN)
    if scalars == 3:
        refs[-1][...] = total.astype(BF16)
        return
    got, sent_ref, left_ref = refs[2 * count + 2 :]
    total = (total + got[...].astype(F32)).astype(BF16)

    @pl.when(pl.program_id(1) < blocks // 2)
    def _():
        sent_ref[...] = total

    @pl.when(pl.program_id(1) >= blocks // 2)
    def _():
        left_ref[...] = total


def weight_terms(chain, perm, wide, wide_pair, cols, cols_pair, narrow, narrow_pair, size, part, received=None, order=None, zero=False):
    tokens, units = narrow.shape
    units //= part[1]
    blocks = cols.shape[0]
    block = units if units <= 2048 else math.gcd(2048, units)
    first = part[0] * (units // block)
    rows = tokens // len(wide)
    units_spec = pl.BlockSpec((tokens, block), lambda j, i, *_: (0, first + j))
    scalars = [cols, cols_pair, perm]
    in_specs = (
        part_specs(wide, rows, size, lambda j, i, *s: s[-3][i])
        + part_specs(wide_pair, rows, size, lambda j, i, *s: s[-2][i])
        + [units_spec, units_spec]
    )
    args = [*part_arrays(wide), *part_arrays(wide_pair), narrow, narrow_pair]
    if received is None:
        out_specs = [pl.BlockSpec((size, block), lambda j, i, *_: (i, j))]
        out = [jax.ShapeDtypeStruct((blocks * size, units), BF16)]
    else:
        half = blocks // 2
        scalars = [order] + scalars
        args.append(received)
        in_specs.append(pl.BlockSpec((size, block), lambda j, i, io, *_: (io[i], j)))
        out_specs = [
            pl.BlockSpec((size, block), lambda j, i, *_: (jnp.minimum(i, half - 1), j)),
            pl.BlockSpec((size, block), lambda j, i, *_: (jnp.maximum(i - half, 0), j)),
        ]
        out = [jax.ShapeDtypeStruct((half * size, units), BF16)] * 2
    return chain.call(
        "weight_terms",
        functools.partial(terms_body, len(wide), blocks, len(scalars)),
        (*scalars, *args),
        in_specs,
        out_specs,
        out,
        4 * tokens * units * blocks * size,
        grid=(units // block, blocks),
        scalars=len(scalars),
        zero=zero or received is not None,
    )


def own_terms_body(count, blocks, scalars, *refs):
    refs = refs[scalars:]
    total = dot(rows_of(refs[:count]), refs[count][...], TN)
    if scalars == 2:
        refs[-1][...] = total.astype(BF16)
        return
    got, sent_ref, left_ref = refs[count + 1 :]
    total = (total + got[...].astype(F32)).astype(BF16)

    @pl.when(pl.program_id(0) < blocks // 2)
    def _():
        sent_ref[...] = total

    @pl.when(pl.program_id(0) >= blocks // 2)
    def _():
        left_ref[...] = total


def own_terms(chain, perm, wide, cols, narrow, size, received=None, order=None):
    tokens, units = narrow.shape
    blocks = cols.shape[0]
    rows = tokens // len(wide)
    half = blocks // 2
    scalars = [cols, perm]
    args = [*part_arrays(wide), narrow]
    in_specs = part_specs(wide, rows, size, lambda i, *s: s[-2][i]) + [whole(narrow)]
    if received is None:
        out_specs = [pl.BlockSpec((size, units), lambda i, *_: (i, 0))]
        out = [jax.ShapeDtypeStruct((blocks * size, units), BF16)]
    else:
        scalars = [order] + scalars
        args.append(received)
        in_specs.append(pl.BlockSpec((size, units), lambda i, io, *_: (io[i], 0)))
        out_specs = [
            pl.BlockSpec((size, units), lambda i, *_: (jnp.minimum(i, half - 1), 0)),
            pl.BlockSpec((size, units), lambda i, *_: (jnp.maximum(i - half, 0), 0)),
        ]
        out = [jax.ShapeDtypeStruct((half * size, units), BF16)] * 2
    return chain.call(
        "own_terms",
        functools.partial(own_terms_body, len(wide), blocks, len(scalars)),
        (*scalars, *args),
        in_specs,
        out_specs,
        out,
        2 * tokens * units * blocks * size,
        grid=(blocks,),
        scalars=len(scalars),
        zero=True,
    )


def halve_body(mine, kept_send, got_send, kept, got, sent_ref, left_ref):
    sent_ref[...] = (kept_send[...].astype(F32) + got_send[...].astype(F32)).astype(BF16)
    left_ref[...] = (kept[...].astype(F32) + got[...].astype(F32)).astype(BF16)


def halve(chain, kept, received, mine, dim):
    steps = math.gcd(4, kept.shape[1 - dim] // 128)
    shape = list(kept.shape)
    shape[dim] //= 2
    block = list(shape)
    block[1 - dim] //= steps

    def spec(flip_half):
        def at(j, m):
            half = 1 - m[0] if flip_half else m[0]
            return (half, j) if dim == 0 else (j, half)

        return pl.BlockSpec(tuple(block), at)

    out_spec = pl.BlockSpec(tuple(block), lambda j, m: (0, j) if dim == 0 else (j, 0))
    out = jax.ShapeDtypeStruct(tuple(shape), BF16)
    return chain.call(
        "halve",
        halve_body,
        (mine, kept, received, kept, received),
        [spec(True), spec(True), spec(False), spec(False)],
        [out_spec, out_spec],
        [out, out],
        kept.size,
        grid=(steps,),
        scalars=1,
        zero=True,
    )


def swap_halves(values_in):
    half = HD // 2
    width = values_in.shape[1]
    if width % 128:
        parts = []
        for at in range(0, width, HD):
            parts += [values_in[:, at + half : at + HD], values_in[:, at : at + half]]
        return jnp.concatenate(parts, axis=1)
    lane = lax.broadcasted_iota(jnp.int32, values_in.shape, 1)
    return jnp.where(
        lane % HD < half,
        pltpu.roll(values_in, width - half, 1),
        pltpu.roll(values_in, half, 1),
    )


def turn(values_in, cos_ref, sin_ref, sign):
    count = values_in.shape[1] // HD
    cos = jnp.concatenate([cos_ref[...]] * count, axis=1)
    sin = jnp.concatenate([sin_ref[...]] * count, axis=1)
    return values_in * cos + sign * (swap_halves(values_in) * sin)


def project_body(count, *refs):
    q_ref, k_ref, v_ref, cos_ref, sin_ref, kv_ref, query_ref = refs[count:]
    rows = rows_of(refs[:count])
    width = k_ref.shape[1]
    kv_ref[:, :width] = turn(dot(rows, k_ref[...]), cos_ref, sin_ref, 1.0).astype(BF16)
    kv_ref[:, width:] = dot(rows, v_ref[...]).astype(BF16)
    queries = turn(dot(rows, q_ref[...]), cos_ref, sin_ref, 1.0).astype(BF16)
    query_ref[...] = (queries.astype(F32) * (1.0 / math.sqrt(HD))).astype(BF16)


def project(chain, parts, w_query, w_key, w_value, cos, sin):
    count = sum(p.shape[0] for p in parts)
    kv = jax.ShapeDtypeStruct((count, 2 * w_key.shape[1]), BF16)
    query = jax.ShapeDtypeStruct((count, w_query.shape[1]), BF16)
    return chain.call(
        "project",
        functools.partial(project_body, len(parts)),
        (*parts, w_query, w_key, w_value, cos, sin),
        [VMEM] * (len(parts) + 5),
        [VMEM] * 2,
        [kv, query],
        2 * count * parts[0].shape[1] * (query.shape[1] + kv.shape[1]),
    )


def half_piece(places_ref, half, halves):
    top = places_ref[2] // halves
    return jnp.where(top == half, places_ref[0], 2 * places_ref[1] - 1 - places_ref[0])


def doc_start(places_ref, docs, position):
    end = 0
    start = position * 0
    for i in range(docs):
        end = end + places_ref[4 + i]
        start = jnp.where(position >= end, end, start)
    return start, position < end


def positions_of(places_ref, piece, halves, rows, shape, dim):
    row = lax.broadcasted_iota(jnp.int32, shape, dim)
    inner = lax.rem(places_ref[2], halves) * places_ref[3]
    return piece * rows + (row ^ inner)


def tile_count(tiles, rows):
    return sum(t.shape[0] for t in tiles) // rows + 2


def half_of(places_ref, docs, halves, half, rows, group):
    piece = half_piece(places_ref, half, halves)
    position = positions_of(places_ref, piece, halves, rows, (1, rows), 1)
    start, valid = doc_start(places_ref, docs, position)
    first = doc_start(places_ref, docs, piece * rows)[0]
    position, start, valid = (
        jnp.concatenate([v] * group, axis=1) for v in (position, start, valid.astype(jnp.int32))
    )
    return piece, position, start, valid, first


def tile_piece(places_ref, docs, halves, t):
    given = places_ref[4 + docs + jnp.maximum(t - 2, 0)]
    own = jnp.where(t == 0, half_piece(places_ref, 0, halves), half_piece(places_ref, 1, halves))
    return jnp.where(t < 2, own, given)


def split_tiles(kv_refs, rows, keys_ref, values_ref, ones):
    kv_heads = keys_ref.shape[0]
    t = 0
    for ref in kv_refs:
        for row in range(0, ref.shape[0], rows):
            for g in range(kv_heads):
                keys_ref[g, t] = ref[row : row + rows, g * HD : (g + 1) * HD]
                values = ref[row : row + rows, (kv_heads + g) * HD : (kv_heads + g + 1) * HD]
                if ones:
                    values = jnp.concatenate([values, jnp.ones_like(values)], axis=1)
                values_ref[g, t] = values
            t += 1


def split_heads(ref, rows, group, out_ref, change=lambda v, half: v):
    kv_heads = out_ref.shape[0] // 2
    for half in range(2):
        for g in range(kv_heads):
            for i in range(group):
                head = (g * group + i) * HD
                values = ref[half * rows : (half + 1) * rows, head : head + HD]
                out_ref[half * kv_heads + g, i * rows : (i + 1) * rows] = change(values, half)


def attend_body(docs, halves, count, places_ref, q_ref, kv_ref, *refs):
    tile_refs, (merged_ref, total_ref) = refs[:count], refs[count : count + 2]
    keys_ref, values_ref, stack_ref, scores_ref, peak_ref, sums_ref, out_ref = refs[count + 2 :]
    rows = q_ref.shape[0] // 2
    kv_heads, tiles = keys_ref.shape[:2]
    group = q_ref.shape[1] // HD // kv_heads
    split_tiles([kv_ref, *tile_refs], rows, keys_ref, values_ref, True)
    split_heads(q_ref, rows, group, stack_ref)

    def one(hg, carry):
        half, g = hg // kv_heads, hg % kv_heads
        q_piece, q_pos, q_start, valid, first = half_of(places_ref, docs, halves, half, rows, group)
        peak_ref[...] = jnp.full(peak_ref.shape, NEGATIVE, F32)
        sums_ref[...] = jnp.zeros(sums_ref.shape, F32)

        def score(t, carry):
            piece = tile_piece(places_ref, docs, halves, t)

            @pl.when((piece <= q_piece) & ((piece + 1) * rows > first))
            def _():
                k_pos = positions_of(places_ref, piece, halves, rows, (rows, 1), 0)
                scores = dot(keys_ref[g, t], stack_ref[hg], NT)
                scores = jnp.where((k_pos <= q_pos) & (k_pos >= q_start), scores, NEGATIVE)
                scores_ref[t] = scores
                top = jnp.max(scores.reshape(rows // 8, 8, group * rows), axis=0)
                peak_ref[...] = jnp.maximum(peak_ref[...], top)

            return carry

        lax.fori_loop(0, tiles, score, 0)
        peak = jnp.max(peak_ref[...], axis=0, keepdims=True)

        def weigh(t, carry):
            piece = tile_piece(places_ref, docs, halves, t)

            @pl.when((piece <= q_piece) & ((piece + 1) * rows > first))
            def _():
                expo = jnp.exp(scores_ref[t] - peak).astype(BF16)
                sums_ref[...] += dot(values_ref[g, t], expo, TN)

            return carry

        lax.fori_loop(0, tiles, weigh, 0)
        total = sums_ref[HD : HD + 1]
        out_ref[hg] = jnp.where(valid > 0, sums_ref[...] / total, 0.0).T.astype(BF16)
        total_ref[hg] = peak + jnp.log(total)
        return carry

    lax.fori_loop(0, 2 * kv_heads, one, 0)
    for half in range(2):
        for g in range(kv_heads):
            for i in range(group):
                head = (g * group + i) * HD
                merged_ref[half * rows : (half + 1) * rows, head : head + HD] = out_ref[
                    half * kv_heads + g, i * rows : (i + 1) * rows, :HD
                ]


def attend(chain, places, docs, halves, query, kv, tiles):
    tokens, width = query.shape
    rows = tokens // 2
    heads, kv_heads = width // HD, kv.shape[1] // 2 // HD
    span = heads // kv_heads * rows
    tile_num = tile_count(tiles, rows)
    return chain.call(
        "attend",
        functools.partial(attend_body, docs, halves, len(tiles)),
        (places, query, kv, *tiles),
        [SMEM] + [VMEM] * (2 + len(tiles)),
        [VMEM] * 2,
        [
            jax.ShapeDtypeStruct((tokens, width), BF16),
            jax.ShapeDtypeStruct((2 * kv_heads, 1, span), F32),
        ],
        8 * tokens * rows * tile_num * width,
        scratch=[
            pltpu.VMEM((kv_heads, tile_num, rows, HD), BF16),
            pltpu.VMEM((kv_heads, tile_num, rows, 2 * HD), BF16),
            pltpu.VMEM((2 * kv_heads, span, HD), BF16),
            pltpu.VMEM((tile_num, rows, span), F32),
            pltpu.VMEM((8, span), F32),
            pltpu.VMEM((2 * HD, span), F32),
            pltpu.VMEM((2 * kv_heads, span, 2 * HD), BF16),
        ],
    )


def attend_back_body(docs, halves, count, parts, *refs):
    places_ref, q_ref, merged_ref, total_ref, cos_ref, sin_ref, w_ref = refs[:7]
    kv_ref, tile_refs = refs[7 + parts], refs[8 + parts : 8 + parts + count]
    grad_q_ref, grad_own_ref, *grad_tile_refs = refs[8 + parts + count : 10 + parts + 2 * count]
    grad_ref, keys_ref, values_ref, stack_ref, grads_ref, outs_ref, q_sum_ref, kv_sum_ref = refs[
        10 + parts + 2 * count :
    ]
    rows = q_ref.shape[0] // 2
    kv_heads, tiles = keys_ref.shape[:2]
    group = q_ref.shape[1] // HD // kv_heads
    grad_ref[...] = dot(rows_of(refs[7 : 7 + parts]), w_ref[...], NT).astype(BF16)
    split_tiles([kv_ref, *tile_refs], rows, keys_ref, values_ref, False)
    split_heads(q_ref, rows, group, stack_ref)
    split_heads(merged_ref, rows, group, outs_ref)
    shown = []
    for half in range(2):
        piece = half_piece(places_ref, half, halves)
        position = positions_of(places_ref, piece, halves, rows, (rows, 1), 0)
        shown.append(doc_start(places_ref, docs, position)[1])

    def masked(values, half):
        return jnp.where(shown[half], values.astype(F32), 0.0).astype(BF16)

    split_heads(grad_ref, rows, group, grads_ref, masked)
    kv_sum_ref[...] = jnp.zeros(kv_sum_ref.shape, F32)
    q_sum_ref[...] = jnp.zeros(q_sum_ref.shape, F32)

    def one(hg, carry):
        half, g = hg // kv_heads, hg % kv_heads
        q_piece, q_pos, q_start, _, first = half_of(places_ref, docs, halves, half, rows, group)
        product = grads_ref[hg].astype(F32) * outs_ref[hg].astype(F32)
        high = product.astype(BF16)
        low = (product - high.astype(F32)).astype(BF16)
        ones = jnp.ones((8, HD), BF16)
        delta = (dot(ones, high, NT) + dot(ones, low, NT))[:1]
        totals = total_ref[hg]

        def back(t, carry):
            piece = tile_piece(places_ref, docs, halves, t)

            @pl.when((piece <= q_piece) & ((piece + 1) * rows > first))
            def _():
                k_pos = positions_of(places_ref, piece, halves, rows, (rows, 1), 0)
                keys, queries, grads = keys_ref[g, t], stack_ref[hg], grads_ref[hg]
                scores = dot(keys, queries, NT) - totals
                scores = jnp.where((k_pos <= q_pos) & (k_pos >= q_start), scores, NEGATIVE)
                probs = jnp.exp(scores)
                grad_probs = dot(values_ref[g, t], grads, NT)
                grad_scores = (probs * (grad_probs - delta)).astype(BF16)
                q_sum_ref[hg, :HD] += dot(keys, grad_scores, TN)
                kv_sum_ref[t, 0, g] += dot(grad_scores, queries)
                kv_sum_ref[t, 1, g] += dot(probs.astype(BF16), grads)

            return carry

        lax.fori_loop(0, tiles, back, 0)
        return carry

    lax.fori_loop(0, 2 * kv_heads, one, 0)
    for half in range(2):
        at = pl.ds(half * rows, rows)
        for g in range(kv_heads):
            q_sum = q_sum_ref[half * kv_heads + g].T
            for i in range(group):
                head = (g * group + i) * HD
                part = q_sum[i * rows : (i + 1) * rows, :HD] * (1.0 / math.sqrt(HD))
                part = part * cos_ref[at] - swap_halves(part) * sin_ref[at]
                grad_q_ref[at, head : head + HD] = part.astype(BF16)
    targets = [
        (out, row) for out in (grad_own_ref, *grad_tile_refs) for row in range(0, out.shape[0], rows)
    ]
    for t, (out_ref, row) in enumerate(targets):
        for part in range(2):
            for g in range(kv_heads):
                cols = slice((part * kv_heads + g) * HD, (part * kv_heads + g + 1) * HD)
                out_ref[row : row + rows, cols] = kv_sum_ref[t, part, g].astype(out_ref.dtype)


def attend_back(chain, places, docs, halves, query, merged, totals, cos, sin, w_out, grads, kv, tiles):
    tokens, width = query.shape
    rows = tokens // 2
    kv_heads = kv.shape[1] // 2 // HD
    span = width // HD // kv_heads * rows
    tile_num = tile_count(tiles, rows)
    stack = pltpu.VMEM((2 * kv_heads, span, HD), BF16)
    return chain.call(
        "attend_back",
        functools.partial(attend_back_body, docs, halves, len(tiles), len(grads)),
        (places, query, merged, totals, cos, sin, w_out, *grads, kv, *tiles),
        [SMEM] + [VMEM] * (7 + len(grads) + len(tiles)),
        [VMEM] * (2 + len(tiles)),
        [jax.ShapeDtypeStruct((tokens, width), BF16), jax.ShapeDtypeStruct(kv.shape, F32)]
        + [jax.ShapeDtypeStruct(t.shape, BF16) for t in tiles],
        16 * tokens * rows * tile_num * width,
        scratch=[
            pltpu.VMEM((tokens, width), BF16),
            pltpu.VMEM((kv_heads, tile_num, rows, HD), BF16),
            pltpu.VMEM((kv_heads, tile_num, rows, HD), BF16),
            stack,
            stack,
            stack,
            pltpu.VMEM((2 * kv_heads, 2 * HD, span), F32),
            pltpu.VMEM((tile_num, 2, kv_heads, rows, HD), F32),
        ],
    )


def finish_body(starts_ref, cos_ref, sin_ref, query_ref, own_ref, *refs):
    parts, (all_ref, key_ref, value_ref, total_ref) = refs[:-4], refs[-4:]
    total_ref[...] = own_ref[...]
    rows = own_ref.shape[0] // 2
    tiles = [(part, row) for part in parts for row in range(0, part.shape[0], rows)]
    for t, (part, row) in enumerate(tiles):
        at = pl.ds(pl.multiple_of(starts_ref[t] * rows, rows), rows)
        total_ref[at] += part[row : row + rows].astype(F32)
    width = key_ref.shape[1]
    keys = turn(total_ref[:, :width], cos_ref, sin_ref, -1.0).astype(BF16)
    values = total_ref[:, width:].astype(BF16)
    key_ref[...] = keys
    value_ref[...] = values
    wide = query_ref.shape[1]
    all_ref[:, :wide] = query_ref[...]
    all_ref[:, wide : wide + width] = keys
    all_ref[:, wide + width :] = values


def finish(chain, starts, cos, sin, grad_query, own, parts):
    tokens, width = own.shape
    wide = grad_query.shape[1] + width
    one = jax.ShapeDtypeStruct((tokens, width // 2), BF16)
    return chain.call(
        "finish",
        finish_body,
        (starts, cos, sin, grad_query, own, *parts),
        [SMEM] + [VMEM] * (4 + len(parts)),
        [VMEM] * 3,
        [jax.ShapeDtypeStruct((tokens, wide), BF16), one, one],
        20 * tokens * width,
        scratch=[pltpu.VMEM((tokens, width), F32)],
    )


def flip(values_in, axis, mask):
    count = lax.axis_size(axis)
    return lax.ppermute(values_in, axis, [(i, i ^ mask) for i in range(count)])


def later(values_in, zero):
    return (values_in.astype(F32) + zero).astype(BF16)


def tp_gather(shard, zero=None):
    count = lax.axis_size("tp")
    parts = {0: shard}
    mask = 2
    while mask < count:
        parts.update({j ^ mask: flip(part, "tp", mask) for j, part in parts.items()})
        mask *= 2
    for j, part in list(parts.items()):
        parts[j ^ 1] = flip(later(part, zero) if j and zero is not None else part, "tp", 1)
    return [parts[j] for j in range(count)]


def tp_scatter(terms):
    count = len(terms)
    received = {j: flip(terms[j + 1], "tp", 1) for j in reversed(range(0, count, 2))}
    blocks = {j: terms[j].astype(F32) + part.astype(F32) for j, part in received.items()}
    mask = count // 2
    while mask > 2:
        for j in range(0, mask, 2):
            blocks[j] = blocks[j] + flip(blocks[j + mask].astype(BF16), "tp", mask).astype(F32)
        mask //= 2
    sent = blocks[2].astype(BF16)
    return sent, lambda: blocks[0] + flip(sent, "tp", 2).astype(F32)


def sum_over(values_in, axis):
    mask = 1
    while mask < lax.axis_size(axis):
        values_in = values_in + flip(values_in, axis, mask)
        mask *= 2
    return values_in


def tile_plan(count):
    ends = 2 * count + 3
    needed = []
    for c in range(count):
        pieces = set()
        for held in (c, 2 * count - 1 - c):
            first = ends // 2 if 2 * held >= ends else 0
            pieces |= set(range(first, held + 1))
        needed.append(pieces - {c, 2 * count - 1 - c})
    plan = []
    for k in range(1, count):
        chosen = {}
        for c in range(count):
            source = (c + k) % count
            pieces = sorted(needed[c] & {source, 2 * count - 1 - source})
            if pieces:
                chosen[source] = (c, pieces)
        if chosen:
            plan.append(([(s, c) for s, (c, _) in chosen.items()], {s: p for s, (_, p) in chosen.items()}))
    return plan


def other_columns(values_in, pick_odd, size):
    blocks = values_in.shape[1] // size
    even, odd = (
        jnp.concatenate([values_in[:, b * size : (b + 1) * size] for b in range(at, blocks, 2)], axis=1)
        for at in (0, 1)
    )
    return jnp.where(pick_odd, odd, even)


def per_device(
    tokens,
    attn_gain,
    w_query,
    w_key,
    w_value,
    w_out,
    ffn_gain,
    w_gate,
    w_up,
    w_down,
    out_cotangent,
    doc_lengths,
):
    ctx_count, ctx_rank = lax.axis_size("ctx"), lax.axis_index("ctx")
    dp_count, dp_rank = lax.axis_size("dp"), lax.axis_index("dp")
    tp_count, tp_rank = lax.axis_size("tp"), lax.axis_index("tp")
    tp_rows, width = tokens.shape[1:]
    ctx_rows = tp_rows * tp_count
    near_rows = ctx_rows // 2
    halves = tp_count // 2
    docs = doc_lengths.shape[1]
    size = width // (dp_count * ctx_count)
    chain = Chain()

    plan = tile_plan(ctx_count)
    nowhere = 2 * ctx_count
    widths = [max(len(p) for p in pieces.values()) for _, pieces in plan]
    got = np.full((ctx_count, sum(widths)), nowhere, np.int32)
    gave = np.zeros((ctx_count, sum(widths)), np.int32)
    for t, (moves, pieces) in enumerate(plan):
        first = sum(widths[:t])
        for source, target in moves:
            listed = pieces[source]
            got[target, first : first + len(listed)] = listed
            high = int(listed[0] != source)
            gave[source, first : first + widths[t]] = [high, 1 - high][: widths[t]]
    top = tp_rank // halves
    starts = jnp.asarray(gave)[ctx_rank] ^ top
    here = jnp.stack([ctx_rank, jnp.int32(ctx_count), tp_rank, jnp.int32(tp_rows)])
    places = jnp.concatenate([here, doc_lengths[0], jnp.asarray(got)[ctx_rank]]).astype(jnp.int32)

    within = jnp.arange(ctx_rows, dtype=jnp.int32) ^ (tp_rank * tp_rows)
    piece = jnp.where(within < near_rows, ctx_rank, 2 * ctx_count - 1 - ctx_rank)
    position = (piece * near_rows + within % near_rows).astype(F32)
    inv_freq = jnp.asarray(rope_table(HD), F32)
    angles = position[:, None] * inv_freq[None, :]
    cosine, sine = jnp.cos(angles), jnp.sin(angles)
    cos = jnp.concatenate([cosine, cosine], axis=1)
    sin = jnp.concatenate([-sine, sine], axis=1)

    perm = jnp.arange(tp_count, dtype=jnp.int32) ^ tp_rank
    mine = ctx_rank % 2
    pairs = ctx_count // 2
    steps = jnp.arange(pairs, dtype=jnp.int32)

    def cols_of(dp_index):
        return (dp_index * ctx_count + 2 * steps + mine).astype(jnp.int32)

    def packed_cols_of(dp_index):
        return (dp_index * pairs + steps).astype(jnp.int32)

    bit = ctx_rank // pairs % 2
    order = ((1 - bit) * (pairs // 2) + steps) % pairs

    class WeightGrad:
        def __init__(self, wide, wide_pair, packed, narrow, narrow_pair, part=(0, 1)):
            def terms(dp_index, *received, zero=False):
                cols = cols_of(dp_index)
                cols_pair = packed_cols_of(dp_index) if packed else cols
                if received:
                    cols, cols_pair = cols[order], cols_pair[order]
                return weight_terms(
                    chain, perm, wide, wide_pair, cols, cols_pair, narrow, narrow_pair, size, part, *received, zero=zero
                )

            self.terms = terms

        def send(self, zero=False):
            self.sent = self.terms(1 - dp_rank, zero=zero)[0]
            self.received = flip(self.sent, "dp", 1)
            return self

        def keep(self):
            chain.wait(self.received)
            sent, self.kept = self.terms(dp_rank, self.received, order)
            self.received = flip(sent, "ctx", pairs)
            self.spread(pairs // 2)

        def spread(self, mask):
            while mask > 1:
                half = jnp.reshape(ctx_rank // mask % 2, (1,))
                sent, self.kept = halve(chain, self.kept, self.received, half, 0)
                self.received = flip(sent, "ctx", mask)
                mask //= 2

        def total(self, zero):
            return (self.kept.astype(F32) + zero) + self.received.astype(F32)

    class OutGrad(WeightGrad):
        def __init__(self, wide, narrow):
            self.wide, self.narrow = wide, narrow

        def pair(self):
            both = jnp.concatenate([steps, steps + pairs])
            cols = (2 * both + 1 - mine).astype(jnp.int32)
            self.received = flip(own_terms(chain, perm, self.wide, cols, self.narrow, size)[0], "ctx", 1)

        def send(self):
            half = ((1 - dp_rank) * pairs + steps).astype(jnp.int32)
            order = jnp.concatenate([half, (dp_rank * pairs + steps).astype(jnp.int32)])
            chain.wait(self.received)
            sent, self.kept = own_terms(
                chain, perm, self.wide, 2 * order + mine, self.narrow, size, self.received, order
            )
            self.received = flip(sent, "dp", 1)

        def keep(self):
            chain.wait(self.received)
            self.spread(pairs)

    inputs = tokens[0].astype(F32)
    normed_local = rms_norm(inputs, attn_gain).astype(BF16)
    normed = tp_gather(normed_local)
    grad_fb_local = out_cotangent[0]
    from_pair = flip(
        jnp.concatenate([grad_fb_local, other_columns(normed_local, mine == 0, size)], axis=1), "ctx", 1
    )
    gathered = lax.all_gather(
        jnp.concatenate([grad_fb_local, from_pair], axis=1), "tp", axis=0, tiled=True
    )
    grad_fb, grad_fb_pair, normed_pair = (
        [(gathered, j, first) for j in range(tp_count)] for first in (0, width, 2 * width)
    )
    kv, query = project(chain, normed, w_query, w_key, w_value, cos, sin)
    low_half = lax.dynamic_slice_in_dim(kv, top * near_rows, near_rows, 0)
    high_half = lax.dynamic_slice_in_dim(kv, (1 - top) * near_rows, near_rows, 0)
    tiles = []
    for t, (moves, _) in enumerate(plan):
        low_first = jnp.asarray(gave)[ctx_rank, sum(widths[:t])] == 0
        held = [jnp.where(low_first, low_half, high_half), jnp.where(low_first, high_half, low_half)]
        held = jnp.concatenate(held[: widths[t]], axis=0)
        tiles.append(lax.ppermute(held, "ctx", moves))
    chain.wait(*tiles)
    merged, totals = attend(chain, places, docs, halves, query, kv, tiles)
    out_terms = pull(chain, [merged], [w_out], tp_count, NN)
    hidden_state = inputs + tp_scatter(out_terms)[1]()

    normed_ffn_local = rms_norm(hidden_state, ffn_gain).astype(BF16)
    normed_ffn = tp_gather(normed_ffn_local)
    chain.room = 52 * 1024 * 1024
    chain.cost = 58 * 10**8
    act, slope, silu = ffn_front(chain, normed_ffn, w_gate, w_up)
    normed_ffn_pair = tp_gather(flip(normed_ffn_local, "ctx", 1), chain.zero)
    act_pair, slope_pair, silu_pair = ffn_front(chain, normed_ffn_pair, w_gate, w_up)

    down_w = WeightGrad(grad_fb, grad_fb_pair, False, act, act_pair).send()
    grad_gate, grad_up = ffn_back(chain, perm, grad_fb, w_down, slope, silu)
    nffn_terms = pull(chain, [grad_gate, grad_up], [w_gate, w_up], tp_count)
    nffn_sent, nffn_sum = tp_scatter(nffn_terms)
    grad_gate_pair, grad_up_pair = ffn_back(chain, perm, grad_fb_pair, w_down, slope_pair, silu_pair)
    chain.wait(nffn_sent)
    gate_w = WeightGrad(normed_ffn, normed_ffn_pair, False, grad_gate, grad_gate_pair).send()
    up_w = WeightGrad(normed_ffn, normed_ffn_pair, False, grad_up, grad_up_pair)
    down_w.keep()
    grad_nffn = nffn_sum() + chain.zero
    grad_state_norm, grad_ffn_gain = jax.vjp(rms_norm, hidden_state, ffn_gain)[1](grad_nffn)
    grad_state = grad_fb_local.astype(F32) + grad_state_norm
    grad_sb_local = grad_state.astype(BF16)
    grad_sb = tp_gather(grad_sb_local)
    chain.wait(grad_sb_local)
    up_w.send()

    grad_query, own, *sent = attend_back(
        chain, places, docs, halves, query, merged, totals, cos, sin, w_out, grad_sb, kv, tiles
    )
    chain.room = VMEM_BYTES * 3 // 4
    returned = [
        lax.ppermute(part, "ctx", [(target, source) for source, target in moves])
        for part, (moves, _) in zip(sent, plan)
    ]
    chain.wait(down_w.received)
    gate_w.keep()
    chain.wait(*returned)
    grad_qkv, grad_key, grad_value = finish(chain, starts, cos, sin, grad_query, own, returned)
    grad_qkv_pair = flip(grad_qkv, "ctx", 1)
    up_w.keep()
    out_w = OutGrad(grad_sb, merged)
    out_w.pair()
    back_terms = pull(chain, [grad_query, grad_key, grad_value], [w_query, w_key, w_value], tp_count)
    layer_terms = push(chain, perm, act, w_down)
    layer_sum = lax.psum_scatter(layer_terms, "tp", scatter_dimension=0, tiled=True)
    layer_out = (hidden_state + layer_sum.astype(F32)).astype(BF16)
    normed_sent, normed_sum = tp_scatter(back_terms)
    chain.wait(grad_qkv_pair)
    qkv_w = WeightGrad(normed, normed_pair, True, grad_qkv, grad_qkv_pair).send(True)
    grad_normed = normed_sum() + chain.zero
    grad_input_norm, grad_attn_gain = jax.vjp(rms_norm, inputs, attn_gain)[1](grad_normed)
    input_grad = grad_state + grad_input_norm
    sent_zero = chain.zero
    chain.wait(gate_w.received)
    qkv_w.keep()
    out_w.send()
    out_zero = chain.zero
    chain.wait(up_w.received)
    out_w.keep()
    zero = chain.zero
    gains = sum_over(jnp.stack([grad_attn_gain, grad_ffn_gain]) + out_zero, "tp")
    gains = sum_over(sum_over(gains + zero, "dp"), "ctx")
    q_width, kv_width = w_query.shape[1], w_key.shape[1]
    out_total = out_w.total(zero).T
    qkv_total = qkv_w.total(zero)
    return (
        layer_out[None],
        input_grad[None],
        gains[0],
        qkv_total[:, :q_width],
        qkv_total[:, q_width : q_width + kv_width],
        qkv_total[:, q_width + kv_width :],
        out_total,
        gains[1],
        gate_w.total(out_zero),
        up_w.total(zero),
        down_w.total(sent_zero).T,
    )


def solution(mesh):
    placed = (
        P("dp", ("ctx", "tp"), None),
        P(),
        P(None, "tp"),
        P(None, "tp"),
        P(None, "tp"),
        P("tp", None),
        P(),
        P(None, "tp"),
        P(None, "tp"),
        P("tp", None),
        P("dp", ("ctx", "tp"), None),
        P("dp", None),
    )
    return jax.shard_map(
        per_device,
        mesh=mesh,
        in_specs=placed,
        out_specs=(
            P("dp", ("ctx", "tp"), None),
            P("dp", ("ctx", "tp"), None),
            P(),
            P(("dp", "ctx"), "tp"),
            P(("dp", "ctx"), "tp"),
            P(("dp", "ctx"), "tp"),
            P("tp", ("dp", "ctx")),
            P(),
            P(("dp", "ctx"), "tp"),
            P(("dp", "ctx"), "tp"),
            P("tp", ("dp", "ctx")),
        ),
        check_vma=False,
    )
```

```python
import functools
import math

import jax
import jax.numpy as jnp
import numpy as np
from jax import lax
from jax.experimental import pallas as pl
from jax.experimental.pallas import tpu as pltpu
from jax.sharding import PartitionSpec as P

HD = 64
EPSILON = 1e-05
NEGATIVE = -1e30
ROPE_THETA = 500000.0


def rope_table(head_size):
    base_freq = np.array(
        [ROPE_THETA ** (-2.0 * index / head_size) for index in range(head_size // 2)]
    )
    wavelength = 2.0 * math.pi / base_freq
    blend = (8192.0 / wavelength - 1.0) / 3.0
    middle = (1.0 - blend) * base_freq / 32.0 + blend * base_freq
    return np.where(
        wavelength > 8192.0, base_freq / 32.0, np.where(wavelength < 2048.0, base_freq, middle)
    )


def rms_norm(values_in, gain_vec):
    return (
        values_in
        * lax.rsqrt(jnp.mean(values_in * values_in, axis=-1, keepdims=True) + EPSILON)
        * gain_vec
    )


F32, BF16 = jnp.float32, jnp.bfloat16
VMEM_BYTES = 62 * 1024 * 1024
NN = (((1,), (0,)), ((), ()))
NT = (((1,), (1,)), ((), ()))
TN = (((0,), (0,)), ((), ()))
VMEM = pl.BlockSpec(memory_space=pltpu.VMEM)
SMEM = pl.BlockSpec(memory_space=pltpu.SMEM)
ANYWHERE = pl.BlockSpec(memory_space=pl.ANY)


def dot(left, right, dims=NN):
    return lax.dot_general(left, right, dims, preferred_element_type=F32)


def part_specs(parts, rows, width, col):
    def spec(part):
        if not isinstance(part, tuple):
            return pl.BlockSpec((rows, width), lambda *at: (0, col(*at)))
        j, first = part[1:]
        return pl.BlockSpec(
            (rows, width), lambda *at: (0 if j is None else at[-1][j], first // width + col(*at))
        )

    return [spec(part) for part in parts]


def part_arrays(parts):
    return [part[0] if isinstance(part, tuple) else part for part in parts]


def rows_of(refs):
    return jnp.concatenate([ref[...] for ref in refs], axis=0)


class Chain:
    def __init__(self):
        self.held = []
        self.cost = 69 * 10**8
        self.room = VMEM_BYTES // 2

    def wait(self, *arrays):
        self.held = [*arrays, *self.held]

    def call(
        self, name, body, args, in_specs, out_specs, out_shape, flops, grid=(), scalars=0, scratch=(), zero=False
    ):
        held, count, outs = self.held, len(args), len(out_shape)
        marks, mark_specs = [jax.ShapeDtypeStruct((8, 128), F32)], [ANYWHERE]
        if zero:
            marks.append(jax.ShapeDtypeStruct((1, 1), F32))
            mark_specs.append(SMEM)

        def inner(*refs):
            rest = refs[count + len(held) :]
            given = refs[:scalars] + refs[scalars + len(held) : count + len(held)]
            body(*given, *rest[:outs], *rest[outs + len(marks) :])
            if zero:
                rest[outs + 1][0, 0] = 0.0

        results = pl.pallas_call(
            inner,
            grid_spec=pltpu.PrefetchScalarGridSpec(
                num_scalar_prefetch=scalars,
                grid=grid,
                in_specs=[ANYWHERE] * len(held) + list(in_specs),
                out_specs=[*out_specs, *mark_specs],
                scratch_shapes=list(scratch),
            ),
            out_shape=[*out_shape, *marks],
            compiler_params=pltpu.CompilerParams(
                vmem_limit_bytes=self.room, dimension_semantics=("arbitrary",) * len(grid)
            ),
            cost_estimate=pl.CostEstimate(flops=self.cost, bytes_accessed=1, transcendentals=0),
            name=name,
        )(*args[:scalars], *held, *args[scalars:])
        self.held = [results[outs]]
        if zero:
            self.zero = results[outs + 1][0, 0]
        return results[:outs]


def fill_rows(parts, rows_ref):
    @pl.when(pl.program_id(0) == 0)
    def _():
        rows_ref[...] = rows_of(parts)


def ffn_front_body(count, *refs):
    gate_ref, up_ref, act_ref, slope_ref, silu_ref, rows_ref = refs[count:]
    fill_rows(refs[:count], rows_ref)
    rows = rows_ref[...]
    gate = dot(rows, gate_ref[...])
    up = dot(rows, up_ref[...])
    sigma = 1.0 / (1.0 + jnp.exp(-gate))
    silu = gate * sigma
    act_ref[...] = (silu * up).astype(BF16)
    slope_ref[...] = (up * sigma * (1.0 + gate * (1.0 - sigma))).astype(BF16)
    silu_ref[...] = silu.astype(BF16)


def whole(array):
    return pl.BlockSpec(array.shape, lambda *_: (0,) * array.ndim)


def ffn_front(chain, parts, w_gate, w_up, part=(0, 1), block=512):
    count, width = sum(p.shape[0] for p in parts), parts[0].shape[1]
    units = w_gate.shape[1] // part[1]
    block = min(block, units)
    first = part[0] * (units // block)
    weight = pl.BlockSpec((width, block), lambda j: (0, first + j))
    return chain.call(
        "ffn_front",
        functools.partial(ffn_front_body, len(parts)),
        (*parts, w_gate, w_up),
        [whole(p) for p in parts] + [weight, weight],
        [pl.BlockSpec((count, block), lambda j: (0, j))] * 3,
        [jax.ShapeDtypeStruct((count, units), BF16)] * 3,
        4 * count * width * units,
        grid=(units // block,),
        scratch=[pltpu.VMEM((count, width), BF16)],
        zero=True,
    )


def ffn_back_body(count, perm_ref, *refs):
    down_ref, slope_ref, silu_ref, gate_ref, up_ref, rows_ref = refs[count:]
    fill_rows(refs[:count], rows_ref)
    grad_act = dot(rows_ref[...], down_ref[...], NT)
    gate_ref[...] = (grad_act * slope_ref[...].astype(F32)).astype(BF16)
    up_ref[...] = (grad_act * silu_ref[...].astype(F32)).astype(BF16)


def ffn_back(chain, perm, parts, w_down, slope, silu, block=512):
    count, units = slope.shape
    width = w_down.shape[1]
    block = min(block, units)
    tile = pl.BlockSpec((count, block), lambda j, _: (0, j))
    return chain.call(
        "ffn_back",
        functools.partial(ffn_back_body, len(parts)),
        (perm, *part_arrays(parts), w_down, slope, silu),
        part_specs(parts, count // len(parts), width, lambda *_: 0)
        + [pl.BlockSpec((block, width), lambda j, _: (j, 0)), tile, tile],
        [tile, tile],
        [jax.ShapeDtypeStruct((count, units), BF16)] * 2,
        2 * count * width * units,
        grid=(units // block,),
        scalars=1,
        scratch=[pltpu.VMEM((count, width), BF16)],
    )


def pull_body(count, dims, *refs):
    total = dot(refs[0][...], refs[count][...], dims)
    for i in range(1, count):
        total = total + dot(refs[i][...], refs[count + i][...], dims)
    outs = refs[2 * count :]
    rows = total.shape[0] // len(outs)
    for j, out in enumerate(outs):
        out[...] = total[j * rows : (j + 1) * rows].astype(BF16)


def pull(chain, grads, weights, blocks, dims=NT, block=1024):
    rows, at = grads[0].shape[0], 0 if dims == NT else 1
    width = weights[0].shape[at]
    depth = sum(w.shape[1 - at] for w in weights)
    return chain.call(
        "pull",
        functools.partial(pull_body, len(grads), dims),
        (*grads, *weights),
        [whole(g) for g in grads]
        + [
            pl.BlockSpec((block, w.shape[1]), lambda j: (j, 0))
            if dims == NT
            else pl.BlockSpec((w.shape[0], block), lambda j: (0, j))
            for w in weights
        ],
        [pl.BlockSpec((rows // blocks, block), lambda j: (0, j))] * blocks,
        [jax.ShapeDtypeStruct((rows // blocks, width), BF16)] * blocks,
        2 * rows * width * depth,
        grid=(width // block,),
        zero=True,
    )


def push_body(blocks, perm_ref, rows_ref, weight_ref, out_ref):
    total = dot(rows_ref[...], weight_ref[...]).astype(BF16)
    rows = total.shape[0] // blocks
    for j in range(blocks):
        at = pl.ds(pl.multiple_of(perm_ref[j] * rows, rows), rows)
        out_ref[at] = total[j * rows : (j + 1) * rows]


def push(chain, perm, rows, weight, block=1024):
    count, depth = rows.shape
    width = weight.shape[1]
    return chain.call(
        "push",
        functools.partial(push_body, perm.shape[0]),
        (perm, rows, weight),
        [
            pl.BlockSpec((count, depth), lambda j, _: (0, 0)),
            pl.BlockSpec((depth, block), lambda j, _: (0, j)),
        ],
        [pl.BlockSpec((count, block), lambda j, _: (0, j))],
        [jax.ShapeDtypeStruct((count, width), BF16)],
        2 * count * depth * width,
        grid=(width // block,),
        scalars=1,
    )[0]


def terms_body(count, blocks, scalars, *refs):
    refs = refs[scalars:]
    wide, wide_pair = rows_of(refs[:count]), rows_of(refs[count : 2 * count])
    own, pair = refs[2 * count : 2 * count + 2]
    total = dot(wide, own[...], TN) + dot(wide_pair, pair[...], TN)
    if scalars == 3:
        refs[-1][...] = total.astype(BF16)
        return
    got, sent_ref, left_ref = refs[2 * count + 2 :]
    total = (total + got[...].astype(F32)).astype(BF16)

    @pl.when(pl.program_id(1) < blocks // 2)
    def _():
        sent_ref[...] = total

    @pl.when(pl.program_id(1) >= blocks // 2)
    def _():
        left_ref[...] = total


def weight_terms(chain, perm, wide, wide_pair, cols, cols_pair, narrow, narrow_pair, size, part, received=None, order=None, zero=False):
    tokens, units = narrow.shape
    units //= part[1]
    blocks = cols.shape[0]
    block = units if units <= 2048 else math.gcd(2048, units)
    first = part[0] * (units // block)
    rows = tokens // len(wide)
    units_spec = pl.BlockSpec((tokens, block), lambda j, i, *_: (0, first + j))
    scalars = [cols, cols_pair, perm]
    in_specs = (
        part_specs(wide, rows, size, lambda j, i, *s: s[-3][i])
        + part_specs(wide_pair, rows, size, lambda j, i, *s: s[-2][i])
        + [units_spec, units_spec]
    )
    args = [*part_arrays(wide), *part_arrays(wide_pair), narrow, narrow_pair]
    if received is None:
        out_specs = [pl.BlockSpec((size, block), lambda j, i, *_: (i, j))]
        out = [jax.ShapeDtypeStruct((blocks * size, units), BF16)]
    else:
        half = blocks // 2
        scalars = [order] + scalars
        args.append(received)
        in_specs.append(pl.BlockSpec((size, block), lambda j, i, io, *_: (io[i], j)))
        out_specs = [
            pl.BlockSpec((size, block), lambda j, i, *_: (jnp.minimum(i, half - 1), j)),
            pl.BlockSpec((size, block), lambda j, i, *_: (jnp.maximum(i - half, 0), j)),
        ]
        out = [jax.ShapeDtypeStruct((half * size, units), BF16)] * 2
    return chain.call(
        "weight_terms",
        functools.partial(terms_body, len(wide), blocks, len(scalars)),
        (*scalars, *args),
        in_specs,
        out_specs,
        out,
        4 * tokens * units * blocks * size,
        grid=(units // block, blocks),
        scalars=len(scalars),
        zero=zero or received is not None,
    )


def own_terms_body(count, blocks, scalars, *refs):
    refs = refs[scalars:]
    total = dot(rows_of(refs[:count]), refs[count][...], TN)
    if scalars == 2:
        refs[-1][...] = total.astype(BF16)
        return
    got, sent_ref, left_ref = refs[count + 1 :]
    total = (total + got[...].astype(F32)).astype(BF16)

    @pl.when(pl.program_id(0) < blocks // 2)
    def _():
        sent_ref[...] = total

    @pl.when(pl.program_id(0) >= blocks // 2)
    def _():
        left_ref[...] = total


def own_terms(chain, perm, wide, cols, narrow, size, received=None, order=None):
    tokens, units = narrow.shape
    blocks = cols.shape[0]
    rows = tokens // len(wide)
    half = blocks // 2
    scalars = [cols, perm]
    args = [*part_arrays(wide), narrow]
    in_specs = part_specs(wide, rows, size, lambda i, *s: s[-2][i]) + [whole(narrow)]
    if received is None:
        out_specs = [pl.BlockSpec((size, units), lambda i, *_: (i, 0))]
        out = [jax.ShapeDtypeStruct((blocks * size, units), BF16)]
    else:
        scalars = [order] + scalars
        args.append(received)
        in_specs.append(pl.BlockSpec((size, units), lambda i, io, *_: (io[i], 0)))
        out_specs = [
            pl.BlockSpec((size, units), lambda i, *_: (jnp.minimum(i, half - 1), 0)),
            pl.BlockSpec((size, units), lambda i, *_: (jnp.maximum(i - half, 0), 0)),
        ]
        out = [jax.ShapeDtypeStruct((half * size, units), BF16)] * 2
    return chain.call(
        "own_terms",
        functools.partial(own_terms_body, len(wide), blocks, len(scalars)),
        (*scalars, *args),
        in_specs,
        out_specs,
        out,
        2 * tokens * units * blocks * size,
        grid=(blocks,),
        scalars=len(scalars),
        zero=True,
    )


def halve_body(mine, kept_send, got_send, kept, got, sent_ref, left_ref):
    sent_ref[...] = (kept_send[...].astype(F32) + got_send[...].astype(F32)).astype(BF16)
    left_ref[...] = (kept[...].astype(F32) + got[...].astype(F32)).astype(BF16)


def halve(chain, kept, received, mine, dim):
    steps = math.gcd(4, kept.shape[1 - dim] // 128)
    shape = list(kept.shape)
    shape[dim] //= 2
    block = list(shape)
    block[1 - dim] //= steps

    def spec(flip_half):
        def at(j, m):
            half = 1 - m[0] if flip_half else m[0]
            return (half, j) if dim == 0 else (j, half)

        return pl.BlockSpec(tuple(block), at)

    out_spec = pl.BlockSpec(tuple(block), lambda j, m: (0, j) if dim == 0 else (j, 0))
    out = jax.ShapeDtypeStruct(tuple(shape), BF16)
    return chain.call(
        "halve",
        halve_body,
        (mine, kept, received, kept, received),
        [spec(True), spec(True), spec(False), spec(False)],
        [out_spec, out_spec],
        [out, out],
        kept.size,
        grid=(steps,),
        scalars=1,
        zero=True,
    )


def swap_halves(values_in):
    half = HD // 2
    width = values_in.shape[1]
    if width % 128:
        parts = []
        for at in range(0, width, HD):
            parts += [values_in[:, at + half : at + HD], values_in[:, at : at + half]]
        return jnp.concatenate(parts, axis=1)
    lane = lax.broadcasted_iota(jnp.int32, values_in.shape, 1)
    return jnp.where(
        lane % HD < half,
        pltpu.roll(values_in, width - half, 1),
        pltpu.roll(values_in, half, 1),
    )


def turn(values_in, cos_ref, sin_ref, sign):
    count = values_in.shape[1] // HD
    cos = jnp.concatenate([cos_ref[...]] * count, axis=1)
    sin = jnp.concatenate([sin_ref[...]] * count, axis=1)
    return values_in * cos + sign * (swap_halves(values_in) * sin)


def project_body(count, *refs):
    q_ref, k_ref, v_ref, cos_ref, sin_ref, kv_ref, query_ref = refs[count:]
    rows = rows_of(refs[:count])
    width = k_ref.shape[1]
    kv_ref[:, :width] = turn(dot(rows, k_ref[...]), cos_ref, sin_ref, 1.0).astype(BF16)
    kv_ref[:, width:] = dot(rows, v_ref[...]).astype(BF16)
    queries = turn(dot(rows, q_ref[...]), cos_ref, sin_ref, 1.0).astype(BF16)
    query_ref[...] = (queries.astype(F32) * (1.0 / math.sqrt(HD))).astype(BF16)


def project(chain, parts, w_query, w_key, w_value, cos, sin):
    count = sum(p.shape[0] for p in parts)
    kv = jax.ShapeDtypeStruct((count, 2 * w_key.shape[1]), BF16)
    query = jax.ShapeDtypeStruct((count, w_query.shape[1]), BF16)
    return chain.call(
        "project",
        functools.partial(project_body, len(parts)),
        (*parts, w_query, w_key, w_value, cos, sin),
        [VMEM] * (len(parts) + 5),
        [VMEM] * 2,
        [kv, query],
        2 * count * parts[0].shape[1] * (query.shape[1] + kv.shape[1]),
    )


def half_piece(places_ref, half, halves):
    top = places_ref[2] // halves
    return jnp.where(top == half, places_ref[0], 2 * places_ref[1] - 1 - places_ref[0])


def doc_start(places_ref, docs, position):
    end = 0
    start = position * 0
    for i in range(docs):
        end = end + places_ref[4 + i]
        start = jnp.where(position >= end, end, start)
    return start, position < end


def positions_of(places_ref, piece, halves, rows, shape, dim):
    row = lax.broadcasted_iota(jnp.int32, shape, dim)
    inner = lax.rem(places_ref[2], halves) * places_ref[3]
    return piece * rows + (row ^ inner)


def tile_count(tiles, rows):
    return sum(t.shape[0] for t in tiles) // rows + 2


def half_of(places_ref, docs, halves, half, rows, group):
    piece = half_piece(places_ref, half, halves)
    position = positions_of(places_ref, piece, halves, rows, (1, rows), 1)
    start, valid = doc_start(places_ref, docs, position)
    first = doc_start(places_ref, docs, piece * rows)[0]
    position, start, valid = (
        jnp.concatenate([v] * group, axis=1) for v in (position, start, valid.astype(jnp.int32))
    )
    return piece, position, start, valid, first


def tile_piece(places_ref, docs, halves, t):
    given = places_ref[4 + docs + jnp.maximum(t - 2, 0)]
    own = jnp.where(t == 0, half_piece(places_ref, 0, halves), half_piece(places_ref, 1, halves))
    return jnp.where(t < 2, own, given)


def split_tiles(kv_refs, rows, keys_ref, values_ref, ones):
    kv_heads = keys_ref.shape[0]
    t = 0
    for ref in kv_refs:
        for row in range(0, ref.shape[0], rows):
            for g in range(kv_heads):
                keys_ref[g, t] = ref[row : row + rows, g * HD : (g + 1) * HD]
                values = ref[row : row + rows, (kv_heads + g) * HD : (kv_heads + g + 1) * HD]
                if ones:
                    values = jnp.concatenate([values, jnp.ones_like(values)], axis=1)
                values_ref[g, t] = values
            t += 1


def split_heads(ref, rows, group, out_ref, change=lambda v, half: v):
    kv_heads = out_ref.shape[0] // 2
    for half in range(2):
        for g in range(kv_heads):
            for i in range(group):
                head = (g * group + i) * HD
                values = ref[half * rows : (half + 1) * rows, head : head + HD]
                out_ref[half * kv_heads + g, i * rows : (i + 1) * rows] = change(values, half)


def attend_body(docs, halves, count, places_ref, q_ref, kv_ref, *refs):
    tile_refs, (merged_ref, total_ref) = refs[:count], refs[count : count + 2]
    keys_ref, values_ref, stack_ref, scores_ref, peak_ref, sums_ref, out_ref = refs[count + 2 :]
    rows = q_ref.shape[0] // 2
    kv_heads, tiles = keys_ref.shape[:2]
    group = q_ref.shape[1] // HD // kv_heads
    split_tiles([kv_ref, *tile_refs], rows, keys_ref, values_ref, True)
    split_heads(q_ref, rows, group, stack_ref)

    def one(hg, carry):
        half, g = hg // kv_heads, hg % kv_heads
        q_piece, q_pos, q_start, valid, first = half_of(places_ref, docs, halves, half, rows, group)
        peak_ref[...] = jnp.full(peak_ref.shape, NEGATIVE, F32)
        sums_ref[...] = jnp.zeros(sums_ref.shape, F32)

        def score(t, carry):
            piece = tile_piece(places_ref, docs, halves, t)

            @pl.when((piece <= q_piece) & ((piece + 1) * rows > first))
            def _():
                k_pos = positions_of(places_ref, piece, halves, rows, (rows, 1), 0)
                scores = dot(keys_ref[g, t], stack_ref[hg], NT)
                scores = jnp.where((k_pos <= q_pos) & (k_pos >= q_start), scores, NEGATIVE)
                scores_ref[t] = scores
                top = jnp.max(scores.reshape(rows // 8, 8, group * rows), axis=0)
                peak_ref[...] = jnp.maximum(peak_ref[...], top)

            return carry

        lax.fori_loop(0, tiles, score, 0)
        peak = jnp.max(peak_ref[...], axis=0, keepdims=True)

        def weigh(t, carry):
            piece = tile_piece(places_ref, docs, halves, t)

            @pl.when((piece <= q_piece) & ((piece + 1) * rows > first))
            def _():
                expo = jnp.exp(scores_ref[t] - peak).astype(BF16)
                sums_ref[...] += dot(values_ref[g, t], expo, TN)

            return carry

        lax.fori_loop(0, tiles, weigh, 0)
        total = sums_ref[HD : HD + 1]
        out_ref[hg] = jnp.where(valid > 0, sums_ref[...] / total, 0.0).T.astype(BF16)
        total_ref[hg] = peak + jnp.log(total)
        return carry

    lax.fori_loop(0, 2 * kv_heads, one, 0)
    for half in range(2):
        for g in range(kv_heads):
            for i in range(group):
                head = (g * group + i) * HD
                merged_ref[half * rows : (half + 1) * rows, head : head + HD] = out_ref[
                    half * kv_heads + g, i * rows : (i + 1) * rows, :HD
                ]


def attend(chain, places, docs, halves, query, kv, tiles):
    tokens, width = query.shape
    rows = tokens // 2
    heads, kv_heads = width // HD, kv.shape[1] // 2 // HD
    span = heads // kv_heads * rows
    tile_num = tile_count(tiles, rows)
    return chain.call(
        "attend",
        functools.partial(attend_body, docs, halves, len(tiles)),
        (places, query, kv, *tiles),
        [SMEM] + [VMEM] * (2 + len(tiles)),
        [VMEM] * 2,
        [
            jax.ShapeDtypeStruct((tokens, width), BF16),
            jax.ShapeDtypeStruct((2 * kv_heads, 1, span), F32),
        ],
        8 * tokens * rows * tile_num * width,
        scratch=[
            pltpu.VMEM((kv_heads, tile_num, rows, HD), BF16),
            pltpu.VMEM((kv_heads, tile_num, rows, 2 * HD), BF16),
            pltpu.VMEM((2 * kv_heads, span, HD), BF16),
            pltpu.VMEM((tile_num, rows, span), F32),
            pltpu.VMEM((8, span), F32),
            pltpu.VMEM((2 * HD, span), F32),
            pltpu.VMEM((2 * kv_heads, span, 2 * HD), BF16),
        ],
    )


def attend_back_body(docs, halves, count, parts, *refs):
    places_ref, q_ref, merged_ref, total_ref, cos_ref, sin_ref, w_ref = refs[:7]
    kv_ref, tile_refs = refs[7 + parts], refs[8 + parts : 8 + parts + count]
    grad_q_ref, grad_own_ref, *grad_tile_refs = refs[8 + parts + count : 10 + parts + 2 * count]
    grad_ref, keys_ref, values_ref, stack_ref, grads_ref, outs_ref, q_sum_ref, kv_sum_ref = refs[
        10 + parts + 2 * count :
    ]
    rows = q_ref.shape[0] // 2
    kv_heads, tiles = keys_ref.shape[:2]
    group = q_ref.shape[1] // HD // kv_heads
    grad_ref[...] = dot(rows_of(refs[7 : 7 + parts]), w_ref[...], NT).astype(BF16)
    split_tiles([kv_ref, *tile_refs], rows, keys_ref, values_ref, False)
    split_heads(q_ref, rows, group, stack_ref)
    split_heads(merged_ref, rows, group, outs_ref)
    shown = []
    for half in range(2):
        piece = half_piece(places_ref, half, halves)
        position = positions_of(places_ref, piece, halves, rows, (rows, 1), 0)
        shown.append(doc_start(places_ref, docs, position)[1])

    def masked(values, half):
        return jnp.where(shown[half], values.astype(F32), 0.0).astype(BF16)

    split_heads(grad_ref, rows, group, grads_ref, masked)
    kv_sum_ref[...] = jnp.zeros(kv_sum_ref.shape, F32)
    q_sum_ref[...] = jnp.zeros(q_sum_ref.shape, F32)

    def one(hg, carry):
        half, g = hg // kv_heads, hg % kv_heads
        q_piece, q_pos, q_start, _, first = half_of(places_ref, docs, halves, half, rows, group)
        product = grads_ref[hg].astype(F32) * outs_ref[hg].astype(F32)
        high = product.astype(BF16)
        low = (product - high.astype(F32)).astype(BF16)
        ones = jnp.ones((8, HD), BF16)
        delta = (dot(ones, high, NT) + dot(ones, low, NT))[:1]
        totals = total_ref[hg]

        def back(t, carry):
            piece = tile_piece(places_ref, docs, halves, t)

            @pl.when((piece <= q_piece) & ((piece + 1) * rows > first))
            def _():
                k_pos = positions_of(places_ref, piece, halves, rows, (rows, 1), 0)
                keys, queries, grads = keys_ref[g, t], stack_ref[hg], grads_ref[hg]
                scores = dot(keys, queries, NT) - totals
                scores = jnp.where((k_pos <= q_pos) & (k_pos >= q_start), scores, NEGATIVE)
                probs = jnp.exp(scores)
                grad_probs = dot(values_ref[g, t], grads, NT)
                grad_scores = (probs * (grad_probs - delta)).astype(BF16)
                q_sum_ref[hg, :HD] += dot(keys, grad_scores, TN)
                kv_sum_ref[t, 0, g] += dot(grad_scores, queries)
                kv_sum_ref[t, 1, g] += dot(probs.astype(BF16), grads)

            return carry

        lax.fori_loop(0, tiles, back, 0)
        return carry

    lax.fori_loop(0, 2 * kv_heads, one, 0)
    for half in range(2):
        at = pl.ds(half * rows, rows)
        for g in range(kv_heads):
            q_sum = q_sum_ref[half * kv_heads + g].T
            for i in range(group):
                head = (g * group + i) * HD
                part = q_sum[i * rows : (i + 1) * rows, :HD] * (1.0 / math.sqrt(HD))
                part = part * cos_ref[at] - swap_halves(part) * sin_ref[at]
                grad_q_ref[at, head : head + HD] = part.astype(BF16)
    targets = [
        (out, row) for out in (grad_own_ref, *grad_tile_refs) for row in range(0, out.shape[0], rows)
    ]
    for t, (out_ref, row) in enumerate(targets):
        for part in range(2):
            for g in range(kv_heads):
                cols = slice((part * kv_heads + g) * HD, (part * kv_heads + g + 1) * HD)
                out_ref[row : row + rows, cols] = kv_sum_ref[t, part, g].astype(out_ref.dtype)


def attend_back(chain, places, docs, halves, query, merged, totals, cos, sin, w_out, grads, kv, tiles):
    tokens, width = query.shape
    rows = tokens // 2
    kv_heads = kv.shape[1] // 2 // HD
    span = width // HD // kv_heads * rows
    tile_num = tile_count(tiles, rows)
    stack = pltpu.VMEM((2 * kv_heads, span, HD), BF16)
    return chain.call(
        "attend_back",
        functools.partial(attend_back_body, docs, halves, len(tiles), len(grads)),
        (places, query, merged, totals, cos, sin, w_out, *grads, kv, *tiles),
        [SMEM] + [VMEM] * (7 + len(grads) + len(tiles)),
        [VMEM] * (2 + len(tiles)),
        [jax.ShapeDtypeStruct((tokens, width), BF16), jax.ShapeDtypeStruct(kv.shape, F32)]
        + [jax.ShapeDtypeStruct(t.shape, BF16) for t in tiles],
        16 * tokens * rows * tile_num * width,
        scratch=[
            pltpu.VMEM((tokens, width), BF16),
            pltpu.VMEM((kv_heads, tile_num, rows, HD), BF16),
            pltpu.VMEM((kv_heads, tile_num, rows, HD), BF16),
            stack,
            stack,
            stack,
            pltpu.VMEM((2 * kv_heads, 2 * HD, span), F32),
            pltpu.VMEM((tile_num, 2, kv_heads, rows, HD), F32),
        ],
    )


def finish_body(starts_ref, cos_ref, sin_ref, query_ref, own_ref, *refs):
    parts, (all_ref, key_ref, value_ref, total_ref) = refs[:-4], refs[-4:]
    total_ref[...] = own_ref[...]
    rows = own_ref.shape[0] // 2
    tiles = [(part, row) for part in parts for row in range(0, part.shape[0], rows)]
    for t, (part, row) in enumerate(tiles):
        at = pl.ds(pl.multiple_of(starts_ref[t] * rows, rows), rows)
        total_ref[at] += part[row : row + rows].astype(F32)
    width = key_ref.shape[1]
    keys = turn(total_ref[:, :width], cos_ref, sin_ref, -1.0).astype(BF16)
    values = total_ref[:, width:].astype(BF16)
    key_ref[...] = keys
    value_ref[...] = values
    wide = query_ref.shape[1]
    all_ref[:, :wide] = query_ref[...]
    all_ref[:, wide : wide + width] = keys
    all_ref[:, wide + width :] = values


def finish(chain, starts, cos, sin, grad_query, own, parts):
    tokens, width = own.shape
    wide = grad_query.shape[1] + width
    one = jax.ShapeDtypeStruct((tokens, width // 2), BF16)
    return chain.call(
        "finish",
        finish_body,
        (starts, cos, sin, grad_query, own, *parts),
        [SMEM] + [VMEM] * (4 + len(parts)),
        [VMEM] * 3,
        [jax.ShapeDtypeStruct((tokens, wide), BF16), one, one],
        20 * tokens * width,
        scratch=[pltpu.VMEM((tokens, width), F32)],
    )


def flip(values_in, axis, mask):
    count = lax.axis_size(axis)
    return lax.ppermute(values_in, axis, [(i, i ^ mask) for i in range(count)])


def later(values_in, zero):
    return (values_in.astype(F32) + zero).astype(BF16)


def tp_gather(shard, zero=None):
    count = lax.axis_size("tp")
    parts = {0: shard}
    mask = 2
    while mask < count:
        parts.update({j ^ mask: flip(part, "tp", mask) for j, part in parts.items()})
        mask *= 2
    for j, part in list(parts.items()):
        parts[j ^ 1] = flip(later(part, zero) if j and zero is not None else part, "tp", 1)
    return [parts[j] for j in range(count)]


def tp_scatter(terms):
    count = len(terms)
    received = {j: flip(terms[j + 1], "tp", 1) for j in reversed(range(0, count, 2))}
    blocks = {j: terms[j].astype(F32) + part.astype(F32) for j, part in received.items()}
    mask = count // 2
    while mask > 2:
        for j in range(0, mask, 2):
            blocks[j] = blocks[j] + flip(blocks[j + mask].astype(BF16), "tp", mask).astype(F32)
        mask //= 2
    sent = blocks[2].astype(BF16)
    return sent, lambda: blocks[0] + flip(sent, "tp", 2).astype(F32)


def sum_over(values_in, axis):
    mask = 1
    while mask < lax.axis_size(axis):
        values_in = values_in + flip(values_in, axis, mask)
        mask *= 2
    return values_in


def tile_plan(count):
    ends = 2 * count + 3
    needed = []
    for c in range(count):
        pieces = set()
        for held in (c, 2 * count - 1 - c):
            first = ends // 2 if 2 * held >= ends else 0
            pieces |= set(range(first, held + 1))
        needed.append(pieces - {c, 2 * count - 1 - c})
    plan = []
    for k in range(1, count):
        chosen = {}
        for c in range(count):
            source = (c + k) % count
            pieces = sorted(needed[c] & {source, 2 * count - 1 - source})
            if pieces:
                chosen[source] = (c, pieces)
        if chosen:
            plan.append(([(s, c) for s, (c, _) in chosen.items()], {s: p for s, (_, p) in chosen.items()}))
    return plan


def other_columns(values_in, pick_odd, size):
    blocks = values_in.shape[1] // size
    even, odd = (
        jnp.concatenate([values_in[:, b * size : (b + 1) * size] for b in range(at, blocks, 2)], axis=1)
        for at in (0, 1)
    )
    return jnp.where(pick_odd, odd, even)


def per_device(
    tokens,
    attn_gain,
    w_query,
    w_key,
    w_value,
    w_out,
    ffn_gain,
    w_gate,
    w_up,
    w_down,
    out_cotangent,
    doc_lengths,
):
    ctx_count, ctx_rank = lax.axis_size("ctx"), lax.axis_index("ctx")
    dp_count, dp_rank = lax.axis_size("dp"), lax.axis_index("dp")
    tp_count, tp_rank = lax.axis_size("tp"), lax.axis_index("tp")
    tp_rows, width = tokens.shape[1:]
    ctx_rows = tp_rows * tp_count
    near_rows = ctx_rows // 2
    halves = tp_count // 2
    docs = doc_lengths.shape[1]
    size = width // (dp_count * ctx_count)
    chain = Chain()

    plan = tile_plan(ctx_count)
    nowhere = 2 * ctx_count
    widths = [max(len(p) for p in pieces.values()) for _, pieces in plan]
    got = np.full((ctx_count, sum(widths)), nowhere, np.int32)
    gave = np.zeros((ctx_count, sum(widths)), np.int32)
    for t, (moves, pieces) in enumerate(plan):
        first = sum(widths[:t])
        for source, target in moves:
            listed = pieces[source]
            got[target, first : first + len(listed)] = listed
            high = int(listed[0] != source)
            gave[source, first : first + widths[t]] = [high, 1 - high][: widths[t]]
    top = tp_rank // halves
    starts = jnp.asarray(gave)[ctx_rank] ^ top
    here = jnp.stack([ctx_rank, jnp.int32(ctx_count), tp_rank, jnp.int32(tp_rows)])
    places = jnp.concatenate([here, doc_lengths[0], jnp.asarray(got)[ctx_rank]]).astype(jnp.int32)

    within = jnp.arange(ctx_rows, dtype=jnp.int32) ^ (tp_rank * tp_rows)
    piece = jnp.where(within < near_rows, ctx_rank, 2 * ctx_count - 1 - ctx_rank)
    position = (piece * near_rows + within % near_rows).astype(F32)
    inv_freq = jnp.asarray(rope_table(HD), F32)
    angles = position[:, None] * inv_freq[None, :]
    cosine, sine = jnp.cos(angles), jnp.sin(angles)
    cos = jnp.concatenate([cosine, cosine], axis=1)
    sin = jnp.concatenate([-sine, sine], axis=1)

    perm = jnp.arange(tp_count, dtype=jnp.int32) ^ tp_rank
    mine = ctx_rank % 2
    pairs = ctx_count // 2
    steps = jnp.arange(pairs, dtype=jnp.int32)

    def cols_of(dp_index):
        return (dp_index * ctx_count + 2 * steps + mine).astype(jnp.int32)

    def packed_cols_of(dp_index):
        return (dp_index * pairs + steps).astype(jnp.int32)

    bit = ctx_rank // pairs % 2
    order = ((1 - bit) * (pairs // 2) + steps) % pairs

    class WeightGrad:
        def __init__(self, wide, wide_pair, packed, narrow, narrow_pair, part=(0, 1)):
            def terms(dp_index, *received, zero=False):
                cols = cols_of(dp_index)
                cols_pair = packed_cols_of(dp_index) if packed else cols
                if received:
                    cols, cols_pair = cols[order], cols_pair[order]
                return weight_terms(
                    chain, perm, wide, wide_pair, cols, cols_pair, narrow, narrow_pair, size, part, *received, zero=zero
                )

            self.terms = terms

        def send(self, zero=False):
            self.sent = self.terms(1 - dp_rank, zero=zero)[0]
            self.received = flip(self.sent, "dp", 1)
            return self

        def keep(self):
            chain.wait(self.received)
            sent, self.kept = self.terms(dp_rank, self.received, order)
            self.received = flip(sent, "ctx", pairs)
            self.spread(pairs // 2)

        def spread(self, mask):
            while mask > 1:
                half = jnp.reshape(ctx_rank // mask % 2, (1,))
                sent, self.kept = halve(chain, self.kept, self.received, half, 0)
                self.received = flip(sent, "ctx", mask)
                mask //= 2

        def total(self, zero):
            return (self.kept.astype(F32) + zero) + self.received.astype(F32)

    class OutGrad(WeightGrad):
        def __init__(self, wide, narrow):
            self.wide, self.narrow = wide, narrow

        def pair(self):
            both = jnp.concatenate([steps, steps + pairs])
            cols = (2 * both + 1 - mine).astype(jnp.int32)
            self.received = flip(own_terms(chain, perm, self.wide, cols, self.narrow, size)[0], "ctx", 1)

        def send(self):
            half = ((1 - dp_rank) * pairs + steps).astype(jnp.int32)
            order = jnp.concatenate([half, (dp_rank * pairs + steps).astype(jnp.int32)])
            chain.wait(self.received)
            sent, self.kept = own_terms(
                chain, perm, self.wide, 2 * order + mine, self.narrow, size, self.received, order
            )
            self.received = flip(sent, "dp", 1)

        def keep(self):
            chain.wait(self.received)
            self.spread(pairs)

    inputs = tokens[0].astype(F32)
    normed_local = rms_norm(inputs, attn_gain).astype(BF16)
    normed = tp_gather(normed_local)
    grad_fb_local = out_cotangent[0]
    from_pair = flip(
        jnp.concatenate([grad_fb_local, other_columns(normed_local, mine == 0, size)], axis=1), "ctx", 1
    )
    gathered = lax.all_gather(
        jnp.concatenate([grad_fb_local, from_pair], axis=1), "tp", axis=0, tiled=True
    )
    grad_fb, grad_fb_pair, normed_pair = (
        [(gathered, j, first) for j in range(tp_count)] for first in (0, width, 2 * width)
    )
    kv, query = project(chain, normed, w_query, w_key, w_value, cos, sin)
    low_half = lax.dynamic_slice_in_dim(kv, top * near_rows, near_rows, 0)
    high_half = lax.dynamic_slice_in_dim(kv, (1 - top) * near_rows, near_rows, 0)
    tiles = []
    for t, (moves, _) in enumerate(plan):
        low_first = jnp.asarray(gave)[ctx_rank, sum(widths[:t])] == 0
        held = [jnp.where(low_first, low_half, high_half), jnp.where(low_first, high_half, low_half)]
        held = jnp.concatenate(held[: widths[t]], axis=0)
        tiles.append(lax.ppermute(held, "ctx", moves))
    chain.wait(*tiles)
    merged, totals = attend(chain, places, docs, halves, query, kv, tiles)
    out_terms = pull(chain, [merged], [w_out], tp_count, NN)
    hidden_state = inputs + tp_scatter(out_terms)[1]()

    normed_ffn_local = rms_norm(hidden_state, ffn_gain).astype(BF16)
    normed_ffn = tp_gather(normed_ffn_local)
    chain.room = 52 * 1024 * 1024
    chain.cost = 58 * 10**8
    act, slope, silu = ffn_front(chain, normed_ffn, w_gate, w_up)
    normed_ffn_pair = tp_gather(flip(normed_ffn_local, "ctx", 1), chain.zero)
    act_pair, slope_pair, silu_pair = ffn_front(chain, normed_ffn_pair, w_gate, w_up)

    down_w = WeightGrad(grad_fb, grad_fb_pair, False, act, act_pair).send()
    grad_gate, grad_up = ffn_back(chain, perm, grad_fb, w_down, slope, silu)
    nffn_terms = pull(chain, [grad_gate, grad_up], [w_gate, w_up], tp_count)
    nffn_sent, nffn_sum = tp_scatter(nffn_terms)
    grad_gate_pair, grad_up_pair = ffn_back(chain, perm, grad_fb_pair, w_down, slope_pair, silu_pair)
    chain.wait(nffn_sent)
    gate_w = WeightGrad(normed_ffn, normed_ffn_pair, False, grad_gate, grad_gate_pair).send()
    up_w = WeightGrad(normed_ffn, normed_ffn_pair, False, grad_up, grad_up_pair)
    down_w.keep()
    grad_nffn = nffn_sum() + chain.zero
    grad_state_norm, grad_ffn_gain = jax.vjp(rms_norm, hidden_state, ffn_gain)[1](grad_nffn)
    grad_state = grad_fb_local.astype(F32) + grad_state_norm
    grad_sb_local = grad_state.astype(BF16)
    grad_sb = tp_gather(grad_sb_local)
    chain.wait(grad_sb_local)
    up_w.send()

    grad_query, own, *sent = attend_back(
        chain, places, docs, halves, query, merged, totals, cos, sin, w_out, grad_sb, kv, tiles
    )
    chain.room = VMEM_BYTES * 3 // 4
    returned = [
        lax.ppermute(part, "ctx", [(target, source) for source, target in moves])
        for part, (moves, _) in zip(sent, plan)
    ]
    chain.wait(down_w.received)
    gate_w.keep()
    chain.wait(*returned)
    grad_qkv, grad_key, grad_value = finish(chain, starts, cos, sin, grad_query, own, returned)
    grad_qkv_pair = flip(grad_qkv, "ctx", 1)
    up_w.keep()
    out_w = OutGrad(grad_sb, merged)
    out_w.pair()
    back_terms = pull(chain, [grad_query, grad_key, grad_value], [w_query, w_key, w_value], tp_count)
    layer_terms = push(chain, perm, act, w_down)
    layer_sum = lax.psum_scatter(layer_terms, "tp", scatter_dimension=0, tiled=True)
    layer_out = (hidden_state + layer_sum.astype(F32)).astype(BF16)
    normed_sent, normed_sum = tp_scatter(back_terms)
    chain.wait(grad_qkv_pair)
    qkv_w = WeightGrad(normed, normed_pair, True, grad_qkv, grad_qkv_pair).send(True)
    grad_normed = normed_sum() + chain.zero
    grad_input_norm, grad_attn_gain = jax.vjp(rms_norm, inputs, attn_gain)[1](grad_normed)
    input_grad = grad_state + grad_input_norm
    sent_zero = chain.zero
    chain.wait(gate_w.received)
    qkv_w.keep()
    out_w.send()
    out_zero = chain.zero
    chain.wait(up_w.received, layer_out)
    out_w.keep()
    zero = chain.zero
    gains = sum_over(jnp.stack([grad_attn_gain, grad_ffn_gain]) + out_zero, "tp")
    gains = sum_over(sum_over(gains + zero, "dp"), "ctx")
    q_width, kv_width = w_query.shape[1], w_key.shape[1]
    out_total = out_w.total(zero).T
    qkv_total = qkv_w.total(zero)
    return (
        layer_out[None],
        input_grad[None],
        gains[0],
        qkv_total[:, :q_width],
        qkv_total[:, q_width : q_width + kv_width],
        qkv_total[:, q_width + kv_width :],
        out_total,
        gains[1],
        gate_w.total(out_zero),
        up_w.total(zero),
        down_w.total(sent_zero).T,
    )


def solution(mesh):
    placed = (
        P("dp", ("ctx", "tp"), None),
        P(),
        P(None, "tp"),
        P(None, "tp"),
        P(None, "tp"),
        P("tp", None),
        P(),
        P(None, "tp"),
        P(None, "tp"),
        P("tp", None),
        P("dp", ("ctx", "tp"), None),
        P("dp", None),
    )
    return jax.shard_map(
        per_device,
        mesh=mesh,
        in_specs=placed,
        out_specs=(
            P("dp", ("ctx", "tp"), None),
            P("dp", ("ctx", "tp"), None),
            P(),
            P(("dp", "ctx"), "tp"),
            P(("dp", "ctx"), "tp"),
            P(("dp", "ctx"), "tp"),
            P("tp", ("dp", "ctx")),
            P(),
            P(("dp", "ctx"), "tp"),
            P(("dp", "ctx"), "tp"),
            P("tp", ("dp", "ctx")),
        ),
        check_vma=False,
    )
```
